128 devices in a mesh: dp: 64 (over x_lo, z, y, core), tensor: 2 (over x_hi).
Axes of the slice: x: 4 (x_hi: 2, x_lo: 2; x = x_hi * 2 + x_lo), y: 4, z: 4, core: 2. Of those that a mesh axis runs over, the one named last changes fastest.
Arguments:
- tokens: bfloat16 [65536, 1024], P('dp'), may hold values from -6 to 6
- norm_gain: float32 [1024], replicated, may hold values from 0.5 to 1.5
- norm_shift: float32 [1024], replicated, may hold values from -4 to 4
- qkv_weight: bfloat16 [1024, 3, 1024], P(None, None, 'tensor'), may hold values from -0.25 to 0.25
- merge_weight: bfloat16 [1024, 1024], P('tensor'), may hold values from -0.5 to 0.5
- up_weight: bfloat16 [1024, 4096], P(None, 'tensor'), may hold values from -0.1875 to 0.1875
- inner_shift: float32 [4096], P('tensor'), may hold values from -6 to 6
- down_weight: bfloat16 [4096, 1024], P('tensor'), may hold values from -0.09375 to 0.09375
- outer_shift: float32 [1024], replicated, may hold values from -6 to 6
- cotangent: bfloat16 [65536, 1024], P('dp'), may hold values from -6 to 6
Outputs:
- block_out: bfloat16 [65536, 1024], P('dp')
- token_grad: bfloat16 [65536, 1024], P('dp')
- gain_grad: float32 [1024], replicated
- shift_grad: float32 [1024], replicated
- qkv_grad: float32 [1024, 3, 1024], P(None, None, 'tensor')
- merge_grad: float32 [1024, 1024], P('tensor')
- up_grad: float32 [1024, 4096], P(None, 'tensor')
- inner_grad: float32 [4096], P('tensor')
- down_grad: float32 [4096, 1024], P('tensor')
- outer_grad: float32 [1024], replicated
The draws below stay inside these ranges and needn't reach their ends.
All inputs are finite; a program needn't handle non-finite values.
Results may differ from the reference program's by a relative error of at most 0.0065.
The reference program's roundings to bfloat16 on the way count: a program that leaves them out, or rounds other values in their place, can miss the bound.
Values sent between devices are 32-bit elements; how exact they have to be, the bound alone decides.
No kernel may reach another device: no remote copies, remote signals or barrier semaphores. Data moves between devices by JAX's collectives and lax.ppermute only.
A program may use at most 256 MiB of HBM per device.

```python
import math
import jax
import jax.numpy as jnp
from jax import lax

HEADS = 16
HEAD = 64
ROT = 32
D = 1024
FF = 4096
TOK_DEV = 1024
TOKENS = 65536
N_DP = 64


def levels(rng, dims, pieces, least, high):
    loudness, own = 1.0, jax.random.fold_in(rng, 6)
    for position, shards_of in pieces:
        draws = jnp.exp(jax.random.uniform(jax.random.fold_in(own, position), (shards_of,), jnp.float32, least / len(pieces), high / len(pieces)))
        loudness = loudness * jnp.repeat(draws, dims[position] // shards_of).reshape([-1 if axis == position else 1 for axis in range(len(dims))])
    return loudness


def gaussian(own_key, dims, width, limit, cuts=(), dtype=jnp.bfloat16):
    loudness = levels(own_key, dims, cuts, -0.22, 0.18) if cuts else 1.0
    result = jax.random.normal(own_key, dims, jnp.float32) * width * loudness
    return jnp.minimum(jnp.maximum(result, -limit), limit).astype(dtype)


def setup_inputs(seed: int = 0) -> dict:
    streams_of = jax.random.split(jax.random.key(seed), 11)
    tokens = gaussian(streams_of[0], (TOKENS, D), 1.0, 6.0, ((0, 64),))
    norm_gain = jnp.clip(1.0 + 0.1 * jax.random.normal(streams_of[1], (D,), jnp.float32), 0.5, 1.5)
    norm_shift = gaussian(streams_of[2], (D,), 0.3, 4.0, (), jnp.float32)
    qkv_weight = gaussian(streams_of[3], (D, 3, D), (D // 2) ** -0.5, 0.25, ((2, 2),))
    merge_weight = gaussian(streams_of[4], (D, D), (D // 8) ** -0.5, 0.5, ((0, 2),))
    up_weight = gaussian(streams_of[5], (D, FF), D ** -0.5, 0.1875, ((1, 2),))
    inner_shift = gaussian(streams_of[6], (FF,), 0.5, 6.0, ((0, 2),), jnp.float32)
    down_weight = gaussian(streams_of[7], (FF, D), FF ** -0.5, 0.09375, ((0, 2),))
    outer_shift = gaussian(streams_of[8], (D,), 0.5, 6.0, (), jnp.float32)
    cotangent = gaussian(streams_of[9], (TOKENS, D), 1.0, 6.0, ((0, 64),))
    return dict(tokens=tokens, norm_gain=norm_gain, norm_shift=norm_shift, qkv_weight=qkv_weight, merge_weight=merge_weight, up_weight=up_weight, inner_shift=inner_shift, down_weight=down_weight, outer_shift=outer_shift, cotangent=cotangent)


epsilon = 1e-05

@jax.custom_vjp
def low(v):
    return lax.optimization_barrier(v.astype(jnp.bfloat16)).astype(jnp.float32)

@jax.custom_vjp
def low_back(v):
    return v

def low_keep(v):
    return (low(v), None)

def low_pass(kept, grad):
    return (grad,)

def back_keep(v):
    return (v, None)

def back_low(kept, grad):
    return (low(grad),)
low.defvjp(low_keep, low_pass)
low_back.defvjp(back_keep, back_low)

def angle_tables(length):
    half = ROT // 2
    positions = jnp.arange(length).astype(jnp.float32)
    rates = 10000.0 ** (-jnp.arange(half).astype(jnp.float32) / half)
    angles = positions[:, None] * rates[None, :]
    return (jnp.cos(angles)[:, None, :], jnp.sin(angles)[:, None, :])

def rotate(block, cosine, sine):
    half = ROT // 2
    paired = block[..., :ROT].reshape(block.shape[:-1] + (half, 2))
    leading = paired[..., 0]
    trailing = paired[..., 1]
    turned = jnp.stack([leading * cosine - trailing * sine, trailing * cosine + leading * sine], axis=-1)
    turned = turned.reshape(block.shape[:-1] + (ROT,))
    return jnp.concatenate([turned, block[..., ROT:]], axis=-1)

def attend(query, keys, values):
    length = query.shape[1]
    scores = jnp.einsum('gqhd,gkhd->ghqk', query, keys, precision=lax.Precision.HIGHEST) * HEAD ** (-0.5)
    scores = low_back(scores)
    rows = jnp.arange(length)[:, None]
    cols = jnp.arange(length)[None, :]
    scores = jnp.where(cols <= rows, scores, -1e+30)
    peak = lax.optimization_barrier(jnp.max(scores, axis=-1, keepdims=True))
    expo = jnp.exp(scores - peak)
    probs = low(expo / lax.optimization_barrier(jnp.sum(expo, axis=-1, keepdims=True)))
    return jnp.einsum('ghqk,gkhd->gqhd', probs, values, precision=lax.Precision.HIGHEST)

def layer(inputs, norm_gain, norm_shift, qkv_weight, merge_weight, up_weight, inner_shift, down_weight, outer_shift):
    rows_all = inputs.shape[0]
    groups = rows_all // TOK_DEV
    average = lax.optimization_barrier(jnp.mean(inputs, axis=-1, keepdims=True))
    centred = inputs - average
    spread = lax.optimization_barrier(jnp.mean(centred * centred, axis=-1, keepdims=True))
    normed = low(centred * lax.rsqrt(spread + epsilon) * norm_gain + norm_shift)
    joined = low_back(jnp.dot(normed, qkv_weight.reshape(D, 3 * D), precision=lax.Precision.HIGHEST))
    parts = joined.reshape(groups, TOK_DEV, 3, HEADS, HEAD)
    cosine, sine = angle_tables(TOK_DEV)
    query = low(rotate(parts[:, :, 0], cosine, sine))
    keys = low(rotate(parts[:, :, 1], cosine, sine))
    values = low(parts[:, :, 2])
    mixed = jax.checkpoint(attend)(query, keys, values)
    heads_out = low(low_back(mixed)).reshape(rows_all, D)
    attention = jnp.dot(heads_out, merge_weight, precision=lax.Precision.HIGHEST)
    before = low_back(jnp.dot(normed, up_weight, precision=lax.Precision.HIGHEST) + inner_shift)
    active = low(jax.nn.gelu(before, approximate=True))
    feedfwd = jnp.dot(active, down_weight, precision=lax.Precision.HIGHEST)
    return inputs + attention + feedfwd + outer_shift

def reference(tokens, norm_gain, norm_shift, qkv_weight, merge_weight, up_weight, inner_shift, down_weight, outer_shift, cotangent):
    group = math.gcd(N_DP, max(1, 4096 // TOK_DEV))
    rounds = N_DP // group
    params = tuple((item.astype(jnp.float32) for item in (norm_gain, norm_shift, qkv_weight, merge_weight, up_weight, inner_shift, down_weight, outer_shift)))
    inputs = tokens.astype(jnp.float32).reshape(rounds, group * TOK_DEV, D)
    upstream = cotangent.astype(jnp.float32).reshape(rounds, group * TOK_DEV, D)

    def one_round(totals, pair):
        rows_in, rows_up = pair
        output, pullback = jax.vjp(layer, rows_in, *params)
        grads = pullback(rows_up)
        totals = tuple((total + grad for total, grad in zip(totals, grads[1:])))
        return (totals, (output.astype(jnp.bfloat16), grads[0].astype(jnp.bfloat16)))
    start = tuple((jnp.zeros_like(item) for item in params))
    totals, (outputs, token_grads) = lax.scan(one_round, start, (inputs, upstream))
    block_out = outputs.reshape(TOKENS, D)
    token_grad = token_grads.reshape(TOKENS, D)
    return (block_out, token_grad, totals[0], totals[1], totals[2], totals[3], totals[4], totals[5], totals[6], totals[7])
```

```python
import functools

import jax
import jax.numpy as jnp
import numpy as np
from jax import lax
from jax.experimental import pallas as pl
from jax.experimental.pallas import tpu as pltpu
from jax.sharding import Mesh
from jax.sharding import PartitionSpec as P

F32 = jnp.float32
BF16 = jnp.bfloat16
HEAD = 64
ROT = 32
PAIR = 2 * HEAD
epsilon = 1e-05


def nn(a, b):
    return jnp.dot(a, b, preferred_element_type=F32)


def nt(a, b):
    return lax.dot_general(a, b, (((1,), (1,)), ((), ())), preferred_element_type=F32)


def tn(a, b):
    return lax.dot_general(a, b, (((0,), (0,)), ((), ())), preferred_element_type=F32)


def rotary_tables(length):
    half = ROT // 2
    rates = 10000.0 ** (-jnp.arange(half, dtype=F32) / half)
    angles = jnp.arange(length, dtype=F32)[:, None] * rates[None, :]
    cosine = jnp.repeat(jnp.cos(angles), 2, axis=1)
    sine = jnp.repeat(jnp.sin(angles), 2, axis=1)
    sine = sine * jnp.where(jnp.arange(ROT) % 2 == 0, -1.0, 1.0)
    cosine = jnp.concatenate([cosine, jnp.ones((length, HEAD - ROT), F32)], axis=1)
    sine = jnp.concatenate([sine, jnp.zeros((length, HEAD - ROT), F32)], axis=1)
    return jnp.tile(cosine, (1, 2)), jnp.tile(sine, (1, 2))


def swap_pairs(x):
    lane = lax.broadcasted_iota(jnp.int32, x.shape, 1)
    return jnp.where(lane % 2 == 0, pltpu.roll(x, PAIR - 1, 1), pltpu.roll(x, 1, 1))


def project_kernel(tok, gain, shift, w, mw, cot, cos, sin, normed, normed_t, q, k, v, dh):
    x = tok[...].astype(F32)
    centred = x - jnp.mean(x, axis=1, keepdims=True)
    inverse = lax.rsqrt(jnp.mean(centred * centred, axis=1, keepdims=True) + epsilon)
    n = (centred * inverse * gain[...] + shift[...]).astype(BF16)
    normed[...] = n
    normed_t[...] = n.T
    dh[...] = nt(cot[...], mw[...]).astype(BF16)
    c = cos[...]
    s = sin[...]
    for which, ref in enumerate((q, k, v)):
        joined = nn(n, w[which])
        if which == 2:
            ref[...] = joined.astype(BF16)
            continue
        for p in range(joined.shape[1] // PAIR):
            block = joined[:, p * PAIR : (p + 1) * PAIR]
            turned = (block * c + swap_pairs(block) * s).astype(BF16)
            if which == 0:
                turned = turned * jnp.asarray(HEAD**-0.5, BF16)
            ref[:, p * PAIR : (p + 1) * PAIR] = turned


def project(tok, gain, shift, w3, mw, cot, cos, sin, rows=256):
    length, width = tok.shape
    local = mw.shape[0]

    def row_block(n):
        return pl.BlockSpec((rows, n), lambda i: (i, 0))

    def full(*s):
        return pl.BlockSpec(s, lambda i: (0,) * len(s))

    def out(*s):
        return jax.ShapeDtypeStruct(s, BF16)

    return pl.pallas_call(
        project_kernel,
        grid=(length // rows,),
        in_specs=[
            row_block(width),
            full(1, width),
            full(1, width),
            full(3, width, local),
            full(local, width),
            row_block(width),
            row_block(PAIR),
            row_block(PAIR),
        ],
        out_specs=[row_block(width), pl.BlockSpec((width, rows), lambda i: (0, i))]
        + [row_block(local)] * 4,
        out_shape=[out(length, width), out(width, length)] + [out(length, local)] * 4,
        compiler_params=pltpu.CompilerParams(vmem_limit_bytes=48 << 20),
        cost_estimate=pl.CostEstimate(
            flops=8 * length * width * local, bytes_accessed=16 << 20, transcendentals=0
        ),
        name="project",
    )(tok, gain, shift, w3, mw, cot, cos, sin)


def attend_kernel(q, k, v, do, cos, sin, ho, dq, dk, dv, dk_sum, dv_sum, *, block):
    length = q.shape[0]
    lane = lax.broadcasted_iota(jnp.int32, (block, PAIR), 1)
    causal = lax.broadcasted_iota(jnp.int32, (block, block), 1) <= lax.broadcasted_iota(
        jnp.int32, (block, block), 0
    )
    dk_sum[...] = jnp.zeros_like(dk_sum)
    dv_sum[...] = jnp.zeros_like(dv_sum)
    zero = jnp.zeros((block, PAIR), BF16)
    for i in range(length // block):
        rows = slice(i * block, (i + 1) * block)
        seen = (i + 1) * block
        q_rows = q[rows, :]
        do_rows = do[rows, :]
        keys = k[0:seen, :]
        values = v[0:seen, :]
        mixed = d_query = None
        for h in range(2):
            mine = (lane < HEAD) if h == 0 else (lane >= HEAD)
            q_head = jnp.where(mine, q_rows, zero)
            do_head = jnp.where(mine, do_rows, zero)
            scores = nt(q_head, keys)
            edge = jnp.where(causal, scores[:, seen - block :], -1e30)
            if i > 0:
                edge = jnp.concatenate([scores[:, : seen - block], edge], axis=1)
            scores = edge
            expo = jnp.exp(scores - jnp.max(scores, axis=1, keepdims=True))
            probs = expo * (1.0 / jnp.sum(expo, axis=1, keepdims=True))
            probs_low = probs.astype(BF16)
            mixed_head = nn(probs_low, values)
            d_probs = nt(do_head, values)
            inner = jnp.sum(probs * d_probs, axis=1, keepdims=True)
            d_scores = (probs * (d_probs - inner)).astype(BF16)
            d_query_head = nn(d_scores, keys)
            dv_sum[0:seen, :] += tn(probs_low, do_head)
            dk_sum[0:seen, :] += tn(d_scores, q_head)
            mixed = mixed_head if h == 0 else jnp.where(mine, mixed_head, mixed)
            d_query = d_query_head if h == 0 else jnp.where(mine, d_query_head, d_query)
        ho[rows, :] = mixed.astype(BF16)
        d_query = d_query * HEAD**-0.5
        dq[rows, :] = (d_query * cos[rows, :] - swap_pairs(d_query) * sin[rows, :]).astype(BF16)
    for i in range(length // block):
        rows = slice(i * block, (i + 1) * block)
        d_keys = dk_sum[rows, :]
        dk[rows, :] = (d_keys * cos[rows, :] - swap_pairs(d_keys) * sin[rows, :]).astype(BF16)
        dv[rows, :] = dv_sum[rows, :].astype(BF16)


def attend(q, k, v, do, cos, sin, block=512):
    length, local = q.shape
    pairs = local // PAIR
    spec = pl.BlockSpec((length, PAIR), lambda p: (0, p))
    table = pl.BlockSpec((length, PAIR), lambda p: (0, 0))
    out = jax.ShapeDtypeStruct((length, local), BF16)
    return pl.pallas_call(
        functools.partial(attend_kernel, block=block),
        grid=(pairs,),
        in_specs=[spec] * 4 + [table] * 2,
        out_specs=[spec] * 4,
        out_shape=[out] * 4,
        scratch_shapes=[pltpu.VMEM((length, PAIR), F32)] * 2,
        compiler_params=pltpu.CompilerParams(vmem_limit_bytes=48 << 20),
        cost_estimate=pl.CostEstimate(
            flops=20 * length * length * PAIR * pairs,
            bytes_accessed=8 << 20,
            transcendentals=length * length * pairs,
        ),
        name="attend",
    )(q, k, v, do, cos, sin)


gelu_rate = float(np.sqrt(2 / np.pi))


def feed_kernel(normed, normed_t, cot, up, shift, down, out, dn, dg, ug, ig):
    j = pl.program_id(0)
    n = normed[...]
    c = cot[...]
    v = nn(n, up[...]) + shift[...]
    da = nt(c, down[...])
    square = v * v
    t = jnp.tanh(gelu_rate * v * (1.0 + 0.044715 * square))
    h = 0.5 * (1.0 + t)
    active = (v * h).astype(BF16)
    slope = h + (0.5 * gelu_rate) * v * (1.0 - t * t) * (1.0 + (3 * 0.044715) * square)
    d_pre = (da * slope).astype(BF16)
    ig[...] = jnp.sum(d_pre.astype(F32), axis=0, keepdims=True)
    o = nn(active, down[...])
    d = nt(d_pre, up[...])

    @pl.when(j == 0)
    def _():
        out[...] = o
        dn[...] = d

    @pl.when(j > 0)
    def _():
        out[...] += o
        dn[...] += d

    grad = tn(active, c)
    for y in range(4):
        for core in range(2):
            rows = grad.shape[0] // 8
            first = (2 * y + core) * rows
            for z in range(4):
                spot = spot_of(z, y, core, 0)

                @pl.when(j == z)
                def _():
                    dg[core * 16 + spot] = grad[first : first + rows, :]

    grad = nn(normed_t[...], d_pre)
    for z in range(4):
        for y in range(4):
            for core in range(2):
                rows = grad.shape[0] // 32
                first = ((z * 4 + y) * 2 + core) * rows
                ug[core * 16 + spot_of(z, y, core, 1)] = grad[first : first + rows, :]


def feed(normed, normed_t, cot, up, shift, down):
    length, width = normed.shape
    hidden = up.shape[1]
    step = hidden // 4

    def full(*s):
        return pl.BlockSpec(s, lambda i: (0,) * len(s))

    return pl.pallas_call(
        feed_kernel,
        grid=(4,),
        in_specs=[
            full(length, width),
            full(width, length),
            full(length, width),
            pl.BlockSpec((width, step), lambda i: (0, i)),
            pl.BlockSpec((1, step), lambda i: (0, i)),
            pl.BlockSpec((step, width), lambda i: (i, 0)),
        ],
        out_specs=[
            full(length, width),
            full(length, width),
            full(32, hidden // 32, width),
            pl.BlockSpec((32, width // 32, step), lambda i: (0, 0, i)),
            pl.BlockSpec((1, step), lambda i: (0, i)),
        ],
        out_shape=[
            jax.ShapeDtypeStruct(s, F32)
            for s in (
                (length, width),
                (length, width),
                (32, hidden // 32, width),
                (32, width // 32, hidden),
                (1, hidden),
            )
        ],
        compiler_params=pltpu.CompilerParams(vmem_limit_bytes=60 << 20),
        cost_estimate=pl.CostEstimate(
            flops=12 * length * width * hidden,
            bytes_accessed=36 << 20,
            transcendentals=length * hidden,
        ),
        name="feed",
    )(normed, normed_t, cot, up, shift, down)


def tail_kernel(normed_t, ho, cot, dq, dk, dv, grads):
    which = pl.program_id(0)
    n = normed_t[...]
    for w, ref in enumerate((dq, dk, dv)):

        @pl.when(which == w)
        def _():
            grads[0] = nn(n, ref[...])

    @pl.when(which == 3)
    def _():
        g = tn(ho[...], cot[...])
        half = g.shape[1] // 2
        grads[0, :half, :] = g[:, :half]
        grads[0, half:, :] = g[:, half:]


def tail_grads(normed_t, ho, cot, dq, dk, dv):
    width, length = normed_t.shape
    local = ho.shape[1]
    assert 2 * local == width

    def full(*s):
        return pl.BlockSpec(s, lambda i: (0,) * len(s))

    return pl.pallas_call(
        tail_kernel,
        grid=(4,),
        in_specs=[full(width, length), full(length, local), full(length, width)]
        + [full(length, local)] * 3,
        out_specs=pl.BlockSpec((1, width, local), lambda i: (i, 0, 0)),
        out_shape=jax.ShapeDtypeStruct((4, width, local), F32),
        compiler_params=pltpu.CompilerParams(vmem_limit_bytes=48 << 20),
        cost_estimate=pl.CostEstimate(
            flops=8 * length * width * local, bytes_accessed=16 << 20, transcendentals=0
        ),
        name="tail",
    )(normed_t, ho, cot, dq, dk, dv)


AXES = ("xlo", "z", "y", "core", "tensor")
RINGS = ("z", "y", "core")
DIRECTIONS = (("y", 0), ("z", 0), ("y", 1), ("z", 1))
SWAP = ((0, 1), (1, 0))


def partner(place, bit):
    return place ^ 1 if bit == 0 else 3 - place


def bit_at(place, bit):
    return int(place in (1, 2)) if bit == 0 else int(place >= 2)


def order_of(core, part):
    return [(core + 2 * part + step) % 4 for step in range(4)]


def spot_of(z, y, core, part):
    spot = 0
    for direction in order_of(core, part):
        axis, bit = DIRECTIONS[direction]
        spot = 2 * spot + bit_at(y if axis == "y" else z, bit)
    return spot


def step_pairs(part, step):
    pairs = []
    for z in range(4):
        for y in range(4):
            for core in range(2):
                axis, bit = DIRECTIONS[order_of(core, part)[step]]
                z2, y2 = (z, partner(y, bit)) if axis == "y" else (partner(z, bit), y)
                pairs.append(((z * 4 + y) * 2 + core, (z2 * 4 + y2) * 2 + core))
    return pairs


def step_bit(part, step):
    table = np.zeros((32,), np.int32)
    for z in range(4):
        for y in range(4):
            for core in range(2):
                axis, bit = DIRECTIONS[order_of(core, part)[step]]
                table[(z * 4 + y) * 2 + core] = bit_at(y if axis == "y" else z, bit)
    return jnp.asarray(table)[lax.axis_index(RINGS)]


def halves(x, bit):
    h = x.shape[0] // 2
    keep = lax.dynamic_slice_in_dim(x, bit * h, h, 0)
    send = lax.dynamic_slice_in_dim(x, (1 - bit) * h, h, 0)
    return keep, send


def scatter_rings(x, part):
    for step in range(4):
        keep, send = halves(x, step_bit(part, step))
        x = keep + lax.ppermute(send, RINGS, step_pairs(part, step))
    return x


def gather_rings(x, part):
    for step in reversed(range(4)):
        other = lax.ppermute(x, RINGS, step_pairs(part, step))
        first = step_bit(part, step) == 0
        x = jnp.where(
            first, jnp.concatenate([x, other], axis=0), jnp.concatenate([other, x], axis=0)
        )
    return x


def exchange(x, axis):
    return lax.ppermute(x, axis, SWAP)


def sum_small(v):
    for step in range(4):
        v = v + lax.ppermute(v, RINGS, step_pairs(0, step))
    v = v + exchange(v, "core")
    return v + exchange(v, "xlo")


def body(
    tokens,
    norm_gain,
    norm_shift,
    qkv_weight,
    merge_weight,
    up_weight,
    inner_shift,
    down_weight,
    outer_shift,
    cotangent,
):
    length, width = tokens.shape
    local = merge_weight.shape[0]
    hidden = up_weight.shape[1]
    core = lax.axis_index("core")
    cos, sin = rotary_tables(length)
    w3 = qkv_weight.transpose(1, 0, 2)
    gain, shift = norm_gain[None], norm_shift[None]
    normed, normed_t, q, k, v, dh = project(
        tokens, gain, shift, w3, merge_weight, cotangent, cos, sin
    )
    out_ffn, dn_ffn, down_g, up_g, inner_g = feed(
        normed, normed_t, cotangent, up_weight, inner_shift[None], down_weight
    )

    down_keep, down_send = halves(down_g, core)
    up_keep, up_send = halves(up_g, core)
    down_x = down_keep + exchange(down_send, "core")
    up_x = up_keep + exchange(up_send, "core")
    down_x = scatter_rings(down_x, 0)
    up_x = scatter_rings(up_x, 1)
    down_x = (down_x + exchange(down_x, "xlo")).reshape(hidden // 32, width)
    up_x = (up_x + exchange(up_x, "xlo")).reshape(width // 32, hidden)
    down_out = lax.all_gather(down_x, RINGS, tiled=True)
    up_out = lax.all_gather(up_x, RINGS, tiled=True)

    ho, dq, dk, dv = attend(q, k, v, dh, cos, sin)

    inputs = tokens.astype(F32)
    average = jnp.mean(inputs, axis=-1, keepdims=True)
    centred = inputs - average
    inverse = lax.rsqrt(jnp.mean(centred * centred, axis=-1, keepdims=True) + epsilon)
    unit = centred * inverse
    upstream = cotangent.astype(F32)

    chunks = 2
    rows = length // chunks
    slices = [slice(i * rows, (i + 1) * rows) for i in range(chunks)]
    outs = []
    for r in slices:
        mine = nn(ho[r], merge_weight) + out_ffn[r]
        outs.append((inputs[r] + (mine + exchange(mine, "tensor")) + outer_shift).astype(BF16))
    block_out = jnp.concatenate(outs, axis=0)

    grads = []
    gain_g = jnp.zeros((width,), F32)
    shift_g = jnp.zeros((width,), F32)
    for r in slices:
        mine = dn_ffn[r] + nt(dq[r], w3[0]) + nt(dk[r], w3[1]) + nt(dv[r], w3[2])
        gain_g = gain_g + jnp.sum(mine * unit[r], axis=0)
        shift_g = shift_g + jnp.sum(mine, axis=0)
        d_normed = mine + exchange(mine, "tensor")
        d_unit = d_normed * norm_gain
        centre = jnp.mean(d_unit, axis=-1, keepdims=True)
        slope = jnp.mean(d_unit * unit[r], axis=-1, keepdims=True)
        grads.append((upstream[r] + inverse[r] * (d_unit - centre - unit[r] * slope)).astype(BF16))
    token_grad = jnp.concatenate(grads, axis=0)

    late = tail_grads(normed_t, ho, cotangent, dq, dk, dv)
    late_keep, late_send = halves(late, core)
    late_x = late_keep + exchange(late_send, "core")
    parts = [scatter_rings(late_x[i], i) for i in range(2)]
    parts = [x + exchange(x, "xlo") for x in parts]
    parts = [gather_rings(x, i) for i, x in enumerate(parts)]
    own = jnp.stack(parts)
    other = exchange(own, "core")
    first = core == 0
    qkv_out = jnp.stack(
        [
            jnp.where(first, own[0], other[0]),
            jnp.where(first, own[1], other[1]),
            jnp.where(first, other[0], own[0]),
        ],
        axis=1,
    )
    merge_out = jnp.where(first, other[1], own[1])
    merge_out = jnp.concatenate([merge_out[:local], merge_out[local:]], axis=1)

    small = jnp.concatenate(
        [
            gain_g[None],
            shift_g[None],
            jnp.sum(upstream, axis=0)[None],
            inner_g.reshape(hidden // width, width),
            jnp.zeros((8 - 3 - hidden // width, width), F32),
        ],
        axis=0,
    )
    small = sum_small(small)
    pair = small[:2] + exchange(small[:2], "tensor")
    return (
        block_out,
        token_grad,
        pair[0],
        pair[1],
        qkv_out,
        merge_out,
        up_out,
        small[3 : 3 + hidden // width].reshape(hidden),
        down_out,
        small[2],
    )


def solution(mesh):
    dp = AXES[:4]
    finer = Mesh(mesh.devices.reshape(2, 4, 4, 2, 2), AXES)
    return jax.shard_map(
        body,
        mesh=finer,
        in_specs=(
            P(dp, None),
            P(),
            P(),
            P(None, None, "tensor"),
            P("tensor", None),
            P(None, "tensor"),
            P("tensor"),
            P("tensor", None),
            P(),
            P(dp, None),
        ),
        out_specs=(
            P(dp, None),
            P(dp, None),
            P(),
            P(),
            P(None, None, "tensor"),
            P("tensor", None),
            P(None, "tensor"),
            P("tensor"),
            P("tensor", None),
            P(),
        ),
        check_vma=False,
    )
```

```python
import functools

import jax
import jax.numpy as jnp
import numpy as np
from jax import lax
from jax.experimental import pallas as pl
from jax.experimental.pallas import tpu as pltpu
from jax.sharding import Mesh
from jax.sharding import PartitionSpec as P

F32 = jnp.float32
BF16 = jnp.bfloat16
HEAD = 64
ROT = 32
PAIR = 2 * HEAD
epsilon = 1e-05


def nn(a, b):
    return jnp.dot(a, b, preferred_element_type=F32)


def nt(a, b):
    return lax.dot_general(a, b, (((1,), (1,)), ((), ())), preferred_element_type=F32)


def tn(a, b):
    return lax.dot_general(a, b, (((0,), (0,)), ((), ())), preferred_element_type=F32)


def rotary_tables(length):
    half = ROT // 2
    rates = np.float32(10000.0) ** (-np.arange(half, dtype=np.float32) / np.float32(half))
    angles = np.arange(length, dtype=np.float32)[:, None] * rates[None, :].astype(np.float32)
    angles = np.repeat(angles, 2, axis=1)
    sign = np.where(np.arange(ROT) % 2 == 0, -1.0, 1.0)
    rest = np.ones((length, HEAD - ROT))
    cosine = np.concatenate([np.cos(angles), rest], axis=1)
    sine = np.concatenate([np.sin(angles) * sign, 0 * rest], axis=1)
    return tuple(jnp.asarray(np.tile(x, (1, 2)).astype(np.float32)) for x in (cosine, sine))


def swap_pairs(x):
    lane = lax.broadcasted_iota(jnp.int32, x.shape, 1)
    return jnp.where(lane % 2 == 0, pltpu.roll(x, PAIR - 1, 1), pltpu.roll(x, 1, 1))


def launch(kernel, name, grid, scalars, after, ins, outs, scratch=(), vmem=16, flops=0):
    first, skipped = len(scalars), len(after)

    def without(*refs):
        kernel(*refs[:first], *refs[first + skipped :])

    got = pl.pallas_call(
        without,
        grid_spec=pltpu.PrefetchScalarGridSpec(
            num_scalar_prefetch=first,
            grid=grid,
            in_specs=[pl.BlockSpec(memory_space=pltpu.HBM)] * skipped + [spec for _, spec in ins],
            out_specs=[spec for _, _, spec in outs],
            scratch_shapes=list(scratch),
        ),
        out_shape=[jax.ShapeDtypeStruct(shape, dtype) for shape, dtype, _ in outs],
        compiler_params=pltpu.CompilerParams(vmem_limit_bytes=vmem << 20),
        cost_estimate=pl.CostEstimate(
            flops=flops,
            bytes_accessed=sum(x.size * x.dtype.itemsize for x, _ in ins)
            + sum(int(np.prod(shape)) * jnp.dtype(dtype).itemsize for shape, dtype, _ in outs),
            transcendentals=0,
        ),
        name=name,
    )(*scalars, *after, *[array for array, _ in ins])
    return got


def whole(*shape):
    return pl.BlockSpec(shape, lambda *_: (0,) * len(shape))


def once(*shape):
    return pl.BlockSpec(shape, lambda *_: (0,) * len(shape), pipeline_mode=pl.Buffered(1))


gelu_rate = float(np.sqrt(2 / np.pi))


def norm_rows(x):
    centred = x - jnp.mean(x, axis=1, keepdims=True)
    inverse = lax.rsqrt(jnp.mean(centred * centred, axis=1, keepdims=True) + epsilon)
    return centred * inverse, inverse


def project_kernel(tok, gain, shift, w, mw, cot, cos, sin, normed, normed_t, q, k, v, dh, outer):
    unit, _ = norm_rows(tok[...].astype(F32))
    n = (unit * gain[...] + shift[...]).astype(BF16)
    normed[...] = n
    normed_t[...] = n.T
    dh[...] = nt(cot[...], mw[...]).astype(BF16)
    total = jnp.sum(cot[...].astype(F32), axis=0, keepdims=True)

    @pl.when(pl.program_id(0) == 0)
    def _():
        outer[...] = total

    @pl.when(pl.program_id(0) > 0)
    def _():
        outer[...] += total

    c = cos[...]
    s = sin[...]
    for which, ref in enumerate((q, k, v)):
        joined = nn(n, w[which])
        if which == 2:
            ref[...] = joined.astype(BF16)
            continue
        for p in range(joined.shape[1] // PAIR):
            block = joined[:, p * PAIR : (p + 1) * PAIR]
            turned = (block * c + swap_pairs(block) * s).astype(BF16)
            if which == 0:
                turned = turned * jnp.asarray(HEAD**-0.5, BF16)
            ref[:, p * PAIR : (p + 1) * PAIR] = turned


def project(tok, gain, shift, w3, mw, cot, cos, sin, rows=256):
    length, width = tok.shape
    local = mw.shape[0]

    def row_block(n):
        return pl.BlockSpec((rows, n), lambda i: (i, 0))

    def out(n):
        return ((length, n), BF16, row_block(n))

    return launch(
        project_kernel,
        "project",
        (length // rows,),
        (),
        (),
        [
            (tok, row_block(width)),
            (gain, whole(1, width)),
            (shift, whole(1, width)),
            (w3, once(3, width, local)),
            (mw, once(local, width)),
            (cot, row_block(width)),
            (cos, row_block(PAIR)),
            (sin, row_block(PAIR)),
        ],
        [out(width), ((width, length), BF16, pl.BlockSpec((width, rows), lambda i: (0, i)))]
        + [out(local)] * 4
        + [((1, width), F32, whole(1, width))],
        vmem=60,
        flops=8 * length * width * local,
    )


def hidden_kernel(normed, cot, up, shift, down, out, dn, act, dpre, ig, *, cols):
    n = normed[...]
    c = cot[...]
    sums = []
    for j in range(up.shape[1] // cols):
        s = slice(j * cols, (j + 1) * cols)
        v = nn(n, up[:, s]) + shift[:, s]
        da = nt(c, down[s, :])
        square = v * v
        t = jnp.tanh(gelu_rate * v * (1.0 + 0.044715 * square))
        h = 0.5 * (1.0 + t)
        act[:, s] = (v * h).astype(BF16)
        slope = h + (0.5 * gelu_rate) * v * (1.0 - t * t) * (1.0 + (3 * 0.044715) * square)
        d_pre = (da * slope).astype(BF16)
        dpre[:, s] = d_pre
        sums.append(jnp.sum(d_pre.astype(F32), axis=0, keepdims=True))
    sums = jnp.concatenate(sums, axis=1)

    @pl.when(pl.program_id(0) == 0)
    def _():
        ig[...] = sums

    @pl.when(pl.program_id(0) > 0)
    def _():
        ig[...] += sums

    out[...] = nn(act[...], down[...])
    dn[...] = nt(dpre[...], up[...])


def hidden_pass(after, normed, cot, up, shift, down, rows=256, cols=512):
    length, width = normed.shape
    hidden = up.shape[1]

    def here(n):
        return pl.BlockSpec((rows, n), lambda i: (i, 0))

    return launch(
        functools.partial(hidden_kernel, cols=cols),
        "hidden",
        (length // rows,),
        (),
        after,
        [
            (normed, here(width)),
            (cot, here(width)),
            (up, once(width, hidden)),
            (shift, whole(1, hidden)),
            (down, once(hidden, width)),
        ],
        [((length, width), F32, here(width))] * 2
        + [((length, hidden), BF16, here(hidden))] * 2
        + [((1, hidden), F32, whole(1, hidden))],
        vmem=60,
        flops=9 * length * width * hidden,
    )


def grad_kernel(place, lhs, rhs, *rest, base, product, own):
    if own:
        got, keep, send, buf, sems, land, land_sems = rest
    else:
        out, buf, sems = rest
    j = pl.program_id(0)
    size = buf.shape[1] // 8

    def arriving(n):
        return pltpu.make_async_copy(
            got.at[place[base + n]], land.at[pl.ds(n * size, size)], land_sems.at[n]
        )

    if own:

        @pl.when(j == 0)
        def _():
            for n in range(16):
                arriving(n).start()

    buf[j] = product(lhs[...], rhs[...])
    if own:

        @pl.when(j == 0)
        def _():
            for n in range(8):
                arriving(n).wait()

        @pl.when(j == 1)
        def _():
            for n in range(8, 16):
                arriving(n).wait()

        buf[j] += land[pl.ds(pl.multiple_of(j * 8 * size, size), 8 * size), :]

    for i in range(8):
        spot = place[base + j * 8 + i]
        block = buf.at[j, pl.ds(i * size, size)]
        sem = sems.at[j * 8 + i]
        if own:

            @pl.when(spot < 8)
            def _():
                pltpu.make_async_copy(block, keep.at[spot], sem).start()

            @pl.when(spot >= 8)
            def _():
                pltpu.make_async_copy(block, send.at[spot - 8], sem).start()

        else:
            pltpu.make_async_copy(block, out.at[spot], sem).start()

    @pl.when(j == 1)
    def _():
        for n in range(16):
            block = buf.at[n // 8, pl.ds((n % 8) * size, size)]
            pltpu.make_async_copy(block, (keep if own else out).at[0], sems.at[n]).wait()


def grad(place, base, spots, after, lhs, rhs, specs, product, got=None):
    width = 1024
    rows = 1024
    own = got is not None
    piece = rows // 16
    anywhere = pl.BlockSpec(memory_space=pltpu.HBM)
    scratch = [pltpu.VMEM((2, rows // 2, width), F32), pltpu.SemaphoreType.DMA((16,))]
    if own:
        scratch += [pltpu.VMEM((rows, width), F32), pltpu.SemaphoreType.DMA((16,))]
    outs = [((8 if own else 16, piece, width), F32, anywhere)] * (2 if own else 1)
    return launch(
        functools.partial(grad_kernel, base=spots, product=product, own=own),
        "grad",
        (2,),
        (place,),
        after,
        [(lhs, specs[0]), (rhs, specs[1])] + ([(got, anywhere)] if own else []),
        outs,
        scratch,
        vmem=24,
        flops=2 * rows * width * lhs.shape[0],
    )


def down_grad(place, base, after, active, cot, got=None):
    length, width = cot.shape
    block = pl.BlockSpec((length, 512), lambda j, place: (0, place[base] * 2 + j))
    return grad(
        place, base, base + 1, after, active, cot, (block, once(length, width)), tn, got
    )


def up_grad(place, base, after, normed_t, d_pre, got=None):
    width, length = normed_t.shape
    rows = pl.BlockSpec((512, length), lambda j, _: (j, 0))
    half = pl.BlockSpec(
        (length, 1024), lambda j, place: (0, place[base]), pipeline_mode=pl.Buffered(1)
    )
    return grad(place, base, base + 17, after, normed_t, d_pre, (rows, half), nn, got)


def attend_kernel(*refs, last, sub):
    if last:
        q, do, k, v, dk_in, dv_in, cos, sin, ho, dq, dk, dv, dk_sum, dv_sum = refs
    else:
        q, do, k, v, cos, sin, ho, dq, dk_sum, dv_sum = refs
    block = q.shape[0]
    seen = k.shape[0]
    low = lax.broadcasted_iota(jnp.int32, (sub, PAIR), 1) < HEAD
    zero = jnp.zeros((sub, PAIR), BF16)
    causal = lax.broadcasted_iota(jnp.int32, (sub, sub), 1) <= lax.broadcasted_iota(
        jnp.int32, (sub, sub), 0
    )
    for i in range(block // sub):
        before = seen - block + i * sub
        upto = before + sub
        rows = slice(i * sub, (i + 1) * sub)
        keys = k[0:upto, :]
        values = v[0:upto, :]
        heads = [
            [jnp.where(low, x[rows, :], zero), jnp.where(low, zero, x[rows, :])] for x in (q, do)
        ]
        scores = [nt(x, keys) for x in heads[0]]
        d_probs = [nt(x, values) for x in heads[1]]
        probs_low, d_scores = [], []
        for h in range(2):
            edge = jnp.where(causal, scores[h][:, before:], -1e30)
            if before:
                edge = jnp.concatenate([scores[h][:, :before], edge], axis=1)
            expo = jnp.exp(edge - jnp.max(edge, axis=1, keepdims=True))
            probs = expo * (1.0 / jnp.sum(expo, axis=1, keepdims=True))
            inner = jnp.sum(probs * d_probs[h], axis=1, keepdims=True)
            probs_low.append(probs.astype(BF16))
            d_scores.append((probs * (d_probs[h] - inner)).astype(BF16))
        mixed = [nn(x, values) for x in probs_low]
        ho[rows, :] = jnp.where(low, mixed[0], mixed[1]).astype(BF16)
        d_query = [nn(x, keys) for x in d_scores]
        d_query = jnp.where(low, d_query[0], d_query[1]) * HEAD**-0.5
        turn = slice(before, upto)
        dq[rows, :] = (
            d_query * cos[turn, :] - swap_pairs(d_query) * sin[turn, :]
        ).astype(BF16)
        for left, right, total in ((probs_low, heads[1], dv_sum), (d_scores, heads[0], dk_sum)):
            add = tn(left[0], right[0]) + tn(left[1], right[1])
            if i == 0:
                total[0:upto, :] = add
            else:
                total[0:before, :] += add[:before]
                total[before:upto, :] = add[before:]
    if last:
        before = seen - block
        dk_sum[0:before, :] += dk_in[...]
        dv_sum[0:before, :] += dv_in[...]
        for i in range(seen // block):
            rows = slice(i * block, (i + 1) * block)
            d_keys = dk_sum[rows, :]
            dk[rows, :] = (d_keys * cos[rows, :] - swap_pairs(d_keys) * sin[rows, :]).astype(BF16)
            dv[rows, :] = dv_sum[rows, :].astype(BF16)


def attend(part, after, q, k, v, do, cos, sin, carried=(), sub=256):
    length, local = q.shape
    half = length // 2
    seen = half * (part + 1)
    rows = pl.BlockSpec((half, PAIR), lambda p: (part, p))
    keys = pl.BlockSpec((seen, PAIR), lambda p: (0, p))
    table = pl.BlockSpec((seen, PAIR), lambda p: (0, 0))
    here = pl.BlockSpec((half, PAIR), lambda p: (0, p))
    outs = [((half, local), BF16, here)] * 2
    scratch = ()
    if part == 0:
        outs += [((half, local), F32, here)] * 2
    else:
        outs += [((length, local), BF16, keys)] * 2
        scratch = [pltpu.VMEM((length, PAIR), F32)] * 2
    return launch(
        functools.partial(attend_kernel, last=part == 1, sub=sub),
        "attend",
        (local // PAIR,),
        (),
        after,
        [(q, rows), (do, rows), (k, keys), (v, keys)]
        + [(x, here) for x in carried]
        + [(cos, table), (sin, table)],
        outs,
        scratch,
        flops=30 * half * seen * PAIR * local // PAIR,
    )


def forward_kernel(ho, mw, a, *pieces, cuts):
    i = pl.program_id(0)
    total = nn(ho[...], mw[...]) + a[...]
    for n, piece in enumerate(pieces):

        @pl.when(jnp.logical_and(i >= cuts[n], i < cuts[n + 1]))
        def _():
            piece[...] = total


def within(first, last):
    return lambda i, *_: (jnp.clip(i, first, last - 1) - first, 0)


def cut_specs(sizes, rows, width):
    cuts = [int(n) // rows for n in np.cumsum((0,) + tuple(sizes))]
    return cuts, [
        pl.BlockSpec((rows, width), within(cuts[k], cuts[k + 1])) for k in range(len(sizes))
    ]


def forward_part(part, after, ho, mw, a, sizes, rows=128):
    half, local = ho.shape
    width = mw.shape[1]
    steps = half // rows
    cuts, specs = cut_specs(sizes, rows, width)
    there = pl.BlockSpec((rows, width), lambda i: (part * steps + i, 0))
    return launch(
        functools.partial(forward_kernel, cuts=cuts),
        "forward",
        (steps,),
        (),
        after,
        [
            (ho, pl.BlockSpec((rows, local), lambda i: (i, 0))),
            (mw, once(local, width)),
            (a, there),
        ],
        [((n, width), F32, spec) for n, spec in zip(sizes, specs)],
        flops=2 * half * width * local,
    )


def backward_kernel(dq0, dq1, dk, dv, w, a, tok, *rest, cuts):
    pieces, sums = rest[:-1], rest[-1]
    i = pl.program_id(0)

    def one(dq):
        total = nt(dq[...], w[0]) + nt(dk[...], w[1]) + nt(dv[...], w[2]) + a[...]
        for n, piece in enumerate(pieces):

            @pl.when(jnp.logical_and(i >= cuts[n], i < cuts[n + 1]))
            def _():
                piece[...] = total

        unit, _ = norm_rows(tok[...].astype(F32))
        both = jnp.concatenate(
            [jnp.sum(total * unit, axis=0, keepdims=True), jnp.sum(total, axis=0, keepdims=True)],
            axis=0,
        )

        @pl.when(i == 0)
        def _():
            sums[...] = both

        @pl.when(i > 0)
        def _():
            sums[...] += both

    half = pl.num_programs(0) // 2

    @pl.when(i < half)
    def _():
        one(dq0)

    @pl.when(i >= half)
    def _():
        one(dq1)


def backward_pass(after, dq0, dq1, dk, dv, w3, a, tok, sizes, rows=256):
    length, local = dk.shape
    width = w3.shape[1]
    steps = length // rows
    cuts, specs = cut_specs(sizes, rows, width)
    here = pl.BlockSpec((rows, width), lambda i: (i, 0))
    narrow = pl.BlockSpec((rows, local), lambda i: (i, 0))
    return launch(
        functools.partial(backward_kernel, cuts=cuts),
        "backward",
        (steps,),
        (),
        after,
        [
            (dq0, pl.BlockSpec((rows, local), within(0, steps // 2))),
            (dq1, pl.BlockSpec((rows, local), within(steps // 2, steps))),
            (dk, narrow),
            (dv, narrow),
            (w3, once(3, width, local)),
            (a, here),
            (tok, here),
        ],
        [((n, width), F32, spec) for n, spec in zip(sizes, specs)]
        + [((2, width), F32, whole(2, width))],
        vmem=60,
        flops=6 * length * width * local,
    )


def hand_kernel(*refs):
    for x, out in zip(refs[: len(refs) // 2], refs[len(refs) // 2 :]):
        out[...] = x[...]


def hand(after, *arrays):
    def block(x):
        return pl.BlockSpec((x.shape[0] // 4, x.shape[1]), lambda i: (i, 0))

    return launch(
        hand_kernel,
        "hand",
        (4,),
        (),
        after,
        [(x, block(x)) for x in arrays],
        [(x.shape, F32, block(x)) for x in arrays],
    )


def tail_kernel(place, normed_t, ho0, ho1, cot, dq0, dq1, dk, dv, *rest, base, bits, own):
    if own:
        small, got0, got1, keep0, send0, keep1, send1, g0, g1 = rest
    else:
        g0, g1 = rest
    n = normed_t[...]
    half = dq0.shape[0]
    width = g0.shape[0]

    def put(ref, x):
        rows = x.shape[0] // 2
        ref[:rows, :] = x[:rows]
        ref[rows + ROOM : 2 * rows + ROOM, :] = x[rows:]

    blank = jnp.zeros((ROOM, g1.shape[1]), F32)
    g1[width // 2 : width // 2 + ROOM, :] = blank
    g1[width + ROOM :, :] = blank

    @pl.when(place[base] == 0)
    def _():
        g0[...] = nn(n[:, :half], dq0[...]) + nn(n[:, half:], dq1[...])
        put(g1, nn(n, dk[...]))

    @pl.when(place[base] == 1)
    def _():
        g0[...] = nn(n, dv[...])
        g = tn(ho0[...], cot[:half, :]) + tn(ho1[...], cot[half:, :])
        columns = g.shape[1] // 2
        g1[:columns, :] = g[:, :columns]
        g1[columns + ROOM : 2 * columns + ROOM, :] = g[:, columns:]

    if own:
        g1[width // 2 : width // 2 + small.shape[0], :] = small[...]
        for g, got, keep, send, bit in (
            (g0, got0, keep0, send0, bits[0]),
            (g1, got1, keep1, send1, bits[1]),
        ):
            h = keep.shape[0]
            stay = pl.ds(pl.multiple_of(place[bit] * h, h), h)
            go = pl.ds(pl.multiple_of((1 - place[bit]) * h, h), h)
            keep[...] = g[stay, :] + got[stay, :]
            send[...] = g[go, :] + got[go, :]


ROOM = 64


def tail(place, base, bits, after, normed_t, ho0, ho1, cot, dq0, dq1, dk, dv, small=None, got=()):
    width, length = normed_t.shape
    local = dk.shape[1]
    half = length // 2
    assert 2 * local == width
    own = small is not None
    shapes = [(width, local), (width + 2 * ROOM, local)]
    if own:
        outs = [(n // 2, local) for n, _ in shapes for _ in range(2)]
    else:
        outs = shapes
    return launch(
        functools.partial(tail_kernel, base=base, bits=bits, own=own),
        "tail",
        (1,),
        (place,),
        after,
        [(normed_t, once(width, length))]
        + [(x, once(half, local)) for x in (ho0, ho1)]
        + [(cot, once(length, width))]
        + [(x, once(half, local)) for x in (dq0, dq1)]
        + [(x, once(length, local)) for x in (dk, dv)]
        + ([(x, once(*x.shape)) for x in (small, *got)] if own else []),
        [(shape, F32, once(*shape)) for shape in outs],
        [pltpu.VMEM(shape, F32) for shape in shapes] if own else (),
        vmem=28,
        flops=4 * length * width * local,
    )


def finish_kernel(*refs, cuts, last):
    n = len(cuts) - 1
    wide, (mine, got), (row, out) = refs[: -2 * n - 2], (refs[-2 * n - 2 : -n - 2], refs[-n - 2 : -2]), refs[-2:]
    i = pl.program_id(0)
    x = wide[0][...].astype(F32)

    def one(total):
        if not last:
            out[...] = (x + total + row[...]).astype(BF16)
            return
        unit, inverse = norm_rows(x)
        d_unit = total * row[...]
        centre = jnp.mean(d_unit, axis=1, keepdims=True)
        slope = jnp.mean(d_unit * unit, axis=1, keepdims=True)
        out[...] = (
            wide[1][...].astype(F32) + inverse * (d_unit - centre - unit * slope)
        ).astype(BF16)

    for k in range(n):

        @pl.when(jnp.logical_and(i >= cuts[k], i < cuts[k + 1]))
        def _():
            one(mine[k][...] + got[k][...])


def finish(name, after, wide, mine, got, row, rows=128):
    length, width = wide[0].shape
    cuts, pieces = cut_specs([x.shape[0] for x in mine], rows, width)
    here = pl.BlockSpec((rows, width), lambda i: (i, 0))
    return launch(
        functools.partial(finish_kernel, cuts=cuts, last=len(wide) > 1),
        name,
        (length // rows,),
        (),
        after,
        [(x, here) for x in wide]
        + list(zip(mine, pieces))
        + list(zip(got, pieces))
        + [(row, whole(1, width))],
        [((length, width), BF16, here)],
    )[0]


def halve_kernel(place, a, b, c, d, keep, send):
    keep[...] = a[...] + b[...]
    send[...] = c[...] + d[...]


def halve(place, slot, after, mine, got):
    n, width = mine.shape
    h = n // 2
    rows = h // 2 if h * width > (256 << 10) else h
    steps = h // rows

    def bit(place):
        return 0 if slot is None else place[slot]

    keep = pl.BlockSpec((rows, width), lambda i, place: (bit(place) * steps + i, 0))
    send = pl.BlockSpec((rows, width), lambda i, place: ((1 - bit(place)) * steps + i, 0))
    here = pl.BlockSpec((rows, width), lambda i, _: (i, 0))
    return launch(
        halve_kernel,
        "halve",
        (steps,),
        (place,),
        after,
        [(mine, keep), (got, keep), (mine, send), (got, send)],
        [((h, width), F32, here)] * 2,
    )


def pack_kernel(a, b, c, d, out):
    n = a.shape[0]
    out[:n, :] = a[...] + b[...]
    out[n:, :] = c[...] + d[...]


def pack(after, a, b, c, d):
    shape = (a.shape[0] + c.shape[0], a.shape[1])
    return launch(
        pack_kernel,
        "pack",
        (1,),
        (),
        after,
        [(x, whole(*x.shape)) for x in (a, b, c, d)],
        [(shape, F32, whole(*shape))],
    )[0]


def plus_kernel(a, b, out):
    out[...] = a[...] + b[...]


def plus(after, a, b):
    return launch(
        plus_kernel,
        "plus",
        (1,),
        (),
        after,
        [(x, whole(*x.shape)) for x in (a, b)],
        [(a.shape, F32, whole(*a.shape))],
    )[0]


def part_kernel(a, b, first, second):
    n = first.shape[0]
    first[...] = a[:n, :] + b[:n, :]
    second[...] = a[n:, :] + b[n:, :]


def part(after, n, a, b):
    shapes = [(n, a.shape[1]), (a.shape[0] - n, a.shape[1])]
    return launch(
        part_kernel,
        "part",
        (1,),
        (),
        after,
        [(x, whole(*x.shape)) for x in (a, b)],
        [(shape, F32, whole(*shape)) for shape in shapes],
    )


def join_kernel(place, *refs, slots):
    parts, out, sems = refs[:-2], refs[-2], refs[-1]
    copies = []
    start = 0
    for i, slot in enumerate(slots):
        mine, got = parts[2 * i : 2 * i + 2]
        h = mine.shape[0]
        bit = 0 if slot is None else place[slot]
        copies += [
            pltpu.make_async_copy(mine, out.at[pl.ds(start + bit * h, h)], sems.at[2 * i]),
            pltpu.make_async_copy(got, out.at[pl.ds(start + (1 - bit) * h, h)], sems.at[2 * i + 1]),
        ]
        start += 2 * h
    for copy in copies:
        copy.start()
    for copy in copies:
        copy.wait()


def join(place, after, *parts):
    width = parts[0][0].shape[1]
    rows = sum(2 * mine.shape[0] for mine, _, _ in parts)
    anywhere = pl.BlockSpec(memory_space=pltpu.HBM)
    return launch(
        functools.partial(join_kernel, slots=[slot for _, _, slot in parts]),
        "join",
        (1,),
        (place,),
        after,
        [(x, anywhere) for mine, got, _ in parts for x in (mine, got)],
        [((rows, width), F32, once(rows, width))],
        [pltpu.SemaphoreType.DMA((2 * len(parts),))],
    )[0]


def assemble_kernel(place, *refs):
    arrays, (qkv, merge, small) = refs[:8], refs[8:]
    count = qkv.shape[1]
    j, t = pl.program_id(0), pl.program_id(1)
    core = place[0]
    for other in range(2):
        for p in range(2):
            bit = place[bit_slot(p, 0)] if other == 0 else place[NEAR + p]
            for half in range(2):
                x = arrays[4 * other + 2 * p + half]
                mine = (j == 2 * (core if other == 0 else 1 - core) + p) & (
                    t == (bit if half == 0 else 1 - bit)
                )

                @pl.when(mine & (j < 3))
                def _():
                    qkv[0] = x[:count, :]

                @pl.when(mine & (j == 3))
                def _():
                    merge[...] = x[:count, :]

    @pl.when((j == 3) & (t == 1))
    def _():
        rows = slice(count, count + small.shape[0])
        one = jnp.where(place[bit_slot(1, 0)] == 0, arrays[2][rows, :], arrays[3][rows, :])
        two = jnp.where(place[NEAR + 1] == 0, arrays[6][rows, :], arrays[7][rows, :])
        small[...] = one + two


def assemble(place, after, arrays, width):
    local = arrays[0].shape[1]
    half = width // 2
    return launch(
        assemble_kernel,
        "assemble",
        (4, 2),
        (place,),
        after,
        [(x, once(*x.shape)) for x in arrays],
        [
            (
                (3, width, local),
                F32,
                pl.BlockSpec(
                    (1, half, local),
                    lambda j, t, _: (jnp.minimum(j, 2), jnp.where(j < 3, t, 1), 0),
                ),
            ),
            (
                (local, width),
                F32,
                pl.BlockSpec((local, half), lambda j, t, _: (0, jnp.where(j < 3, 0, t))),
            ),
            ((16, local), F32, whole(16, local)),
        ],
        vmem=40,
    )


def spread_kernel(low, high, up, down):
    piece, width = low.shape[1] // 2, low.shape[2]
    down[0] = low[0, :piece, :]
    down[1] = high[0, :piece, :]
    up[:, :width] = low[0, piece:, :]
    up[:, width:] = high[0, piece:, :]


def spread(after, gathered):
    count, rows, width = gathered.shape
    piece = rows // 2
    half = count // 2
    return launch(
        spread_kernel,
        "spread",
        (half,),
        (),
        after,
        [
            (gathered, pl.BlockSpec((1, rows, width), lambda n: (n, 0, 0))),
            (gathered, pl.BlockSpec((1, rows, width), lambda n: (half + n, 0, 0))),
        ],
        [
            ((half * piece, 2 * width), F32, pl.BlockSpec((piece, 2 * width), lambda n: (n, 0))),
            (
                (2, half * piece, width),
                F32,
                pl.BlockSpec((2, piece, width), lambda n: (0, n, 0)),
            ),
        ],
        vmem=60,
    )


AXES = ("xlo", "z", "y", "core", "tensor")
RINGS = ("z", "y", "core")
DIRECTIONS = (("y", 0), ("z", 0), ("y", 1), ("z", 1))
SWAP = ((0, 1), (1, 0))


def partner(place, bit):
    return place ^ 1 if bit == 0 else 3 - place


def bit_at(place, bit):
    return int(place in (1, 2)) if bit == 0 else int(place >= 2)


def order_of(core, part):
    return [(core + 2 * part + step) % 4 for step in range(4)]


def spot_of(z, y, core, part):
    spot = 0
    for direction in order_of(core, part):
        axis, bit = DIRECTIONS[direction]
        spot = 2 * spot + bit_at(y if axis == "y" else z, bit)
    return spot


def step_pairs(part, step):
    pairs = []
    for z in range(4):
        for y in range(4):
            for core in range(2):
                axis, bit = DIRECTIONS[order_of(core, part)[step]]
                z2, y2 = (z, partner(y, bit)) if axis == "y" else (partner(z, bit), y)
                pairs.append(((z * 4 + y) * 2 + core, (z2 * 4 + y2) * 2 + core))
    return pairs


def place_table():
    rows = []
    for z in range(4):
        for y in range(4):
            for core in range(2):
                row = [core]
                for part in range(2):
                    for direction in order_of(core, part):
                        axis, bit = DIRECTIONS[direction]
                        row.append(bit_at(y if axis == "y" else z, bit))
                for half in (core, 1 - core):
                    row.append(half)
                    for part in range(2):
                        here = spot_of(z, y, half, part)
                        row += [
                            here ^ spot_of(z2, y2, half, part) for z2 in range(4) for y2 in range(4)
                        ]
                for part in range(2):
                    axis, bit = DIRECTIONS[order_of(1 - core, part)[0]]
                    row.append(bit_at(y if axis == "y" else z, bit))
                rows.append(row)
    return np.array(rows, np.int32)


OWN = 9
OTHER = OWN + 33
NEAR = OTHER + 33


def bit_slot(part, step):
    return 1 + 4 * part + step


def send_step(x, part, step):
    return lax.ppermute(x, RINGS, step_pairs(part, step))


def exchange(x, axis):
    return lax.ppermute(x, axis, SWAP)


def body(
    tokens,
    norm_gain,
    norm_shift,
    qkv_weight,
    merge_weight,
    up_weight,
    inner_shift,
    down_weight,
    outer_shift,
    cotangent,
):
    length, width = tokens.shape
    local = merge_weight.shape[0]
    hidden = up_weight.shape[1]
    place = lax.dynamic_index_in_dim(
        jnp.asarray(place_table()), lax.axis_index(RINGS), 0, keepdims=False
    )
    cos, sin = rotary_tables(length)
    w3 = qkv_weight.transpose(1, 0, 2)
    gain, shift, inner_row = norm_gain[None], norm_shift[None], inner_shift[None]

    normed, normed_t, q, k, v, dh, outer_g = project(
        tokens, gain, shift, w3, merge_weight, cotangent, cos, sin
    )
    out_f, dn_f, active, d_pre, inner_g = hidden_pass(
        (outer_g,), normed, cotangent, up_weight, inner_row, down_weight
    )

    (down_s,) = down_grad(place, OTHER, (inner_g,), active, cotangent)
    down_got = exchange(down_s, "core")
    (up_s,) = up_grad(place, OTHER, (down_s,), normed_t, d_pre)
    up_got = exchange(up_s, "core")

    ho0, dq0, dk_part, dv_part = attend(0, (up_s,), q, k, v, dh, cos, sin)
    mine = list(forward_part(0, (dq0,), ho0, merge_weight, out_f, (512,)))
    theirs = [exchange(mine[0], "tensor")]

    def flat(x):
        return x.reshape(-1, x.shape[-1])

    down_k, down_s = map(flat, down_grad(place, OWN, (mine[0],), active, cotangent, down_got))
    down_got = send_step(down_s, 0, 0)
    up_k, up_s = map(flat, up_grad(place, OWN, (down_s,), normed_t, d_pre, up_got))
    up_got = send_step(up_s, 1, 0)

    ho1, dq1, dk, dv = attend(1, (up_s,), q, k, v, dh, cos, sin, (dk_part, dv_part))
    mine += forward_part(1, (dq1,), ho1, merge_weight, out_f, (128, 384))
    theirs += [exchange(x, "tensor") for x in mine[1:]]

    late = (normed_t, ho0, ho1, cotangent, dq0, dq1, dk, dv)
    bits = (bit_slot(0, 0), bit_slot(1, 0))

    down_k, down_s = halve(place, None, (mine[1],), down_k, down_got)
    down_got = send_step(down_s, 0, 1)
    tail_s = tail(place, OTHER, bits, (down_s,), *late)
    tail_got = [exchange(x, "core") for x in tail_s]
    up_k, up_s = halve(place, None, (tail_s[0], theirs[0]), up_k, up_got)
    up_got = send_step(up_s, 1, 1)
    back = backward_pass((up_s,), dq0, dq1, dk, dv, w3, dn_f, tokens, (256, 512, 256))
    back, sums = back[:-1], back[-1]

    down_k, down_s = halve(place, None, (sums, theirs[1]), down_k, down_got)
    down_got = send_step(down_s, 0, 2)
    up_k, up_s = halve(place, None, (down_s,), up_k, up_got)
    up_got = send_step(up_s, 1, 2)

    small = jnp.concatenate(
        [
            sums.reshape(4, local),
            outer_g.reshape(2, local),
            inner_g.reshape(hidden // local, local),
            jnp.zeros((16 - 6 - hidden // local, local), F32),
        ],
        axis=0,
    )
    tail_k0, tail_s0, tail_k1, tail_s1 = tail(
        place, OWN, bits, (up_s,), *late, small, tail_got
    )
    tail_got0 = send_step(tail_s0, 0, 0)
    tail_got1 = send_step(tail_s1, 1, 0)

    down_k, down_s = halve(place, None, (tail_s1,), down_k, down_got)
    down_got = send_step(down_s, 0, 3)
    up_k, up_s = halve(place, None, (down_s,), up_k, up_got)
    up_got = send_step(up_s, 1, 3)

    feed_x = pack((up_s, theirs[2]), down_k, down_got, up_k, up_got)
    feed_got = exchange(feed_x, "xlo")

    tail_k0, tail_s0 = halve(place, bit_slot(0, 1), (feed_x,), tail_k0, tail_got0)
    tail_got0 = send_step(tail_s0, 0, 1)
    tail_k1, tail_s1 = halve(place, bit_slot(1, 1), (tail_s0,), tail_k1, tail_got1)
    tail_got1 = send_step(tail_s1, 1, 1)

    tail_k0, tail_s0 = halve(place, bit_slot(0, 2), (tail_s1,), tail_k0, tail_got0)
    tail_got0 = send_step(tail_s0, 0, 2)
    tail_k1, tail_s1 = halve(place, bit_slot(1, 2), (tail_s0,), tail_k1, tail_got1)
    tail_got1 = send_step(tail_s1, 1, 2)

    feed_x = plus((tail_s1,), feed_x, feed_got)
    gathered = lax.all_gather(feed_x, ("core", "z", "y"))

    (back0,) = hand((feed_x,), back[0])
    back_got0 = exchange(back0, "tensor")

    tail_k0, tail_s0 = halve(place, bit_slot(0, 3), (back0,), tail_k0, tail_got0)
    tail_got0 = send_step(tail_s0, 0, 3)
    tail_k1, tail_s1 = halve(place, bit_slot(1, 3), (tail_s0,), tail_k1, tail_got1)
    tail_got1 = send_step(tail_s1, 1, 3)

    tail_x = pack((tail_s1, back_got0), tail_k0, tail_got0, tail_k1, tail_got1)
    tail_got = exchange(tail_x, "xlo")

    tail0, tail1 = part((tail_x,), tail_k0.shape[0], tail_x, tail_got)
    tail_got0 = send_step(tail0, 0, 3)
    tail_got1 = send_step(tail1, 1, 3)

    back_late = hand((tail1,), *back[1:])
    back_got_late = [exchange(x, "tensor") for x in back_late]

    block_out = finish(
        "finish_out", (back_late[0],), (tokens,), mine, theirs, outer_shift[None]
    )

    for step in (3, 2, 1):
        tail0 = join(place, (block_out, tail1), (tail0, tail_got0, bit_slot(0, step)))
        tail_got0 = send_step(tail0, 0, step - 1)
        tail1 = join(place, (tail0,), (tail1, tail_got1, bit_slot(1, step)))
        tail_got1 = send_step(tail1, 1, step - 1)

    up_out, down_out = spread((tail1, back_got_late[0]), gathered)
    down_out = down_out.reshape(hidden, width)

    own = (tail0, tail_got0, tail1, tail_got1)
    near = [exchange(x, "core") for x in own]
    qkv_out, merge_out, small = assemble(place, (up_out,), (*own, *near), width)
    pair = small[:4].reshape(2, width)
    pair = pair + exchange(pair, "tensor")

    token_grad = finish(
        "finish_grad",
        (merge_out,),
        (tokens, cotangent),
        (back0, *back_late),
        (back_got0, *back_got_late),
        gain,
    )
    return (
        block_out,
        token_grad,
        pair[0],
        pair[1],
        qkv_out.transpose(1, 0, 2),
        merge_out,
        up_out,
        small[6 : 6 + hidden // local].reshape(hidden),
        down_out,
        small[4:6].reshape(width),
    )


def solution(mesh):
    dp = AXES[:4]
    finer = Mesh(mesh.devices.reshape(2, 4, 4, 2, 2), AXES)
    return jax.shard_map(
        body,
        mesh=finer,
        in_specs=(
            P(dp, None),
            P(),
            P(),
            P(None, None, "tensor"),
            P("tensor", None),
            P(None, "tensor"),
            P("tensor"),
            P("tensor", None),
            P(),
            P(dp, None),
        ),
        out_specs=(
            P(dp, None),
            P(dp, None),
            P(),
            P(),
            P(None, None, "tensor"),
            P("tensor", None),
            P(None, "tensor"),
            P("tensor"),
            P("tensor", None),
            P(),
        ),
        check_vma=False,
    )
```

```python
import functools

import jax
import jax.numpy as jnp
import numpy as np
from jax import lax
from jax.experimental import pallas as pl
from jax.experimental.pallas import tpu as pltpu
from jax.sharding import Mesh
from jax.sharding import PartitionSpec as P

F32 = jnp.float32
BF16 = jnp.bfloat16
HEAD = 64
ROT = 32
PAIR = 2 * HEAD
epsilon = 1e-05


def nn(a, b):
    return jnp.dot(a, b, preferred_element_type=F32)


def nt(a, b):
    return lax.dot_general(a, b, (((1,), (1,)), ((), ())), preferred_element_type=F32)


def tn(a, b):
    return lax.dot_general(a, b, (((0,), (0,)), ((), ())), preferred_element_type=F32)


def rotary_tables(length):
    half = ROT // 2
    rates = np.float32(10000.0) ** (-np.arange(half, dtype=np.float32) / np.float32(half))
    angles = np.arange(length, dtype=np.float32)[:, None] * rates[None, :].astype(np.float32)
    angles = np.repeat(angles, 2, axis=1)
    sign = np.where(np.arange(ROT) % 2 == 0, -1.0, 1.0)
    rest = np.ones((length, HEAD - ROT))
    cosine = np.concatenate([np.cos(angles), rest], axis=1)
    sine = np.concatenate([np.sin(angles) * sign, 0 * rest], axis=1)
    return tuple(jnp.asarray(np.tile(x, (1, 2)).astype(np.float32)) for x in (cosine, sine))


def swap_pairs(x):
    lane = lax.broadcasted_iota(jnp.int32, x.shape, 1)
    return jnp.where(lane % 2 == 0, pltpu.roll(x, PAIR - 1, 1), pltpu.roll(x, 1, 1))


def launch(kernel, name, grid, scalars, after, ins, outs, scratch=(), vmem=16, flops=0, into=None):
    if into is not None:
        after = (*after, into)
    first, skipped = len(scalars), len(after)

    def without(*refs):
        kernel(*refs[:first], *refs[first + skipped :])

    got = pl.pallas_call(
        without,
        grid_spec=pltpu.PrefetchScalarGridSpec(
            num_scalar_prefetch=first,
            grid=grid,
            in_specs=[pl.BlockSpec(memory_space=pltpu.HBM)] * skipped + [spec for _, spec in ins],
            out_specs=[spec for _, _, spec in outs],
            scratch_shapes=list(scratch),
        ),
        out_shape=[jax.ShapeDtypeStruct(shape, dtype) for shape, dtype, _ in outs],
        compiler_params=pltpu.CompilerParams(vmem_limit_bytes=vmem << 20),
        input_output_aliases={} if into is None else {first + skipped - 1: 0},
        cost_estimate=pl.CostEstimate(
            flops=flops,
            bytes_accessed=sum(x.size * x.dtype.itemsize for x, _ in ins)
            + sum(int(np.prod(shape)) * jnp.dtype(dtype).itemsize for shape, dtype, _ in outs),
            transcendentals=0,
        ),
        name=name,
    )(*scalars, *after, *[array for array, _ in ins])
    return got


def whole(*shape):
    return pl.BlockSpec(shape, lambda *_: (0,) * len(shape))


def once(*shape):
    return pl.BlockSpec(shape, lambda *_: (0,) * len(shape), pipeline_mode=pl.Buffered(1))


gelu_rate = float(np.sqrt(2 / np.pi))
ROOM = 64


def norm_rows(x):
    centred = x - jnp.mean(x, axis=1, keepdims=True)
    inverse = lax.rsqrt(jnp.mean(centred * centred, axis=1, keepdims=True) + epsilon)
    return centred * inverse, inverse


def project_kernel(
    tok, gain, shift, w_in, mw_in, cot, cos, sin, normed, normed_t, q, k, v, dh, outer, w, mw, sems
):
    first = pl.program_id(0) == 0
    copies = [pltpu.make_async_copy(mw_in, mw, sems.at[0])] + [
        pltpu.make_async_copy(w_in.at[which], w.at[which], sems.at[1 + which]) for which in range(3)
    ]

    @pl.when(first)
    def _():
        for copy in copies:
            copy.start()

    def body(arriving):
        unit, _ = norm_rows(tok[...].astype(F32))
        n = (unit * gain[...] + shift[...]).astype(BF16)
        normed[...] = n
        normed_t[...] = n.T
        total = jnp.sum(cot[...].astype(F32), axis=0, keepdims=True)
        outer[...] = total if arriving else outer[...] + total
        if arriving:
            copies[0].wait()
        dh[...] = nt(cot[...], mw[...]).astype(BF16)
        c = cos[...]
        s = sin[...]
        for which, ref in enumerate((q, k, v)):
            if arriving:
                copies[1 + which].wait()
            joined = nn(n, w[which])
            if which == 2:
                ref[...] = joined.astype(BF16)
                continue
            for p in range(joined.shape[1] // PAIR):
                block = joined[:, p * PAIR : (p + 1) * PAIR]
                turned = (block * c + swap_pairs(block) * s).astype(BF16)
                if which == 0:
                    turned = turned * jnp.asarray(HEAD**-0.5, BF16)
                ref[:, p * PAIR : (p + 1) * PAIR] = turned

    @pl.when(first)
    def _():
        body(True)

    @pl.when(jnp.logical_not(first))
    def _():
        body(False)


def project(tok, gain, shift, w3, mw, cot, cos, sin, rows=256):
    length, width = tok.shape
    local = mw.shape[0]

    def row_block(n):
        return pl.BlockSpec((rows, n), lambda i: (i, 0))

    def out(n):
        return ((length, n), BF16, row_block(n))

    return launch(
        project_kernel,
        "project",
        (length // rows,),
        (),
        (),
        [
            (tok, row_block(width)),
            (gain, whole(1, width)),
            (shift, whole(1, width)),
            (w3, pl.BlockSpec(memory_space=pltpu.HBM)),
            (mw, pl.BlockSpec(memory_space=pltpu.HBM)),
            (cot, row_block(width)),
            (cos, row_block(PAIR)),
            (sin, row_block(PAIR)),
        ],
        [out(width), ((width, length), BF16, pl.BlockSpec((width, rows), lambda i: (0, i)))]
        + [out(local)] * 4
        + [((1, width), F32, whole(1, width))],
        [
            pltpu.VMEM((3, width, local), BF16),
            pltpu.VMEM((local, width), BF16),
            pltpu.SemaphoreType.DMA((4,)),
        ],
        vmem=60,
        flops=8 * length * width * local,
    )


def hidden_kernel(normed, cot, up_in, shift, down_in, out, dn, act, dpre, ig, up, down, sems, *, cols):
    first = pl.program_id(0) == 0
    cuts = [slice(j, j + cols) for j in range(0, up.shape[1], cols)]
    copies = []
    for j, s in enumerate(cuts):
        copies.append(
            (
                pltpu.make_async_copy(up_in.at[:, s], up.at[:, s], sems.at[2 * j]),
                pltpu.make_async_copy(down_in.at[s, :], down.at[s, :], sems.at[2 * j + 1]),
            )
        )

    @pl.when(first)
    def _():
        for pair in copies:
            for copy in pair:
                copy.start()

    def body(arriving):
        n = normed[...]
        c = cot[...]
        sums = []
        for j, s in enumerate(cuts):
            if arriving:
                for copy in copies[j]:
                    copy.wait()
            v = nn(n, up[:, s]) + shift[:, s]
            da = nt(c, down[s, :])
            square = v * v
            t = jnp.tanh(gelu_rate * v * (1.0 + 0.044715 * square))
            h = 0.5 * (1.0 + t)
            act[:, s] = (v * h).astype(BF16)
            slope = h + (0.5 * gelu_rate) * v * (1.0 - t * t) * (1.0 + (3 * 0.044715) * square)
            d_pre = (da * slope).astype(BF16)
            dpre[:, s] = d_pre
            sums.append(jnp.sum(d_pre.astype(F32), axis=0, keepdims=True))
        sums = jnp.concatenate(sums, axis=1)
        ig[...] = sums if arriving else ig[...] + sums
        out[...] = nn(act[...], down[...])
        dn[...] = nt(dpre[...], up[...])

    @pl.when(first)
    def _():
        body(True)

    @pl.when(jnp.logical_not(first))
    def _():
        body(False)


def hidden_pass(after, normed, cot, up, shift, down, rows=256, cols=512):
    length, width = normed.shape
    hidden = up.shape[1]

    def here(n):
        return pl.BlockSpec((rows, n), lambda i: (i, 0))

    return launch(
        functools.partial(hidden_kernel, cols=cols),
        "hidden",
        (length // rows,),
        (),
        after,
        [
            (normed, here(width)),
            (cot, here(width)),
            (up, pl.BlockSpec(memory_space=pltpu.HBM)),
            (shift, whole(1, hidden)),
            (down, pl.BlockSpec(memory_space=pltpu.HBM)),
        ],
        [((length, width), F32, here(width))] * 2
        + [((length, hidden), BF16, here(hidden))] * 2
        + [((1, hidden), F32, whole(1, hidden))],
        [
            pltpu.VMEM((width, hidden), BF16),
            pltpu.VMEM((hidden, width), BF16),
            pltpu.SemaphoreType.DMA((2 * hidden // cols,)),
        ],
        vmem=60,
        flops=9 * length * width * hidden,
    )


def grad_kernel(place, lhs, rhs, *rest, base, product, own):
    if own:
        got, keep, send, buf, sems, land, land_sems = rest
    else:
        out, buf, sems = rest
    j = pl.program_id(0)
    size = buf.shape[1] // 8

    def arriving(n):
        return pltpu.make_async_copy(
            got.at[place[base + n]], land.at[pl.ds(n * size, size)], land_sems.at[n]
        )

    if own:

        @pl.when(j == 0)
        def _():
            for n in range(16):
                arriving(n).start()

    buf[j] = product(lhs[...], rhs[...])
    if own:

        @pl.when(j == 0)
        def _():
            for n in range(8):
                arriving(n).wait()

        @pl.when(j == 1)
        def _():
            for n in range(8, 16):
                arriving(n).wait()

        buf[j] += land[pl.ds(pl.multiple_of(j * 8 * size, size), 8 * size), :]

    for i in range(8):
        spot = place[base + j * 8 + i]
        block = buf.at[j, pl.ds(i * size, size)]
        sem = sems.at[j * 8 + i]
        if own:

            @pl.when(spot < 8)
            def _():
                pltpu.make_async_copy(block, keep.at[spot], sem).start()

            @pl.when(spot >= 8)
            def _():
                pltpu.make_async_copy(block, send.at[spot - 8], sem).start()

        else:
            pltpu.make_async_copy(block, out.at[spot], sem).start()

    @pl.when(j == 1)
    def _():
        for n in range(16):
            block = buf.at[n // 8, pl.ds((n % 8) * size, size)]
            pltpu.make_async_copy(block, (keep if own else out).at[0], sems.at[n]).wait()


def grad(place, base, spots, after, lhs, rhs, specs, product, got=None):
    width = 1024
    rows = 1024
    own = got is not None
    piece = rows // 16
    anywhere = pl.BlockSpec(memory_space=pltpu.HBM)
    scratch = [pltpu.VMEM((2, rows // 2, width), F32), pltpu.SemaphoreType.DMA((16,))]
    if own:
        scratch += [pltpu.VMEM((rows, width), F32), pltpu.SemaphoreType.DMA((16,))]
    outs = [((8 if own else 16, piece, width), F32, anywhere)] * (2 if own else 1)
    return launch(
        functools.partial(grad_kernel, base=spots, product=product, own=own),
        "grad",
        (2,),
        (place,),
        after,
        [(lhs, specs[0]), (rhs, specs[1])] + ([(got, anywhere)] if own else []),
        outs,
        scratch,
        vmem=24,
        flops=2 * rows * width * lhs.shape[0],
    )


def down_grad(place, base, after, active, cot, got=None):
    length, width = cot.shape
    block = pl.BlockSpec((length, 512), lambda j, place: (0, place[base] * 2 + j))
    return grad(
        place, base, base + 1, after, active, cot, (block, once(length, width)), tn, got
    )


def up_grad(place, base, after, normed_t, d_pre, got=None):
    width, length = normed_t.shape
    rows = pl.BlockSpec((512, length), lambda j, _: (j, 0))
    half = pl.BlockSpec(
        (length, 1024), lambda j, place: (0, place[base]), pipeline_mode=pl.Buffered(1)
    )
    return grad(place, base, base + 17, after, normed_t, d_pre, (rows, half), nn, got)


def attend_kernel(*refs, last, sub):
    if last:
        q, do, k, v, dk_in, dv_in, cos, sin, ho, dq, dk, dv, dk_sum, dv_sum = refs
    else:
        q, do, k, v, cos, sin, ho, dq, dk_sum, dv_sum = refs
    block = q.shape[0]
    seen = k.shape[0]
    low = lax.broadcasted_iota(jnp.int32, (sub, PAIR), 1) < HEAD
    zero = jnp.zeros((sub, PAIR), BF16)
    causal = lax.broadcasted_iota(jnp.int32, (sub, sub), 1) <= lax.broadcasted_iota(
        jnp.int32, (sub, sub), 0
    )
    for i in range(block // sub):
        before = seen - block + i * sub
        upto = before + sub
        rows = slice(i * sub, (i + 1) * sub)
        keys = k[0:upto, :]
        values = v[0:upto, :]
        heads = [
            [jnp.where(low, x[rows, :], zero), jnp.where(low, zero, x[rows, :])] for x in (q, do)
        ]
        scores = [nt(x, keys) for x in heads[0]]
        d_probs = [nt(x, values) for x in heads[1]]
        probs_low, d_scores = [], []
        for h in range(2):
            edge = jnp.where(causal, scores[h][:, before:], -1e30)
            if before:
                edge = jnp.concatenate([scores[h][:, :before], edge], axis=1)
            expo = jnp.exp(edge - jnp.max(edge, axis=1, keepdims=True))
            probs = expo * (1.0 / jnp.sum(expo, axis=1, keepdims=True))
            inner = jnp.sum(probs * d_probs[h], axis=1, keepdims=True)
            probs_low.append(probs.astype(BF16))
            d_scores.append((probs * (d_probs[h] - inner)).astype(BF16))
        mixed = [nn(x, values) for x in probs_low]
        ho[rows, :] = jnp.where(low, mixed[0], mixed[1]).astype(BF16)
        d_query = [nn(x, keys) for x in d_scores]
        d_query = jnp.where(low, d_query[0], d_query[1]) * HEAD**-0.5
        turn = slice(before, upto)
        dq[rows, :] = (
            d_query * cos[turn, :] - swap_pairs(d_query) * sin[turn, :]
        ).astype(BF16)
        for left, right, total in ((probs_low, heads[1], dv_sum), (d_scores, heads[0], dk_sum)):
            add = tn(left[0], right[0]) + tn(left[1], right[1])
            if i == 0:
                total[0:upto, :] = add
            else:
                total[0:before, :] += add[:before]
                total[before:upto, :] = add[before:]
    if last:
        before = seen - block
        dk_sum[0:before, :] += dk_in[...]
        dv_sum[0:before, :] += dv_in[...]
        for i in range(seen // block):
            rows = slice(i * block, (i + 1) * block)
            d_keys = dk_sum[rows, :]
            dk[rows, :] = (d_keys * cos[rows, :] - swap_pairs(d_keys) * sin[rows, :]).astype(BF16)
            dv[rows, :] = dv_sum[rows, :].astype(BF16)


def attend(part, after, q, k, v, do, cos, sin, carried=(), sub=256):
    length, local = q.shape
    half = length // 2
    seen = half * (part + 1)
    rows = pl.BlockSpec((half, PAIR), lambda p: (part, p))
    keys = pl.BlockSpec((seen, PAIR), lambda p: (0, p))
    table = pl.BlockSpec((seen, PAIR), lambda p: (0, 0))
    here = pl.BlockSpec((half, PAIR), lambda p: (0, p))
    outs = [((half, local), BF16, here)] * 2
    scratch = ()
    if part == 0:
        outs += [((half, local), F32, here)] * 2
    else:
        outs += [((length, local), BF16, keys)] * 2
        scratch = [pltpu.VMEM((length, PAIR), F32)] * 2
    return launch(
        functools.partial(attend_kernel, last=part == 1, sub=sub),
        "attend",
        (local // PAIR,),
        (),
        after,
        [(q, rows), (do, rows), (k, keys), (v, keys)]
        + [(x, here) for x in carried]
        + [(cos, table), (sin, table)],
        outs,
        scratch,
        flops=30 * half * seen * PAIR * local // PAIR,
    )


def forward_kernel(ho, mw, a, *pieces, cuts):
    i = pl.program_id(0)
    total = nn(ho[...], mw[...]) + a[...]
    for n, piece in enumerate(pieces):

        @pl.when(jnp.logical_and(i >= cuts[n], i < cuts[n + 1]))
        def _():
            piece[...] = total


def within(first, last):
    return lambda i, *_: (jnp.clip(i, first, last - 1) - first, 0)


def cut_specs(sizes, rows, width):
    cuts = [int(n) // rows for n in np.cumsum((0,) + tuple(sizes))]
    return cuts, [
        pl.BlockSpec((rows, width), within(cuts[k], cuts[k + 1])) for k in range(len(sizes))
    ]


def forward_part(part, after, ho, mw, a, sizes, rows=128):
    half, local = ho.shape
    width = mw.shape[1]
    steps = half // rows
    cuts, specs = cut_specs(sizes, rows, width)
    there = pl.BlockSpec((rows, width), lambda i: (part * steps + i, 0))
    return launch(
        functools.partial(forward_kernel, cuts=cuts),
        "forward",
        (steps,),
        (),
        after,
        [
            (ho, pl.BlockSpec((rows, local), lambda i: (i, 0))),
            (mw, once(local, width)),
            (a, there),
        ],
        [((n, width), F32, spec) for n, spec in zip(sizes, specs)],
        flops=2 * half * width * local,
    )


def backward_kernel(dq0, dq1, dk, dv, w, a, tok, out, sums):
    i = pl.program_id(0)

    def one(dq):
        total = nt(dq[...], w[0]) + nt(dk[...], w[1]) + nt(dv[...], w[2]) + a[...]
        out[...] = total
        unit, _ = norm_rows(tok[...].astype(F32))
        both = jnp.concatenate(
            [jnp.sum(total * unit, axis=0, keepdims=True), jnp.sum(total, axis=0, keepdims=True)],
            axis=0,
        )

        @pl.when(i == 0)
        def _():
            sums[...] = both

        @pl.when(i > 0)
        def _():
            sums[...] += both

    half = pl.num_programs(0) // 2

    @pl.when(i < half)
    def _():
        one(dq0)

    @pl.when(i >= half)
    def _():
        one(dq1)


def backward_pass(after, dq0, dq1, dk, dv, w3, a, tok, rows=256):
    length, local = dk.shape
    width = w3.shape[1]
    steps = length // rows
    here = pl.BlockSpec((rows, width), lambda i: (i, 0))
    narrow = pl.BlockSpec((rows, local), lambda i: (i, 0))
    return launch(
        backward_kernel,
        "backward",
        (steps,),
        (),
        after,
        [
            (dq0, pl.BlockSpec((rows, local), within(0, steps // 2))),
            (dq1, pl.BlockSpec((rows, local), within(steps // 2, steps))),
            (dk, narrow),
            (dv, narrow),
            (w3, once(3, width, local)),
            (a, here),
            (tok, here),
        ],
        [((length, width), F32, here), ((2, width), F32, whole(2, width))],
        vmem=60,
        flops=6 * length * width * local,
    )


def hand_kernel(x, *pieces, cuts):
    i = pl.program_id(0)
    for n, piece in enumerate(pieces):

        @pl.when(jnp.logical_and(i >= cuts[n], i < cuts[n + 1]))
        def _():
            piece[...] = x[...]


def hand(after, x, start, sizes, rows=128):
    width = x.shape[1]
    first = start // rows
    cuts, specs = cut_specs(sizes, rows, width)
    return launch(
        functools.partial(hand_kernel, cuts=cuts),
        "hand",
        (cuts[-1],),
        (),
        after,
        [(x, pl.BlockSpec((rows, width), lambda i: (first + i, 0)))],
        [((size, width), F32, spec) for size, spec in zip(sizes, specs)],
    )


def hand_all_kernel(*refs):
    half = len(refs) // 2
    for x, out in zip(refs[:half], refs[half:]):
        out[...] = x[...]


def hand_all(after, *arrays):
    return launch(
        hand_all_kernel,
        "hand_all",
        (1,),
        (),
        after,
        [(x, once(*x.shape)) for x in arrays],
        [(x.shape, F32, once(*x.shape)) for x in arrays],
    )


def tail_kernel(place, normed_t, ho0, ho1, cot, dq0, dq1, dk, dv, own0, own1, other0, other1):
    n = normed_t[...]
    width = n.shape[0]
    half = dq0.shape[0]
    first = place[0] == 0

    def put(mine, x, roomy):
        def store(ref):
            if not roomy:
                ref[...] = x
                return
            rows = width // 2
            blank = jnp.zeros((ROOM, x.shape[1]), F32)
            for k in range(2):
                start = k * (rows + ROOM)
                ref[start : start + rows, :] = x[k * rows : (k + 1) * rows]
                ref[start + rows : start + rows + ROOM, :] = blank

        @pl.when(mine)
        def _():
            store(own1 if roomy else own0)

        @pl.when(jnp.logical_not(mine))
        def _():
            store(other1 if roomy else other0)

    put(first, nn(n[:, :half], dq0[...]) + nn(n[:, half:], dq1[...]), False)
    put(first, nn(n, dk[...]), True)
    put(jnp.logical_not(first), nn(n, dv[...]), False)
    g = tn(ho0[...], cot[:half, :]) + tn(ho1[...], cot[half:, :])
    columns = g.shape[1] // 2
    put(jnp.logical_not(first), jnp.concatenate([g[:, :columns], g[:, columns:]], axis=0), True)


def tail(place, after, normed_t, ho0, ho1, cot, dq0, dq1, dk, dv):
    width, length = normed_t.shape
    local = dk.shape[1]
    half = length // 2
    assert 2 * local == width
    shapes = [(width, local), (width + 2 * ROOM, local)] * 2
    return launch(
        tail_kernel,
        "tail",
        (1,),
        (place,),
        after,
        [(normed_t, once(width, length))]
        + [(x, once(half, local)) for x in (ho0, ho1)]
        + [(cot, once(length, width))]
        + [(x, once(half, local)) for x in (dq0, dq1)]
        + [(x, once(length, local)) for x in (dk, dv)],
        [(shape, F32, once(*shape)) for shape in shapes],
        vmem=36,
        flops=8 * length * width * local,
    )


def halve_small_kernel(place, own, got, sums, outer, inner, keep, send, *, slot):
    h, width = keep.shape
    bit = place[slot]
    stay = pl.ds(pl.multiple_of(bit * h, ROOM), h)
    go = pl.ds(pl.multiple_of((1 - bit) * h, ROOM), h)
    keep[...] = own[stay, :] + got[stay, :]
    send[...] = own[go, :] + got[go, :]
    rows = [x[i : i + 1, j : j + width] for x in (sums, outer, inner) for i in range(x.shape[0]) for j in range(0, x.shape[1], width)]

    def put(ref):
        for i, row in enumerate(rows):
            ref[h - ROOM + i : h - ROOM + i + 1, :] += row

    @pl.when(bit == 0)
    def _():
        put(keep)

    @pl.when(bit == 1)
    def _():
        put(send)


def halve_small(place, slot, after, own, got, *small):
    n, width = own.shape
    return launch(
        functools.partial(halve_small_kernel, slot=slot),
        "halve_small",
        (1,),
        (place,),
        after,
        [(x, once(*x.shape)) for x in (own, got, *small)],
        [((n // 2, width), F32, once(n // 2, width))] * 2,
    )


def finish_kernel(*refs, cuts, last):
    n = len(cuts) - 1
    wide, (mine, got), (row, out) = refs[: -2 * n - 2], (refs[-2 * n - 2 : -n - 2], refs[-n - 2 : -2]), refs[-2:]
    i = pl.program_id(0)
    x = wide[0][...].astype(F32)

    def one(total):
        if not last:
            out[...] = (x + total + row[...]).astype(BF16)
            return
        unit, inverse = norm_rows(x)
        d_unit = total * row[...]
        centre = jnp.mean(d_unit, axis=1, keepdims=True)
        slope = jnp.mean(d_unit * unit, axis=1, keepdims=True)
        out[...] = (
            wide[1][...].astype(F32) + inverse * (d_unit - centre - unit * slope)
        ).astype(BF16)

    for k in range(n):

        @pl.when(jnp.logical_and(i >= cuts[k], i < cuts[k + 1]))
        def _():
            one(mine[k][...] + got[k][...])


def finish(name, after, wide, mine, got, row, start=0, into=None, rows=128, vmem=16):
    length, width = wide[0].shape
    cuts, pieces = cut_specs([x.shape[0] for x in mine], rows, width)
    first = start // rows
    here = pl.BlockSpec((rows, width), lambda i: (first + i, 0))
    return launch(
        functools.partial(finish_kernel, cuts=cuts, last=len(wide) > 1),
        name,
        (cuts[-1],),
        (),
        after,
        [(x, here) for x in wide]
        + list(zip(mine, pieces))
        + list(zip(got, pieces))
        + [(row, whole(1, width))],
        [((length, width), BF16, here)],
        vmem=vmem,
        into=into,
    )[0]


def halve_kernel(place, a, b, c, d, keep, send):
    keep[...] = a[...] + b[...]
    send[...] = c[...] + d[...]


def halve(place, slot, after, mine, got):
    n, width = mine.shape
    h = n // 2
    rows = h // 2 if h * width > (256 << 10) else h
    steps = h // rows

    def bit(place):
        return 0 if slot is None else place[slot]

    keep = pl.BlockSpec((rows, width), lambda i, place: (bit(place) * steps + i, 0))
    send = pl.BlockSpec((rows, width), lambda i, place: ((1 - bit(place)) * steps + i, 0))
    here = pl.BlockSpec((rows, width), lambda i, _: (i, 0))
    return launch(
        halve_kernel,
        "halve",
        (steps,),
        (place,),
        after,
        [(mine, keep), (got, keep), (mine, send), (got, send)],
        [((h, width), F32, here)] * 2,
    )


def pack_kernel(a, b, c, d, out):
    n = a.shape[0]
    out[:n, :] = a[...] + b[...]
    out[n:, :] = c[...] + d[...]


def pack(after, a, b, c, d):
    shape = (a.shape[0] + c.shape[0], a.shape[1])
    return launch(
        pack_kernel,
        "pack",
        (1,),
        (),
        after,
        [(x, whole(*x.shape)) for x in (a, b, c, d)],
        [(shape, F32, whole(*shape))],
    )[0]


def plus_kernel(a, b, out):
    out[...] = a[...] + b[...]


def plus(after, a, b):
    return launch(
        plus_kernel,
        "plus",
        (1,),
        (),
        after,
        [(x, whole(*x.shape)) for x in (a, b)],
        [(a.shape, F32, whole(*a.shape))],
    )[0]


def part_kernel(a, b, first, second):
    n = first.shape[0]
    first[...] = a[:n, :] + b[:n, :]
    second[...] = a[n:, :] + b[n:, :]


def part(after, n, a, b):
    shapes = [(n, a.shape[1]), (a.shape[0] - n, a.shape[1])]
    return launch(
        part_kernel,
        "part",
        (1,),
        (),
        after,
        [(x, whole(*x.shape)) for x in (a, b)],
        [(shape, F32, whole(*shape)) for shape in shapes],
    )


def join_kernel(place, *refs, slots):
    parts, out, sems = refs[:-2], refs[-2], refs[-1]
    copies = []
    start = 0
    for i, slot in enumerate(slots):
        mine, got = parts[2 * i : 2 * i + 2]
        h = mine.shape[0]
        bit = 0 if slot is None else place[slot]
        copies += [
            pltpu.make_async_copy(mine, out.at[pl.ds(start + bit * h, h)], sems.at[2 * i]),
            pltpu.make_async_copy(got, out.at[pl.ds(start + (1 - bit) * h, h)], sems.at[2 * i + 1]),
        ]
        start += 2 * h
    for copy in copies:
        copy.start()
    for copy in copies:
        copy.wait()


def join(place, after, *parts):
    width = parts[0][0].shape[1]
    rows = sum(2 * mine.shape[0] for mine, _, _ in parts)
    anywhere = pl.BlockSpec(memory_space=pltpu.HBM)
    return launch(
        functools.partial(join_kernel, slots=[slot for _, _, slot in parts]),
        "join",
        (1,),
        (place,),
        after,
        [(x, anywhere) for mine, got, _ in parts for x in (mine, got)],
        [((rows, width), F32, once(rows, width))],
        [pltpu.SemaphoreType.DMA((2 * len(parts),))],
    )[0]


def assemble_kernel(place, *refs):
    arrays, (qkv, merge) = refs[:8], refs[8:]
    count = qkv.shape[1]
    j, t = pl.program_id(0), pl.program_id(1)
    core = place[0]
    for other in range(2):
        for p in range(2):
            bit = place[bit_slot(p, 0)] if other == 0 else place[NEAR + p]
            for half in range(2):
                x = arrays[4 * other + 2 * p + half]
                mine = (j == 2 * (core if other == 0 else 1 - core) + p) & (
                    t == (bit if half == 0 else 1 - bit)
                )

                @pl.when(mine & (j < 3))
                def _():
                    qkv[0] = x[:count, :]

                @pl.when(mine & (j == 3))
                def _():
                    merge[...] = x[:count, :]


def small_kernel(place, own0, own1, near0, near1, out):
    one = jnp.where(place[bit_slot(1, 0)] == 0, own0[...], own1[...])
    two = jnp.where(place[NEAR + 1] == 0, near0[...], near1[...])
    out[...] = one + two


def small_sums(place, after, arrays, rows=16):
    n, width = arrays[0].shape
    room = pl.BlockSpec((rows, width), lambda i, _: ((n - ROOM) // rows, 0))
    return launch(
        small_kernel,
        "small_sums",
        (1,),
        (place,),
        after,
        [(x, room) for x in arrays],
        [((rows, width), F32, whole(rows, width))],
    )[0]


def assemble(place, after, arrays, width):
    local = arrays[0].shape[1]
    half = width // 2
    return launch(
        assemble_kernel,
        "assemble",
        (4, 2),
        (place,),
        after,
        [(x, once(*x.shape)) for x in arrays],
        [
            (
                (3, width, local),
                F32,
                pl.BlockSpec(
                    (1, half, local),
                    lambda j, t, _: (jnp.minimum(j, 2), jnp.where(j < 3, t, 1), 0),
                ),
            ),
            (
                (local, width),
                F32,
                pl.BlockSpec((local, half), lambda j, t, _: (0, jnp.where(j < 3, 0, t))),
            ),
        ],
        vmem=40,
    )


def spread_kernel(low, high, up, down):
    piece, width = low.shape[1] // 2, low.shape[2]
    down[0] = low[0, :piece, :]
    down[1] = high[0, :piece, :]
    up[:, :width] = low[0, piece:, :]
    up[:, width:] = high[0, piece:, :]


def spread(after, gathered):
    count, rows, width = gathered.shape
    piece = rows // 2
    half = count // 2
    return launch(
        spread_kernel,
        "spread",
        (half,),
        (),
        after,
        [
            (gathered, pl.BlockSpec((1, rows, width), lambda n: (n, 0, 0))),
            (gathered, pl.BlockSpec((1, rows, width), lambda n: (half + n, 0, 0))),
        ],
        [
            ((half * piece, 2 * width), F32, pl.BlockSpec((piece, 2 * width), lambda n: (n, 0))),
            (
                (2, half * piece, width),
                F32,
                pl.BlockSpec((2, piece, width), lambda n: (0, n, 0)),
            ),
        ],
        vmem=60,
    )


AXES = ("xlo", "z", "y", "core", "tensor")
RINGS = ("z", "y", "core")
DIRECTIONS = (("y", 0), ("z", 0), ("y", 1), ("z", 1))
SWAP = ((0, 1), (1, 0))


def partner(place, bit):
    return place ^ 1 if bit == 0 else 3 - place


def bit_at(place, bit):
    return int(place in (1, 2)) if bit == 0 else int(place >= 2)


def order_of(core, part):
    return [(core + 2 * part + step) % 4 for step in range(4)]


def spot_of(z, y, core, part):
    spot = 0
    for direction in order_of(core, part):
        axis, bit = DIRECTIONS[direction]
        spot = 2 * spot + bit_at(y if axis == "y" else z, bit)
    return spot


def step_pairs(part, step):
    pairs = []
    for z in range(4):
        for y in range(4):
            for core in range(2):
                axis, bit = DIRECTIONS[order_of(core, part)[step]]
                z2, y2 = (z, partner(y, bit)) if axis == "y" else (partner(z, bit), y)
                pairs.append(((z * 4 + y) * 2 + core, (z2 * 4 + y2) * 2 + core))
    return pairs


def place_table():
    rows = []
    for z in range(4):
        for y in range(4):
            for core in range(2):
                row = [core]
                for part in range(2):
                    for direction in order_of(core, part):
                        axis, bit = DIRECTIONS[direction]
                        row.append(bit_at(y if axis == "y" else z, bit))
                for half in (core, 1 - core):
                    row.append(half)
                    for part in range(2):
                        here = spot_of(z, y, half, part)
                        row += [
                            here ^ spot_of(z2, y2, half, part) for z2 in range(4) for y2 in range(4)
                        ]
                for part in range(2):
                    axis, bit = DIRECTIONS[order_of(1 - core, part)[0]]
                    row.append(bit_at(y if axis == "y" else z, bit))
                rows.append(row)
    return np.array(rows, np.int32)


OWN = 9
OTHER = OWN + 33
NEAR = OTHER + 33


def bit_slot(part, step):
    return 1 + 4 * part + step


def send_step(x, part, step):
    return lax.ppermute(x, RINGS, step_pairs(part, step))


def exchange(x, axis):
    return lax.ppermute(x, axis, SWAP)


def body(
    tokens,
    norm_gain,
    norm_shift,
    qkv_weight,
    merge_weight,
    up_weight,
    inner_shift,
    down_weight,
    outer_shift,
    cotangent,
):
    length, width = tokens.shape
    local = merge_weight.shape[0]
    hidden = up_weight.shape[1]
    place = lax.dynamic_index_in_dim(
        jnp.asarray(place_table()), lax.axis_index(RINGS), 0, keepdims=False
    )
    cos, sin = rotary_tables(length)
    w3 = qkv_weight.transpose(1, 0, 2)
    gain, shift, inner_row = norm_gain[None], norm_shift[None], inner_shift[None]

    normed, normed_t, q, k, v, dh, outer_g = project(
        tokens, gain, shift, w3, merge_weight, cotangent, cos, sin
    )
    out_f, dn_f, active, d_pre, inner_g = hidden_pass(
        (outer_g,), normed, cotangent, up_weight, inner_row, down_weight
    )

    (down_s,) = down_grad(place, OTHER, (inner_g,), active, cotangent)
    down_got = exchange(down_s, "core")
    (up_s,) = up_grad(place, OTHER, (down_s,), normed_t, d_pre)
    up_got = exchange(up_s, "core")

    ho0, dq0, dk_part, dv_part = attend(0, (up_s,), q, k, v, dh, cos, sin)
    mine = list(forward_part(0, (dq0,), ho0, merge_weight, out_f, (512,)))
    theirs = [exchange(mine[0], "tensor")]

    def flat(x):
        return x.reshape(-1, x.shape[-1])

    down_k, down_s = map(flat, down_grad(place, OWN, (mine[0],), active, cotangent, down_got))
    down_got = send_step(down_s, 0, 0)
    up_k, up_s = map(flat, up_grad(place, OWN, (down_s,), normed_t, d_pre, up_got))
    up_got = send_step(up_s, 1, 0)

    ho1, dq1, dk, dv = attend(1, (up_s,), q, k, v, dh, cos, sin, (dk_part, dv_part))
    mine += forward_part(1, (dq1,), ho1, merge_weight, out_f, (512,))
    theirs += [exchange(x, "tensor") for x in mine[1:]]

    own0, own1, tail_s0, tail_s1 = tail(
        place, (mine[1],), normed_t, ho0, ho1, cotangent, dq0, dq1, dk, dv
    )
    tail_got0 = exchange(tail_s0, "core")
    tail_got1 = exchange(tail_s1, "core")
    down_k, down_s = halve(place, None, (tail_s0, theirs[0]), down_k, down_got)
    down_got = send_step(down_s, 0, 1)
    up_k, up_s = halve(place, None, (down_s,), up_k, up_got)
    up_got = send_step(up_s, 1, 1)
    back, sums = backward_pass((up_s,), dq0, dq1, dk, dv, w3, dn_f, tokens)

    tail_k0, tail_s0 = halve(place, bit_slot(0, 0), (sums,), own0, tail_got0)
    tail_got0 = send_step(tail_s0, 0, 0)
    tail_k1, tail_s1 = halve_small(
        place, bit_slot(1, 0), (tail_s0,), own1, tail_got1, sums, outer_g, inner_g
    )
    tail_got1 = send_step(tail_s1, 1, 0)

    down_k, down_s = halve(place, None, (tail_s1,), down_k, down_got)
    down_got = send_step(down_s, 0, 2)
    up_k, up_s = halve(place, None, (down_s,), up_k, up_got)
    up_got = send_step(up_s, 1, 2)

    tail_k0, tail_s0 = halve(place, bit_slot(0, 1), (up_s,), tail_k0, tail_got0)
    tail_got0 = send_step(tail_s0, 0, 1)
    tail_k1, tail_s1 = halve(place, bit_slot(1, 1), (tail_s0,), tail_k1, tail_got1)
    tail_got1 = send_step(tail_s1, 1, 1)

    down_k, down_s = halve(place, None, (tail_s1,), down_k, down_got)
    down_got = send_step(down_s, 0, 3)
    up_k, up_s = halve(place, None, (down_s,), up_k, up_got)
    up_got = send_step(up_s, 1, 3)

    tail_k0, tail_s0 = halve(place, bit_slot(0, 2), (up_s, theirs[1]), tail_k0, tail_got0)
    tail_got0 = send_step(tail_s0, 0, 2)
    tail_k1, tail_s1 = halve(place, bit_slot(1, 2), (tail_s0,), tail_k1, tail_got1)
    tail_got1 = send_step(tail_s1, 1, 2)

    feed_x = pack((tail_s1,), down_k, down_got, up_k, up_got)
    feed_got = exchange(feed_x, "xlo")
    (back0,) = hand((feed_x,), back, 0, (128,))
    back_got0 = exchange(back0, "tensor")

    tail_k0, tail_s0 = halve(place, bit_slot(0, 3), (back0,), tail_k0, tail_got0)
    tail_got0 = send_step(tail_s0, 0, 3)
    tail_k1, tail_s1 = halve(place, bit_slot(1, 3), (tail_s0,), tail_k1, tail_got1)
    tail_got1 = send_step(tail_s1, 1, 3)

    feed_x = plus((tail_s1,), feed_x, feed_got)
    gathered = lax.all_gather(feed_x, ("core", "z", "y"))

    tail_x = pack((feed_x,), tail_k0, tail_got0, tail_k1, tail_got1)
    tail_got = exchange(tail_x, "xlo")

    tail0, tail1 = part((tail_x, back_got0), tail_k0.shape[0], tail_x, tail_got)
    tail_got0 = send_step(tail0, 0, 3)
    tail_got1 = send_step(tail1, 1, 3)

    backs = list(hand((tail1,), back, 128, (256,)))
    backs += hand((backs[0],), back, 384, (384, 256))
    back_gots = [exchange(x, "tensor") for x in backs]

    turn = backs[1]
    for step in (3, 2, 1):
        sink = (back_gots[0],) if step == 2 else ()
        other = (back_gots[1],) if step == 1 else ()
        tail0 = join(place, (turn, tail1, *sink), (tail0, tail_got0, bit_slot(0, step)))
        tail_got0 = send_step(tail0, 0, step - 1)
        tail1 = join(place, (tail0, *other), (tail1, tail_got1, bit_slot(1, step)))
        tail_got1 = send_step(tail1, 1, step - 1)
        if step == 3:
            block_out = finish(
                "finish_out", (tail1,), (tokens,), mine, theirs, outer_shift[None]
            )
            turn = block_out
        if step == 2:
            token_grad = finish(
                "finish_grad", (tail1,), (tokens, cotangent), (back0, backs[0]),
                (back_got0, back_gots[0]), gain, vmem=60,
            )
            turn = token_grad

    up_out, down_out = spread((tail1,), gathered)
    down_out = down_out.reshape(hidden, width)

    near0, near1 = exchange(tail0, "core"), exchange(tail1, "core")
    tail_got0, tail_got1 = hand_all((up_out,), tail_got0, tail_got1)
    near_got0, near_got1 = exchange(tail_got0, "core"), exchange(tail_got1, "core")
    token_grad = finish(
        "finish_grad", (tail_got0,), (tokens, cotangent), (backs[1],), (back_gots[1],), gain,
        start=384, into=token_grad, vmem=60,
    )
    own = (tail0, tail_got0, tail1, tail_got1)
    near = (near0, near_got0, near1, near_got1)
    small = small_sums(place, (token_grad,), (*own[2:], *near[2:]))
    pair = small[:4].reshape(2, width)
    pair = pair + exchange(pair, "tensor")
    qkv_out, merge_out = assemble(place, (small,), (*own, *near), width)
    token_grad = finish(
        "finish_grad", (merge_out,), (tokens, cotangent), (backs[2],), (back_gots[2],), gain,
        start=768, into=token_grad, vmem=60,
    )
    return (
        block_out,
        token_grad,
        pair[0],
        pair[1],
        qkv_out.transpose(1, 0, 2),
        merge_out,
        up_out,
        small[6 : 6 + hidden // local].reshape(hidden),
        down_out,
        small[4:6].reshape(width),
    )


def solution(mesh):
    dp = AXES[:4]
    finer = Mesh(mesh.devices.reshape(2, 4, 4, 2, 2), AXES)
    return jax.shard_map(
        body,
        mesh=finer,
        in_specs=(
            P(dp, None),
            P(),
            P(),
            P(None, None, "tensor"),
            P("tensor", None),
            P(None, "tensor"),
            P("tensor"),
            P("tensor", None),
            P(),
            P(dp, None),
        ),
        out_specs=(
            P(dp, None),
            P(dp, None),
            P(),
            P(),
            P(None, None, "tensor"),
            P("tensor", None),
            P(None, "tensor"),
            P("tensor"),
            P("tensor", None),
            P(),
        ),
        check_vma=False,
    )
```

```python
import functools

import jax
import jax.numpy as jnp
import numpy as np
from jax import lax
from jax.experimental import pallas as pl
from jax.experimental.pallas import tpu as pltpu
from jax.sharding import Mesh
from jax.sharding import PartitionSpec as P

F32 = jnp.float32
BF16 = jnp.bfloat16
HEAD = 64
ROT = 32
PAIR = 2 * HEAD
epsilon = 1e-05


def nn(a, b):
    return jnp.dot(a, b, preferred_element_type=F32)


def nt(a, b):
    return lax.dot_general(a, b, (((1,), (1,)), ((), ())), preferred_element_type=F32)


def tn(a, b):
    return lax.dot_general(a, b, (((0,), (0,)), ((), ())), preferred_element_type=F32)


def rotary_tables(length):
    half = ROT // 2
    rates = np.float32(10000.0) ** (-np.arange(half, dtype=np.float32) / np.float32(half))
    angles = np.arange(length, dtype=np.float32)[:, None] * rates[None, :].astype(np.float32)
    angles = np.repeat(angles, 2, axis=1)
    sign = np.where(np.arange(ROT) % 2 == 0, -1.0, 1.0)
    rest = np.ones((length, HEAD - ROT))
    cosine = np.concatenate([np.cos(angles), rest], axis=1)
    sine = np.concatenate([np.sin(angles) * sign, 0 * rest], axis=1)
    return tuple(jnp.asarray(np.tile(x, (1, 2)).astype(np.float32)) for x in (cosine, sine))


def swap_pairs(x):
    lane = lax.broadcasted_iota(jnp.int32, x.shape, 1)
    return jnp.where(lane % 2 == 0, pltpu.roll(x, PAIR - 1, 1), pltpu.roll(x, 1, 1))


def launch(kernel, name, grid, scalars, after, ins, outs, scratch=(), vmem=16, flops=0, into=None):
    if into is not None:
        after = (*after, into)
    first, skipped = len(scalars), len(after)

    def without(*refs):
        kernel(*refs[:first], *refs[first + skipped :])

    got = pl.pallas_call(
        without,
        grid_spec=pltpu.PrefetchScalarGridSpec(
            num_scalar_prefetch=first,
            grid=grid,
            in_specs=[pl.BlockSpec(memory_space=pltpu.HBM)] * skipped + [spec for _, spec in ins],
            out_specs=[spec for _, _, spec in outs],
            scratch_shapes=list(scratch),
        ),
        out_shape=[jax.ShapeDtypeStruct(shape, dtype) for shape, dtype, _ in outs],
        compiler_params=pltpu.CompilerParams(vmem_limit_bytes=vmem << 20),
        input_output_aliases={} if into is None else {first + skipped - 1: 0},
        cost_estimate=pl.CostEstimate(
            flops=flops,
            bytes_accessed=sum(x.size * x.dtype.itemsize for x, _ in ins)
            + sum(int(np.prod(shape)) * jnp.dtype(dtype).itemsize for shape, dtype, _ in outs),
            transcendentals=0,
        ),
        name=name,
    )(*scalars, *after, *[array for array, _ in ins])
    return got


TOKEN = ((8, 128), F32, pl.BlockSpec((8, 128), lambda *_: (0, 0)))


def whole(*shape):
    return pl.BlockSpec(shape, lambda *_: (0,) * len(shape))


def once(*shape):
    return pl.BlockSpec(shape, lambda *_: (0,) * len(shape), pipeline_mode=pl.Buffered(1))


gelu_rate = float(np.sqrt(2 / np.pi))
SMALL = 16


def norm_rows(x):
    centred = x - jnp.mean(x, axis=1, keepdims=True)
    inverse = lax.rsqrt(jnp.mean(centred * centred, axis=1, keepdims=True) + epsilon)
    return centred * inverse, inverse


def project_kernel(
    tok, gain, shift, w_in, mw_in, cot, cos, sin, normed, normed_t, q, k, v, dh, outer, w, mw, sems
):
    first = pl.program_id(0) == 0
    copies = [pltpu.make_async_copy(mw_in, mw, sems.at[0])] + [
        pltpu.make_async_copy(w_in.at[which], w.at[which], sems.at[1 + which]) for which in range(3)
    ]

    @pl.when(first)
    def _():
        for copy in copies:
            copy.start()

    def body(arriving):
        unit, _ = norm_rows(tok[...].astype(F32))
        n = (unit * gain[...] + shift[...]).astype(BF16)
        normed[...] = n
        normed_t[...] = n.T
        total = jnp.sum(cot[...].astype(F32), axis=0, keepdims=True)
        outer[...] = total if arriving else outer[...] + total
        if arriving:
            copies[0].wait()
        dh[...] = nt(cot[...], mw[...]).astype(BF16)
        c = cos[...]
        s = sin[...]
        for which, ref in enumerate((q, k, v)):
            if arriving:
                copies[1 + which].wait()
            joined = nn(n, w[which])
            if which == 2:
                ref[...] = joined.astype(BF16)
                continue
            for p in range(joined.shape[1] // PAIR):
                block = joined[:, p * PAIR : (p + 1) * PAIR]
                turned = (block * c + swap_pairs(block) * s).astype(BF16)
                if which == 0:
                    turned = turned * jnp.asarray(HEAD**-0.5, BF16)
                ref[:, p * PAIR : (p + 1) * PAIR] = turned

    @pl.when(first)
    def _():
        body(True)

    @pl.when(jnp.logical_not(first))
    def _():
        body(False)


def project(tok, gain, shift, w3, mw, cot, cos, sin, rows=256):
    length, width = tok.shape
    local = mw.shape[0]

    def row_block(n):
        return pl.BlockSpec((rows, n), lambda i: (i, 0))

    def out(n):
        return ((length, n), BF16, row_block(n))

    return launch(
        project_kernel,
        "project",
        (length // rows,),
        (),
        (),
        [
            (tok, row_block(width)),
            (gain, whole(1, width)),
            (shift, whole(1, width)),
            (w3, pl.BlockSpec(memory_space=pltpu.HBM)),
            (mw, pl.BlockSpec(memory_space=pltpu.HBM)),
            (cot, row_block(width)),
            (cos, row_block(PAIR)),
            (sin, row_block(PAIR)),
        ],
        [out(width), ((width, length), BF16, pl.BlockSpec((width, rows), lambda i: (0, i)))]
        + [out(local)] * 4
        + [((1, width), F32, whole(1, width))],
        [
            pltpu.VMEM((3, width, local), BF16),
            pltpu.VMEM((local, width), BF16),
            pltpu.SemaphoreType.DMA((4,)),
        ],
        vmem=60,
        flops=8 * length * width * local,
    )


def hidden_kernel(normed, cot, up_in, shift, down_in, out, dn, act, dpre, ig, up, down, sems, *, cols):
    first = pl.program_id(0) == 0
    cuts = [slice(j, j + cols) for j in range(0, up.shape[1], cols)]
    copies = []
    for j, s in enumerate(cuts):
        copies.append(
            (
                pltpu.make_async_copy(up_in.at[:, s], up.at[:, s], sems.at[2 * j]),
                pltpu.make_async_copy(down_in.at[s, :], down.at[s, :], sems.at[2 * j + 1]),
            )
        )

    @pl.when(first)
    def _():
        for pair in copies:
            for copy in pair:
                copy.start()

    def body(arriving):
        n = normed[...]
        c = cot[...]
        sums = []
        for j, s in enumerate(cuts):
            if arriving:
                for copy in copies[j]:
                    copy.wait()
            v = nn(n, up[:, s]) + shift[:, s]
            da = nt(c, down[s, :])
            square = v * v
            t = jnp.tanh(gelu_rate * v * (1.0 + 0.044715 * square))
            h = 0.5 * (1.0 + t)
            act[:, s] = (v * h).astype(BF16)
            slope = h + (0.5 * gelu_rate) * v * (1.0 - t * t) * (1.0 + (3 * 0.044715) * square)
            d_pre = (da * slope).astype(BF16)
            dpre[:, s] = d_pre
            sums.append(jnp.sum(d_pre.astype(F32), axis=0, keepdims=True))
        sums = jnp.concatenate(sums, axis=1)
        ig[...] = sums if arriving else ig[...] + sums
        out[...] = nn(act[...], down[...])
        dn[...] = nt(dpre[...], up[...])

    @pl.when(first)
    def _():
        body(True)

    @pl.when(jnp.logical_not(first))
    def _():
        body(False)


def hidden_pass(after, normed, cot, up, shift, down, rows=256, cols=512):
    length, width = normed.shape
    hidden = up.shape[1]

    def here(n):
        return pl.BlockSpec((rows, n), lambda i: (i, 0))

    return launch(
        functools.partial(hidden_kernel, cols=cols),
        "hidden",
        (length // rows,),
        (),
        after,
        [
            (normed, here(width)),
            (cot, here(width)),
            (up, pl.BlockSpec(memory_space=pltpu.HBM)),
            (shift, whole(1, hidden)),
            (down, pl.BlockSpec(memory_space=pltpu.HBM)),
        ],
        [((length, width), F32, here(width))] * 2
        + [((length, hidden), BF16, here(hidden))] * 2
        + [((1, hidden), F32, whole(1, hidden))],
        [
            pltpu.VMEM((width, hidden), BF16),
            pltpu.VMEM((hidden, width), BF16),
            pltpu.SemaphoreType.DMA((2 * hidden // cols,)),
        ],
        vmem=60,
        flops=9 * length * width * hidden,
    )


def grad_kernel(place, lhs, rhs, *rest, base, product, own):
    if own:
        got, keep, send, buf, sems, land, land_sems = rest
    else:
        out, buf, sems = rest
    j = pl.program_id(0)
    size = buf.shape[1] // 8

    def arriving(n):
        return pltpu.make_async_copy(
            got.at[place[base + n]], land.at[pl.ds(n * size, size)], land_sems.at[n]
        )

    if own:

        @pl.when(j == 0)
        def _():
            for n in range(16):
                arriving(n).start()

    buf[j] = product(lhs[...], rhs[...])
    if own:

        @pl.when(j == 0)
        def _():
            for n in range(8):
                arriving(n).wait()

        @pl.when(j == 1)
        def _():
            for n in range(8, 16):
                arriving(n).wait()

        buf[j] += land[pl.ds(pl.multiple_of(j * 8 * size, size), 8 * size), :]

    for i in range(8):
        spot = place[base + j * 8 + i]
        block = buf.at[j, pl.ds(i * size, size)]
        sem = sems.at[j * 8 + i]
        if own:

            @pl.when(spot < 8)
            def _():
                pltpu.make_async_copy(block, keep.at[spot], sem).start()

            @pl.when(spot >= 8)
            def _():
                pltpu.make_async_copy(block, send.at[spot - 8], sem).start()

        else:
            pltpu.make_async_copy(block, out.at[spot], sem).start()

    @pl.when(j == 1)
    def _():
        for n in range(16):
            block = buf.at[n // 8, pl.ds((n % 8) * size, size)]
            pltpu.make_async_copy(block, (keep if own else out).at[0], sems.at[n]).wait()


def grad(place, base, spots, after, lhs, rhs, specs, product, got=None):
    width = 1024
    rows = 1024
    own = got is not None
    piece = rows // 16
    anywhere = pl.BlockSpec(memory_space=pltpu.HBM)
    scratch = [pltpu.VMEM((2, rows // 2, width), F32), pltpu.SemaphoreType.DMA((16,))]
    if own:
        scratch += [pltpu.VMEM((rows, width), F32), pltpu.SemaphoreType.DMA((16,))]
    outs = [((8 if own else 16, piece, width), F32, anywhere)] * (2 if own else 1)
    return launch(
        functools.partial(grad_kernel, base=spots, product=product, own=own),
        "grad",
        (2,),
        (place,),
        after,
        [(lhs, specs[0]), (rhs, specs[1])] + ([(got, anywhere)] if own else []),
        outs,
        scratch,
        vmem=24,
        flops=2 * rows * width * lhs.shape[0],
    )


def down_grad(place, base, after, active, cot, got=None):
    length, width = cot.shape
    block = pl.BlockSpec((length, 512), lambda j, place: (0, place[base] * 2 + j))
    return grad(
        place, base, base + 1, after, active, cot, (block, once(length, width)), tn, got
    )


def up_grad(place, base, after, normed_t, d_pre, got=None):
    width, length = normed_t.shape
    rows = pl.BlockSpec((512, length), lambda j, _: (j, 0))
    half = pl.BlockSpec(
        (length, 1024), lambda j, place: (0, place[base]), pipeline_mode=pl.Buffered(1)
    )
    return grad(place, base, base + 17, after, normed_t, d_pre, (rows, half), nn, got)


def attend_kernel(*refs, last, sub):
    if last:
        q, do, k, v, dk_in, dv_in, cos, sin, ho, dq, dk, dv, dk_sum, dv_sum = refs
    else:
        q, do, k, v, cos, sin, ho, dq, dk_sum, dv_sum = refs
    block = q.shape[0]
    seen = k.shape[0]
    low = lax.broadcasted_iota(jnp.int32, (sub, PAIR), 1) < HEAD
    zero = jnp.zeros((sub, PAIR), BF16)
    causal = lax.broadcasted_iota(jnp.int32, (sub, sub), 1) <= lax.broadcasted_iota(
        jnp.int32, (sub, sub), 0
    )
    for i in range(block // sub):
        before = seen - block + i * sub
        upto = before + sub
        rows = slice(i * sub, (i + 1) * sub)
        keys = k[0:upto, :]
        values = v[0:upto, :]
        heads = [
            [jnp.where(low, x[rows, :], zero), jnp.where(low, zero, x[rows, :])] for x in (q, do)
        ]
        scores = [nt(x, keys) for x in heads[0]]
        d_probs = [nt(x, values) for x in heads[1]]
        probs_low, d_scores = [], []
        for h in range(2):
            edge = jnp.where(causal, scores[h][:, before:], -1e30)
            if before:
                edge = jnp.concatenate([scores[h][:, :before], edge], axis=1)
            expo = jnp.exp(edge - jnp.max(edge, axis=1, keepdims=True))
            probs = expo * (1.0 / jnp.sum(expo, axis=1, keepdims=True))
            inner = jnp.sum(probs * d_probs[h], axis=1, keepdims=True)
            probs_low.append(probs.astype(BF16))
            d_scores.append((probs * (d_probs[h] - inner)).astype(BF16))
        mixed = [nn(x, values) for x in probs_low]
        ho[rows, :] = jnp.where(low, mixed[0], mixed[1]).astype(BF16)
        d_query = [nn(x, keys) for x in d_scores]
        d_query = jnp.where(low, d_query[0], d_query[1]) * HEAD**-0.5
        turn = slice(before, upto)
        dq[rows, :] = (
            d_query * cos[turn, :] - swap_pairs(d_query) * sin[turn, :]
        ).astype(BF16)
        for left, right, total in ((probs_low, heads[1], dv_sum), (d_scores, heads[0], dk_sum)):
            add = tn(left[0], right[0]) + tn(left[1], right[1])
            if i == 0:
                total[0:upto, :] = add
            else:
                total[0:before, :] += add[:before]
                total[before:upto, :] = add[before:]
    if last:
        before = seen - block
        dk_sum[0:before, :] += dk_in[...]
        dv_sum[0:before, :] += dv_in[...]
        for i in range(seen // block):
            rows = slice(i * block, (i + 1) * block)
            d_keys = dk_sum[rows, :]
            dk[rows, :] = (d_keys * cos[rows, :] - swap_pairs(d_keys) * sin[rows, :]).astype(BF16)
            dv[rows, :] = dv_sum[rows, :].astype(BF16)


def attend(part, after, q, k, v, do, cos, sin, carried=(), sub=256):
    length, local = q.shape
    half = length // 2
    seen = half * (part + 1)
    rows = pl.BlockSpec((half, PAIR), lambda p: (part, p))
    keys = pl.BlockSpec((seen, PAIR), lambda p: (0, p))
    table = pl.BlockSpec((seen, PAIR), lambda p: (0, 0))
    here = pl.BlockSpec((half, PAIR), lambda p: (0, p))
    outs = [((half, local), BF16, here)] * 2
    scratch = ()
    if part == 0:
        outs += [((half, local), F32, here)] * 2
    else:
        outs += [((length, local), BF16, keys)] * 2
        scratch = [pltpu.VMEM((length, PAIR), F32)] * 2
    return launch(
        functools.partial(attend_kernel, last=part == 1, sub=sub),
        "attend",
        (local // PAIR,),
        (),
        after,
        [(q, rows), (do, rows), (k, keys), (v, keys)]
        + [(x, here) for x in carried]
        + [(cos, table), (sin, table)],
        outs,
        scratch,
        flops=30 * half * seen * PAIR * local // PAIR,
    )


def forward_kernel(ho, mw, a, *pieces, cuts):
    i = pl.program_id(0)
    total = nn(ho[...], mw[...]) + a[...]
    for n, piece in enumerate(pieces):

        @pl.when(jnp.logical_and(i >= cuts[n], i < cuts[n + 1]))
        def _():
            piece[...] = total


def within(first, last):
    return lambda i, *_: (jnp.clip(i, first, last - 1) - first, 0)


def cut_specs(sizes, rows, width):
    cuts = [int(n) // rows for n in np.cumsum((0,) + tuple(sizes))]
    return cuts, [
        pl.BlockSpec((rows, width), within(cuts[k], cuts[k + 1])) for k in range(len(sizes))
    ]


def forward_part(part, after, ho, mw, a, sizes, rows=128):
    half, local = ho.shape
    width = mw.shape[1]
    steps = half // rows
    cuts, specs = cut_specs(sizes, rows, width)
    there = pl.BlockSpec((rows, width), lambda i: (part * steps + i, 0))
    return launch(
        functools.partial(forward_kernel, cuts=cuts),
        "forward",
        (steps,),
        (),
        after,
        [
            (ho, pl.BlockSpec((rows, local), lambda i: (i, 0))),
            (mw, once(local, width)),
            (a, there),
        ],
        [((n, width), F32, spec) for n, spec in zip(sizes, specs)],
        flops=2 * half * width * local,
    )


def backward_kernel(dq0, dq1, dk, dv, w, a, tok, *rest, cuts):
    pieces, sums = rest[:-1], rest[-1]
    i = pl.program_id(0)

    def one(dq):
        total = nt(dq[...], w[0]) + nt(dk[...], w[1]) + nt(dv[...], w[2]) + a[...]
        for n, piece in enumerate(pieces):

            @pl.when(jnp.logical_and(i >= cuts[n], i < cuts[n + 1]))
            def _():
                piece[...] = total

        unit, _ = norm_rows(tok[...].astype(F32))
        both = jnp.concatenate(
            [jnp.sum(total * unit, axis=0, keepdims=True), jnp.sum(total, axis=0, keepdims=True)],
            axis=0,
        )

        @pl.when(i == 0)
        def _():
            sums[...] = both

        @pl.when(i > 0)
        def _():
            sums[...] += both

    half = pl.num_programs(0) // 2

    @pl.when(i < half)
    def _():
        one(dq0)

    @pl.when(i >= half)
    def _():
        one(dq1)


def backward_pass(after, dq0, dq1, dk, dv, w3, a, tok, sizes, rows=256):
    length, local = dk.shape
    width = w3.shape[1]
    steps = length // rows
    cuts, specs = cut_specs(sizes, rows, width)
    here = pl.BlockSpec((rows, width), lambda i: (i, 0))
    narrow = pl.BlockSpec((rows, local), lambda i: (i, 0))
    return launch(
        functools.partial(backward_kernel, cuts=cuts),
        "backward",
        (steps,),
        (),
        after,
        [
            (dq0, pl.BlockSpec((rows, local), within(0, steps // 2))),
            (dq1, pl.BlockSpec((rows, local), within(steps // 2, steps))),
            (dk, narrow),
            (dv, narrow),
            (w3, once(3, width, local)),
            (a, here),
            (tok, here),
        ],
        [((n, width), F32, spec) for n, spec in zip(sizes, specs)]
        + [((2, width), F32, whole(2, width))],
        vmem=60,
        flops=6 * length * width * local,
    )


def gate_kernel(*refs):
    pass


def gate(after, *arrays):
    anywhere = pl.BlockSpec(memory_space=pltpu.HBM)
    n = len(after)
    return pl.pallas_call(
        gate_kernel,
        in_specs=[anywhere] * (n + len(arrays)),
        out_specs=[anywhere] * len(arrays),
        out_shape=[jax.ShapeDtypeStruct(x.shape, x.dtype) for x in arrays],
        input_output_aliases={n + i: i for i in range(len(arrays))},
        name="gate",
    )(*after, *arrays)


def tail_kernel(place, normed_t, ho0, ho1, cot, dq0, dq1, dk, dv, own0, own1, other0, other1):
    n = normed_t[...]
    half = dq0.shape[0]
    first = place[0] == 0

    def put(mine, x, own, other):
        @pl.when(mine)
        def _():
            own[...] = x

        @pl.when(jnp.logical_not(mine))
        def _():
            other[...] = x

    put(first, nn(n[:, :half], dq0[...]) + nn(n[:, half:], dq1[...]), own0, other0)
    put(first, nn(n, dk[...]), own1, other1)
    put(jnp.logical_not(first), nn(n, dv[...]), own0, other0)
    g = tn(ho0[...], cot[:half, :]) + tn(ho1[...], cot[half:, :])
    columns = g.shape[1] // 2
    g = jnp.concatenate([g[:, :columns], g[:, columns:]], axis=0)
    put(jnp.logical_not(first), g, own1, other1)


def tail(place, after, normed_t, ho0, ho1, cot, dq0, dq1, dk, dv):
    width, length = normed_t.shape
    local = dk.shape[1]
    half = length // 2
    assert 2 * local == width
    return launch(
        tail_kernel,
        "tail",
        (1,),
        (place,),
        after,
        [(normed_t, once(width, length))]
        + [(x, once(half, local)) for x in (ho0, ho1)]
        + [(cot, once(length, width))]
        + [(x, once(half, local)) for x in (dq0, dq1)]
        + [(x, once(length, local)) for x in (dk, dv)],
        [((width, local), F32, once(width, local))] * 4,
        vmem=36,
        flops=8 * length * width * local,
    )


def finish_kernel(*refs, cuts, last):
    refs, token = refs[:-1], refs[-1]
    token[...] = jnp.zeros_like(token)
    n = len(cuts) - 1
    wide, (mine, got), (row, out) = refs[: -2 * n - 2], (refs[-2 * n - 2 : -n - 2], refs[-n - 2 : -2]), refs[-2:]
    i = pl.program_id(0)
    x = wide[0][...].astype(F32)

    def one(total):
        if not last:
            out[...] = (x + total + row[...]).astype(BF16)
            return
        unit, inverse = norm_rows(x)
        d_unit = total * row[...]
        centre = jnp.mean(d_unit, axis=1, keepdims=True)
        slope = jnp.mean(d_unit * unit, axis=1, keepdims=True)
        out[...] = (
            wide[1][...].astype(F32) + inverse * (d_unit - centre - unit * slope)
        ).astype(BF16)

    for k in range(n):

        @pl.when(jnp.logical_and(i >= cuts[k], i < cuts[k + 1]))
        def _():
            one(mine[k][...] + got[k][...])


def finish(name, after, wide, mine, got, row, start=0, into=None, rows=128, vmem=16):
    length, width = wide[0].shape
    cuts, pieces = cut_specs([x.shape[0] for x in mine], rows, width)
    first = start // rows
    here = pl.BlockSpec((rows, width), lambda i: (first + i, 0))
    return launch(
        functools.partial(finish_kernel, cuts=cuts, last=len(wide) > 1),
        name,
        (cuts[-1],),
        (),
        after,
        [(x, here) for x in wide]
        + list(zip(mine, pieces))
        + list(zip(got, pieces))
        + [(row, whole(1, width))],
        [((length, width), BF16, here), TOKEN],
        vmem=vmem,
        into=into,
    )


def halve_kernel(place, a, b, c, d, keep, send):
    keep[...] = a[...] + b[...]
    send[...] = c[...] + d[...]


def halve(place, slot, after, mine, got):
    n, width = mine.shape
    h = n // 2
    rows = h // 2 if h * width > (256 << 10) else h
    steps = h // rows

    def bit(place):
        return 0 if slot is None else place[slot]

    keep = pl.BlockSpec((rows, width), lambda i, place: (bit(place) * steps + i, 0))
    send = pl.BlockSpec((rows, width), lambda i, place: ((1 - bit(place)) * steps + i, 0))
    here = pl.BlockSpec((rows, width), lambda i, _: (i, 0))
    return launch(
        halve_kernel,
        "halve",
        (steps,),
        (place,),
        after,
        [(mine, keep), (got, keep), (mine, send), (got, send)],
        [((h, width), F32, here)] * 2,
    )


def pack_kernel(a, b, c, d, *rest):
    small, out = rest[:-1], rest[-1]
    n, width = a.shape
    top = SMALL if small else 0
    out[top : top + n, :] = a[...] + b[...]
    out[top + n :, :] = c[...] + d[...]
    if small:
        rows = [
            x[i : i + 1, j : j + width]
            for x in small
            for i in range(x.shape[0])
            for j in range(0, x.shape[1], width)
        ]
        rows.append(jnp.zeros((SMALL - len(rows), width), F32))
        out[:top, :] = jnp.concatenate(rows, axis=0)


def pack(after, a, b, c, d, small=()):
    shape = (a.shape[0] + c.shape[0] + (SMALL if small else 0), a.shape[1])
    return launch(
        pack_kernel,
        "pack",
        (1,),
        (),
        after,
        [(x, whole(*x.shape)) for x in (a, b, c, d, *small)],
        [(shape, F32, whole(*shape))],
    )[0]


def plus_kernel(a, b, out):
    out[...] = a[...] + b[...]


def plus(after, a, b):
    return launch(
        plus_kernel,
        "plus",
        (1,),
        (),
        after,
        [(x, whole(*x.shape)) for x in (a, b)],
        [(a.shape, F32, whole(*a.shape))],
    )[0]


def part_kernel(a, b, first, second):
    n = first.shape[0]
    first[...] = a[:n, :] + b[:n, :]
    second[...] = a[n:, :] + b[n:, :]


def part(after, n, a, b):
    shapes = [(n, a.shape[1]), (a.shape[0] - n, a.shape[1])]
    return launch(
        part_kernel,
        "part",
        (1,),
        (),
        after,
        [(x, whole(*x.shape)) for x in (a, b)],
        [(shape, F32, whole(*shape)) for shape in shapes],
    )


def join_kernel(place, mine, got, out, *scratch, slot, top):
    sems = scratch[-1]
    h = mine.shape[0] - top
    bit = place[slot]
    copies = [
        pltpu.make_async_copy(
            mine.at[pl.ds(top, h)], out.at[pl.ds(pl.multiple_of(top + bit * h, 8), h)], sems.at[0]
        ),
        pltpu.make_async_copy(
            got.at[pl.ds(top, h)],
            out.at[pl.ds(pl.multiple_of(top + (1 - bit) * h, 8), h)],
            sems.at[1],
        ),
    ]
    if top:
        small = scratch[0]
        copies += [
            pltpu.make_async_copy(x.at[pl.ds(0, top)], small.at[i], sems.at[2 + i])
            for i, x in enumerate((mine, got))
        ]
    for copy in copies:
        copy.start()
    for copy in copies:
        copy.wait()
    if top:
        out[:top, :] = small[0] + small[1]


def join(place, slot, after, mine, got, top=0):
    n, width = mine.shape
    anywhere = pl.BlockSpec(memory_space=pltpu.HBM)
    rows = 2 * n - top
    return launch(
        functools.partial(join_kernel, slot=slot, top=top),
        "join",
        (1,),
        (place,),
        after,
        [(mine, anywhere), (got, anywhere)],
        [((rows, width), F32, once(rows, width))],
        ([pltpu.VMEM((2, top, width), F32)] if top else []) + [pltpu.SemaphoreType.DMA((4,))],
    )[0]


def assemble_kernel(place, *refs):
    arrays, (qkv, merge) = refs[:8], refs[8:]
    count = qkv.shape[1]
    j, t = pl.program_id(0), pl.program_id(1)
    core = place[0]
    for other in range(2):
        for p in range(2):
            bit = place[bit_slot(p, 0)] if other == 0 else place[NEAR + p]
            for half in range(2):
                x = arrays[4 * other + 2 * p + half]
                mine = (j == 2 * (core if other == 0 else 1 - core) + p) & (
                    t == (bit if half == 0 else 1 - bit)
                )

                @pl.when(mine & (j < 3))
                def _():
                    qkv[0] = x[x.shape[0] - count :, :]

                @pl.when(mine & (j == 3))
                def _():
                    merge[...] = x[x.shape[0] - count :, :]


def small_kernel(own0, own1, near0, near1, out):
    out[...] = (own0[...] + own1[...]) + (near0[...] + near1[...])


def small_sums(after, arrays):
    width = arrays[0].shape[1]
    top = pl.BlockSpec((SMALL, width), lambda i: (0, 0))
    return launch(
        small_kernel,
        "small_sums",
        (1,),
        (),
        after,
        [(x, top) for x in arrays],
        [((SMALL, width), F32, whole(SMALL, width))],
    )[0]


def assemble(place, after, arrays, width):
    local = arrays[0].shape[1]
    half = width // 2
    return launch(
        assemble_kernel,
        "assemble",
        (4, 2),
        (place,),
        after,
        [(x, once(*x.shape)) for x in arrays],
        [
            (
                (3, width, local),
                F32,
                pl.BlockSpec(
                    (1, half, local),
                    lambda j, t, _: (jnp.minimum(j, 2), jnp.where(j < 3, t, 1), 0),
                ),
            ),
            (
                (local, width),
                F32,
                pl.BlockSpec((local, half), lambda j, t, _: (0, jnp.where(j < 3, 0, t))),
            ),
        ],
        vmem=40,
    )


def spread_kernel(gathered, up, down, token, buf, in_sems, out_sems):
    token[...] = jnp.zeros_like(token)
    count, rows, width = gathered.shape
    piece = rows // 2
    half = count // 2
    slots = buf.shape[0]

    def outs(n):
        slot = n % slots
        return (
            pltpu.make_async_copy(
                buf.at[slot, pl.ds(0, piece)],
                down.at[n // half, pl.ds((n % half) * piece, piece)],
                out_sems.at[2 * slot],
            ),
            pltpu.make_async_copy(
                buf.at[slot, pl.ds(piece, piece)],
                up.at[pl.ds((n % half) * piece, piece), pl.ds((n // half) * width, width)],
                out_sems.at[2 * slot + 1],
            ),
        )

    def arrive(n):
        slot = n % slots
        return pltpu.make_async_copy(gathered.at[n], buf.at[slot], in_sems.at[slot])

    ahead = slots // 2
    for n in range(count + ahead):
        if n < count:
            if n >= slots:
                for copy in outs(n - slots):
                    copy.wait()
            arrive(n).start()
        if n >= ahead:
            arrive(n - ahead).wait()
            for copy in outs(n - ahead):
                copy.start()
    for n in range(count - slots, count):
        for copy in outs(n):
            copy.wait()


def spread(after, gathered, slots=16):
    count, rows, width = gathered.shape
    piece = rows // 2
    half = count // 2
    anywhere = pl.BlockSpec(memory_space=pltpu.HBM)
    return launch(
        spread_kernel,
        "spread",
        (1,),
        (),
        after,
        [(gathered, anywhere)],
        [
            ((half * piece, 2 * width), F32, anywhere),
            ((2, half * piece, width), F32, anywhere),
            TOKEN,
        ],
        [
            pltpu.VMEM((slots, rows, width), F32),
            pltpu.SemaphoreType.DMA((slots,)),
            pltpu.SemaphoreType.DMA((2 * slots,)),
        ],
        vmem=60,
    )


AXES = ("xlo", "z", "y", "core", "tensor")
RINGS = ("z", "y", "core")
DIRECTIONS = (("y", 0), ("z", 0), ("y", 1), ("z", 1))
SWAP = ((0, 1), (1, 0))


def partner(place, bit):
    return place ^ 1 if bit == 0 else 3 - place


def bit_at(place, bit):
    return int(place in (1, 2)) if bit == 0 else int(place >= 2)


def order_of(core, part):
    return [(core + 2 * part + step) % 4 for step in range(4)]


def spot_of(z, y, core, part):
    spot = 0
    for direction in order_of(core, part):
        axis, bit = DIRECTIONS[direction]
        spot = 2 * spot + bit_at(y if axis == "y" else z, bit)
    return spot


def step_pairs(part, step):
    pairs = []
    for z in range(4):
        for y in range(4):
            for core in range(2):
                axis, bit = DIRECTIONS[order_of(core, part)[step]]
                z2, y2 = (z, partner(y, bit)) if axis == "y" else (partner(z, bit), y)
                pairs.append(((z * 4 + y) * 2 + core, (z2 * 4 + y2) * 2 + core))
    return pairs


def place_table():
    rows = []
    for z in range(4):
        for y in range(4):
            for core in range(2):
                row = [core]
                for part in range(2):
                    for direction in order_of(core, part):
                        axis, bit = DIRECTIONS[direction]
                        row.append(bit_at(y if axis == "y" else z, bit))
                for half in (core, 1 - core):
                    row.append(half)
                    for part in range(2):
                        here = spot_of(z, y, half, part)
                        row += [
                            here ^ spot_of(z2, y2, half, part) for z2 in range(4) for y2 in range(4)
                        ]
                for part in range(2):
                    axis, bit = DIRECTIONS[order_of(1 - core, part)[0]]
                    row.append(bit_at(y if axis == "y" else z, bit))
                rows.append(row)
    return np.array(rows, np.int32)


OWN = 9
OTHER = OWN + 33
NEAR = OTHER + 33


def bit_slot(part, step):
    return 1 + 4 * part + step


def send_step(x, part, step):
    return lax.ppermute(x, RINGS, step_pairs(part, step))


def exchange(x, axis):
    return lax.ppermute(x, axis, SWAP)


def body(
    tokens,
    norm_gain,
    norm_shift,
    qkv_weight,
    merge_weight,
    up_weight,
    inner_shift,
    down_weight,
    outer_shift,
    cotangent,
):
    length, width = tokens.shape
    local = merge_weight.shape[0]
    hidden = up_weight.shape[1]
    place = lax.dynamic_index_in_dim(
        jnp.asarray(place_table()), lax.axis_index(RINGS), 0, keepdims=False
    )
    cos, sin = rotary_tables(length)
    w3 = qkv_weight.transpose(1, 0, 2)
    gain, shift, inner_row = norm_gain[None], norm_shift[None], inner_shift[None]

    normed, normed_t, q, k, v, dh, outer_g = project(
        tokens, gain, shift, w3, merge_weight, cotangent, cos, sin
    )
    out_f, dn_f, active, d_pre, inner_g = hidden_pass(
        (outer_g,), normed, cotangent, up_weight, inner_row, down_weight
    )

    (down_s,) = down_grad(place, OTHER, (inner_g,), active, cotangent)
    down_got = exchange(down_s, "core")
    (up_s,) = up_grad(place, OTHER, (down_s,), normed_t, d_pre)
    up_got = exchange(up_s, "core")

    ho0, dq0, dk_part, dv_part = attend(0, (up_s,), q, k, v, dh, cos, sin)
    mine = list(forward_part(0, (dq0,), ho0, merge_weight, out_f, (512,)))
    theirs = [exchange(mine[0], "tensor")]

    def flat(x):
        return x.reshape(-1, x.shape[-1])

    down_k, down_s = map(flat, down_grad(place, OWN, (mine[0],), active, cotangent, down_got))
    down_got = send_step(down_s, 0, 0)
    up_k, up_s = map(flat, up_grad(place, OWN, (down_s,), normed_t, d_pre, up_got))
    up_got = send_step(up_s, 1, 0)

    ho1, dq1, dk, dv = attend(1, (up_s,), q, k, v, dh, cos, sin, (dk_part, dv_part))
    mine += forward_part(1, (dq1,), ho1, merge_weight, out_f, (512,))
    theirs += [exchange(x, "tensor") for x in mine[1:]]

    own0, own1, tail_s0, tail_s1 = tail(
        place, (mine[1],), normed_t, ho0, ho1, cotangent, dq0, dq1, dk, dv
    )
    tail_got0 = exchange(tail_s0, "core")
    tail_got1 = exchange(tail_s1, "core")
    down_k, down_s = halve(place, None, (tail_s0, theirs[0]), down_k, down_got)
    down_got = send_step(down_s, 0, 1)
    up_k, up_s = halve(place, None, (down_s,), up_k, up_got)
    up_got = send_step(up_s, 1, 1)

    tail_k0, tail_s0 = halve(place, bit_slot(0, 0), (up_s,), own0, tail_got0)
    tail_got0 = send_step(tail_s0, 0, 0)
    tail_k1, tail_s1 = halve(place, bit_slot(1, 0), (tail_s0,), own1, tail_got1)
    tail_got1 = send_step(tail_s1, 1, 0)

    *back, sums = backward_pass(
        (tail_s1,), dq0, dq1, dk, dv, w3, dn_f, tokens, (512, 512)
    )

    down_k, down_s = halve(place, None, (sums,), down_k, down_got)
    down_got = send_step(down_s, 0, 2)
    up_k, up_s = halve(place, None, (down_s,), up_k, up_got)
    up_got = send_step(up_s, 1, 2)

    tail_k0, tail_s0 = halve(place, bit_slot(0, 1), (up_s,), tail_k0, tail_got0)
    tail_got0 = send_step(tail_s0, 0, 1)
    tail_k1, tail_s1 = halve(place, bit_slot(1, 1), (tail_s0,), tail_k1, tail_got1)
    tail_got1 = send_step(tail_s1, 1, 1)

    down_k, down_s = halve(place, None, (tail_s1,), down_k, down_got)
    down_got = send_step(down_s, 0, 3)
    up_k, up_s = halve(place, None, (down_s,), up_k, up_got)
    up_got = send_step(up_s, 1, 3)

    tail_k0, tail_s0 = halve(place, bit_slot(0, 2), (up_s, theirs[1]), tail_k0, tail_got0)
    tail_got0 = send_step(tail_s0, 0, 2)
    tail_k1, tail_s1 = halve(place, bit_slot(1, 2), (tail_s0,), tail_k1, tail_got1)
    tail_got1 = send_step(tail_s1, 1, 2)

    feed_x = pack((tail_s1,), down_k, down_got, up_k, up_got)
    feed_got = exchange(feed_x, "xlo")

    tail_k0, tail_s0 = halve(place, bit_slot(0, 3), (feed_x,), tail_k0, tail_got0)
    tail_got0 = send_step(tail_s0, 0, 3)
    tail_k1, tail_s1 = halve(place, bit_slot(1, 3), (tail_s0,), tail_k1, tail_got1)
    tail_got1 = send_step(tail_s1, 1, 3)

    feed_x = plus((tail_s1,), feed_x, feed_got)
    gathered = lax.all_gather(feed_x, ("core", "z", "y"))

    tail_x = pack(
        (feed_x,), tail_k0, tail_got0, tail_k1, tail_got1, (sums, outer_g, inner_g)
    )
    tail_got = exchange(tail_x, "xlo")

    tail0, tail1 = part((tail_x,), SMALL + tail_k0.shape[0], tail_x, tail_got)
    tail_got0 = send_step(tail0, 0, 3)
    tail_got1 = send_step(tail1, 1, 3)

    back = gate((tail1,), *back)
    back_got = [exchange(x, "tensor") for x in back]

    turn = back[0]
    for step in (3, 2, 1):
        tail0 = join(
            place, bit_slot(0, step), (turn, tail1), tail0, tail_got0, top=SMALL
        )
        tail_got0 = send_step(tail0, 0, step - 1)
        sink = (back_got[0],) if step == 1 else ()
        tail1 = join(place, bit_slot(1, step), (tail0, *sink), tail1, tail_got1)
        tail_got1 = send_step(tail1, 1, step - 1)
        turn = tail1
        if step == 2:
            block_out, turn = finish(
                "finish_out", (tail1,), (tokens,), mine, theirs, outer_shift[None]
            )

    up_out, down_out, turn = spread((tail1,), gathered)
    down_out = down_out.reshape(hidden, width)

    near0, near1 = exchange(tail0, "core"), exchange(tail1, "core")
    tail_got0, tail_got1 = gate((turn,), tail_got0, tail_got1)
    near_got0, near_got1 = exchange(tail_got0, "core"), exchange(tail_got1, "core")
    token_grad, turn = finish(
        "finish_grad", (tail_got0,), (tokens, cotangent), back[:1], back_got[:1], gain, vmem=60
    )
    own = (tail0, tail_got0, tail1, tail_got1)
    near = (near0, near_got0, near1, near_got1)
    small = small_sums((turn,), (*own[:2], *near[:2]))
    small_got = exchange(small, "tensor")
    qkv_out, merge_out = assemble(place, (small,), (*own, *near), width)
    token_grad, _ = finish(
        "finish_grad", (merge_out,), (tokens, cotangent), back[1:], back_got[1:], gain,
        start=length // 2, into=token_grad, vmem=60,
    )
    pair = (small[:4] + small_got[:4]).reshape(2, width)
    return (
        block_out,
        token_grad,
        pair[0],
        pair[1],
        qkv_out.transpose(1, 0, 2),
        merge_out,
        up_out,
        small[6 : 6 + hidden // local].reshape(hidden),
        down_out,
        small[4:6].reshape(width),
    )


def solution(mesh):
    dp = AXES[:4]
    finer = Mesh(mesh.devices.reshape(2, 4, 4, 2, 2), AXES)
    return jax.shard_map(
        body,
        mesh=finer,
        in_specs=(
            P(dp, None),
            P(),
            P(),
            P(None, None, "tensor"),
            P("tensor", None),
            P(None, "tensor"),
            P("tensor"),
            P("tensor", None),
            P(),
            P(dp, None),
        ),
        out_specs=(
            P(dp, None),
            P(dp, None),
            P(),
            P(),
            P(None, None, "tensor"),
            P("tensor", None),
            P(None, "tensor"),
            P("tensor"),
            P("tensor", None),
            P(),
        ),
        check_vma=False,
    )
```

```python
import functools

import jax
import jax.numpy as jnp
import numpy as np
from jax import lax
from jax.experimental import pallas as pl
from jax.experimental.pallas import tpu as pltpu
from jax.sharding import Mesh
from jax.sharding import PartitionSpec as P

F32 = jnp.float32
BF16 = jnp.bfloat16
HEAD = 64
ROT = 32
PAIR = 2 * HEAD
epsilon = 1e-05


def nn(a, b):
    return jnp.dot(a, b, preferred_element_type=F32)


def nt(a, b):
    return lax.dot_general(a, b, (((1,), (1,)), ((), ())), preferred_element_type=F32)


def tn(a, b):
    return lax.dot_general(a, b, (((0,), (0,)), ((), ())), preferred_element_type=F32)


def rotary_tables(length):
    half = ROT // 2
    rates = np.float32(10000.0) ** (-np.arange(half, dtype=np.float32) / np.float32(half))
    angles = np.arange(length, dtype=np.float32)[:, None] * rates[None, :].astype(np.float32)
    angles = np.repeat(angles, 2, axis=1)
    sign = np.where(np.arange(ROT) % 2 == 0, -1.0, 1.0)
    rest = np.ones((length, HEAD - ROT))
    cosine = np.concatenate([np.cos(angles), rest], axis=1)
    sine = np.concatenate([np.sin(angles) * sign, 0 * rest], axis=1)
    return tuple(jnp.asarray(np.tile(x, (1, 2)).astype(np.float32)) for x in (cosine, sine))


def swap_pairs(x):
    lane = lax.broadcasted_iota(jnp.int32, x.shape, 1)
    return jnp.where(lane % 2 == 0, pltpu.roll(x, PAIR - 1, 1), pltpu.roll(x, 1, 1))


def launch(kernel, name, grid, scalars, after, ins, outs, scratch=(), vmem=16, flops=0, into=None):
    into = into or {}
    after = (*after, *into.values())
    first, skipped = len(scalars), len(after)

    def without(*refs):
        kernel(*refs[:first], *refs[first + skipped :])

    got = pl.pallas_call(
        without,
        grid_spec=pltpu.PrefetchScalarGridSpec(
            num_scalar_prefetch=first,
            grid=grid,
            in_specs=[pl.BlockSpec(memory_space=pltpu.HBM)] * skipped + [spec for _, spec in ins],
            out_specs=[spec for _, _, spec in outs],
            scratch_shapes=list(scratch),
        ),
        out_shape=[jax.ShapeDtypeStruct(shape, dtype) for shape, dtype, _ in outs],
        compiler_params=pltpu.CompilerParams(vmem_limit_bytes=vmem << 20),
        input_output_aliases={
            first + skipped - len(into) + i: out for i, out in enumerate(into)
        },
        cost_estimate=pl.CostEstimate(
            flops=flops,
            bytes_accessed=sum(x.size * x.dtype.itemsize for x, _ in ins)
            + sum(int(np.prod(shape)) * jnp.dtype(dtype).itemsize for shape, dtype, _ in outs),
            transcendentals=0,
        ),
        name=name,
    )(*scalars, *after, *[array for array, _ in ins])
    return got


TOKEN = ((8, 128), F32, pl.BlockSpec((8, 128), lambda *_: (0, 0)))


def whole(*shape):
    return pl.BlockSpec(shape, lambda *_: (0,) * len(shape))


def once(*shape):
    return pl.BlockSpec(shape, lambda *_: (0,) * len(shape), pipeline_mode=pl.Buffered(1))


gelu_rate = float(np.sqrt(2 / np.pi))
SMALL = 16


def norm_rows(x):
    centred = x - jnp.mean(x, axis=1, keepdims=True)
    inverse = lax.rsqrt(jnp.mean(centred * centred, axis=1, keepdims=True) + epsilon)
    return centred * inverse, inverse


def project_kernel(
    tok, gain, shift, w_in, mw_in, cot, cos, sin, normed, normed_t, q, k, v, dh, outer, w, mw, sems
):
    first = pl.program_id(0) == 0
    copies = [pltpu.make_async_copy(mw_in, mw, sems.at[0])] + [
        pltpu.make_async_copy(w_in.at[which], w.at[which], sems.at[1 + which]) for which in range(3)
    ]

    @pl.when(first)
    def _():
        for copy in copies:
            copy.start()

    def body(arriving):
        unit, _ = norm_rows(tok[...].astype(F32))
        n = (unit * gain[...] + shift[...]).astype(BF16)
        normed[...] = n
        normed_t[...] = n.T
        total = jnp.sum(cot[...].astype(F32), axis=0, keepdims=True)
        outer[...] = total if arriving else outer[...] + total
        if arriving:
            copies[0].wait()
        dh[...] = nt(cot[...], mw[...]).astype(BF16)
        c = cos[...]
        s = sin[...]
        for which, ref in enumerate((q, k, v)):
            if arriving:
                copies[1 + which].wait()
            joined = nn(n, w[which])
            if which == 2:
                ref[...] = joined.astype(BF16)
                continue
            for p in range(joined.shape[1] // PAIR):
                block = joined[:, p * PAIR : (p + 1) * PAIR]
                turned = (block * c + swap_pairs(block) * s).astype(BF16)
                if which == 0:
                    turned = turned * jnp.asarray(HEAD**-0.5, BF16)
                ref[:, p * PAIR : (p + 1) * PAIR] = turned

    @pl.when(first)
    def _():
        body(True)

    @pl.when(jnp.logical_not(first))
    def _():
        body(False)


def project(tok, gain, shift, w3, mw, cot, cos, sin, rows=256):
    length, width = tok.shape
    local = mw.shape[0]

    def row_block(n):
        return pl.BlockSpec((rows, n), lambda i: (i, 0))

    def out(n):
        return ((length, n), BF16, row_block(n))

    return launch(
        project_kernel,
        "project",
        (length // rows,),
        (),
        (),
        [
            (tok, row_block(width)),
            (gain, whole(1, width)),
            (shift, whole(1, width)),
            (w3, pl.BlockSpec(memory_space=pltpu.HBM)),
            (mw, pl.BlockSpec(memory_space=pltpu.HBM)),
            (cot, row_block(width)),
            (cos, row_block(PAIR)),
            (sin, row_block(PAIR)),
        ],
        [out(width), ((width, length), BF16, pl.BlockSpec((width, rows), lambda i: (0, i)))]
        + [out(local)] * 4
        + [((1, width), F32, whole(1, width))],
        [
            pltpu.VMEM((3, width, local), BF16),
            pltpu.VMEM((local, width), BF16),
            pltpu.SemaphoreType.DMA((4,)),
        ],
        vmem=60,
        flops=8 * length * width * local,
    )


def hidden_kernel(normed, cot, up_in, shift, down_in, out, dn, act, dpre, ig, up, down, sems, *, cols):
    first = pl.program_id(0) == 0
    cuts = [slice(j, j + cols) for j in range(0, up.shape[1], cols)]
    copies = []
    for j, s in enumerate(cuts):
        copies.append(
            (
                pltpu.make_async_copy(up_in.at[:, s], up.at[:, s], sems.at[2 * j]),
                pltpu.make_async_copy(down_in.at[s, :], down.at[s, :], sems.at[2 * j + 1]),
            )
        )

    @pl.when(first)
    def _():
        for pair in copies:
            for copy in pair:
                copy.start()

    def body(arriving):
        n = normed[...]
        c = cot[...]
        sums = []
        for j, s in enumerate(cuts):
            if arriving:
                for copy in copies[j]:
                    copy.wait()
            v = nn(n, up[:, s]) + shift[:, s]
            da = nt(c, down[s, :])
            square = v * v
            t = jnp.tanh(gelu_rate * v * (1.0 + 0.044715 * square))
            h = 0.5 * (1.0 + t)
            act[:, s] = (v * h).astype(BF16)
            slope = h + (0.5 * gelu_rate) * v * (1.0 - t * t) * (1.0 + (3 * 0.044715) * square)
            d_pre = (da * slope).astype(BF16)
            dpre[:, s] = d_pre
            sums.append(jnp.sum(d_pre.astype(F32), axis=0, keepdims=True))
        sums = jnp.concatenate(sums, axis=1)
        ig[...] = sums if arriving else ig[...] + sums
        out[...] = nn(act[...], down[...])
        dn[...] = nt(dpre[...], up[...])

    @pl.when(first)
    def _():
        body(True)

    @pl.when(jnp.logical_not(first))
    def _():
        body(False)


def hidden_pass(after, normed, cot, up, shift, down, rows=256, cols=512):
    length, width = normed.shape
    hidden = up.shape[1]

    def here(n):
        return pl.BlockSpec((rows, n), lambda i: (i, 0))

    return launch(
        functools.partial(hidden_kernel, cols=cols),
        "hidden",
        (length // rows,),
        (),
        after,
        [
            (normed, here(width)),
            (cot, here(width)),
            (up, pl.BlockSpec(memory_space=pltpu.HBM)),
            (shift, whole(1, hidden)),
            (down, pl.BlockSpec(memory_space=pltpu.HBM)),
        ],
        [((length, width), F32, here(width))] * 2
        + [((length, hidden), BF16, here(hidden))] * 2
        + [((1, hidden), F32, whole(1, hidden))],
        [
            pltpu.VMEM((width, hidden), BF16),
            pltpu.VMEM((hidden, width), BF16),
            pltpu.SemaphoreType.DMA((2 * hidden // cols,)),
        ],
        vmem=60,
        flops=9 * length * width * hidden,
    )


def grad_kernel(place, lhs, rhs, *rest, base, product, own):
    if own:
        got, keep, send, buf, sems, land, land_sems = rest
    else:
        out, buf, sems = rest
    j = pl.program_id(0)
    size = buf.shape[1] // 8

    def arriving(n):
        return pltpu.make_async_copy(
            got.at[place[base + n]], land.at[pl.ds(n * size, size)], land_sems.at[n]
        )

    if own:

        @pl.when(j == 0)
        def _():
            for n in range(16):
                arriving(n).start()

    buf[j] = product(lhs[...], rhs[...])
    if own:

        @pl.when(j == 0)
        def _():
            for n in range(8):
                arriving(n).wait()

        @pl.when(j == 1)
        def _():
            for n in range(8, 16):
                arriving(n).wait()

        buf[j] += land[pl.ds(pl.multiple_of(j * 8 * size, size), 8 * size), :]

    for i in range(8):
        spot = place[base + j * 8 + i]
        block = buf.at[j, pl.ds(i * size, size)]
        sem = sems.at[j * 8 + i]
        if own:

            @pl.when(spot < 8)
            def _():
                pltpu.make_async_copy(block, keep.at[spot], sem).start()

            @pl.when(spot >= 8)
            def _():
                pltpu.make_async_copy(block, send.at[spot - 8], sem).start()

        else:
            pltpu.make_async_copy(block, out.at[spot], sem).start()

    @pl.when(j == 1)
    def _():
        for n in range(16):
            block = buf.at[n // 8, pl.ds((n % 8) * size, size)]
            pltpu.make_async_copy(block, (keep if own else out).at[0], sems.at[n]).wait()


def grad(place, base, spots, after, lhs, rhs, specs, product, got=None):
    width = 1024
    rows = 1024
    own = got is not None
    piece = rows // 16
    anywhere = pl.BlockSpec(memory_space=pltpu.HBM)
    scratch = [pltpu.VMEM((2, rows // 2, width), F32), pltpu.SemaphoreType.DMA((16,))]
    if own:
        scratch += [pltpu.VMEM((rows, width), F32), pltpu.SemaphoreType.DMA((16,))]
    outs = [((8 if own else 16, piece, width), F32, anywhere)] * (2 if own else 1)
    return launch(
        functools.partial(grad_kernel, base=spots, product=product, own=own),
        "grad",
        (2,),
        (place,),
        after,
        [(lhs, specs[0]), (rhs, specs[1])] + ([(got, anywhere)] if own else []),
        outs,
        scratch,
        vmem=24,
        flops=2 * rows * width * lhs.shape[0],
    )


def down_grad(place, base, after, active, cot, got=None):
    length, width = cot.shape
    block = pl.BlockSpec((length, 512), lambda j, place: (0, place[base] * 2 + j))
    return grad(
        place, base, base + 1, after, active, cot, (block, once(length, width)), tn, got
    )


def up_grad(place, base, after, normed_t, d_pre, got=None):
    width, length = normed_t.shape
    rows = pl.BlockSpec((512, length), lambda j, _: (j, 0))
    half = pl.BlockSpec(
        (length, 1024), lambda j, place: (0, place[base]), pipeline_mode=pl.Buffered(1)
    )
    return grad(place, base, base + 17, after, normed_t, d_pre, (rows, half), nn, got)


def attend_kernel(*refs, last, sub):
    if last:
        q, do, k, v, dk_in, dv_in, cos, sin, ho, dq, dk, dv, dk_sum, dv_sum = refs
    else:
        q, do, k, v, cos, sin, ho, dq, dk_sum, dv_sum = refs
    block = q.shape[0]
    seen = k.shape[0]
    low = lax.broadcasted_iota(jnp.int32, (sub, PAIR), 1) < HEAD
    zero = jnp.zeros((sub, PAIR), BF16)
    causal = lax.broadcasted_iota(jnp.int32, (sub, sub), 1) <= lax.broadcasted_iota(
        jnp.int32, (sub, sub), 0
    )
    for i in range(block // sub):
        before = seen - block + i * sub
        upto = before + sub
        rows = slice(i * sub, (i + 1) * sub)
        keys = k[0:upto, :]
        values = v[0:upto, :]
        heads = [
            [jnp.where(low, x[rows, :], zero), jnp.where(low, zero, x[rows, :])] for x in (q, do)
        ]
        scores = [nt(x, keys) for x in heads[0]]
        d_probs = [nt(x, values) for x in heads[1]]
        probs_low, d_scores = [], []
        for h in range(2):
            edge = jnp.where(causal, scores[h][:, before:], -1e30)
            if before:
                edge = jnp.concatenate([scores[h][:, :before], edge], axis=1)
            expo = jnp.exp(edge - jnp.max(edge, axis=1, keepdims=True))
            probs = expo * (1.0 / jnp.sum(expo, axis=1, keepdims=True))
            inner = jnp.sum(probs * d_probs[h], axis=1, keepdims=True)
            probs_low.append(probs.astype(BF16))
            d_scores.append((probs * (d_probs[h] - inner)).astype(BF16))
        mixed = [nn(x, values) for x in probs_low]
        ho[rows, :] = jnp.where(low, mixed[0], mixed[1]).astype(BF16)
        d_query = [nn(x, keys) for x in d_scores]
        d_query = jnp.where(low, d_query[0], d_query[1]) * HEAD**-0.5
        turn = slice(before, upto)
        dq[rows, :] = (
            d_query * cos[turn, :] - swap_pairs(d_query) * sin[turn, :]
        ).astype(BF16)
        for left, right, total in ((probs_low, heads[1], dv_sum), (d_scores, heads[0], dk_sum)):
            add = tn(left[0], right[0]) + tn(left[1], right[1])
            if i == 0:
                total[0:upto, :] = add
            else:
                total[0:before, :] += add[:before]
                total[before:upto, :] = add[before:]
    if last:
        before = seen - block
        dk_sum[0:before, :] += dk_in[...]
        dv_sum[0:before, :] += dv_in[...]
        for i in range(seen // block):
            rows = slice(i * block, (i + 1) * block)
            d_keys = dk_sum[rows, :]
            dk[rows, :] = (d_keys * cos[rows, :] - swap_pairs(d_keys) * sin[rows, :]).astype(BF16)
            dv[rows, :] = dv_sum[rows, :].astype(BF16)


def attend(part, after, q, k, v, do, cos, sin, carried=(), sub=256):
    length, local = q.shape
    half = length // 2
    seen = half * (part + 1)
    rows = pl.BlockSpec((half, PAIR), lambda p: (part, p))
    keys = pl.BlockSpec((seen, PAIR), lambda p: (0, p))
    table = pl.BlockSpec((seen, PAIR), lambda p: (0, 0))
    here = pl.BlockSpec((half, PAIR), lambda p: (0, p))
    outs = [((half, local), BF16, here)] * 2
    scratch = ()
    if part == 0:
        outs += [((half, local), F32, here)] * 2
    else:
        outs += [((length, local), BF16, keys)] * 2
        scratch = [pltpu.VMEM((length, PAIR), F32)] * 2
    return launch(
        functools.partial(attend_kernel, last=part == 1, sub=sub),
        "attend",
        (local // PAIR,),
        (),
        after,
        [(q, rows), (do, rows), (k, keys), (v, keys)]
        + [(x, here) for x in carried]
        + [(cos, table), (sin, table)],
        outs,
        scratch,
        flops=30 * half * seen * PAIR * local // PAIR,
    )


def forward_kernel(ho, mw, a, *pieces, cuts):
    i = pl.program_id(0)
    total = nn(ho[...], mw[...]) + a[...]
    for n, piece in enumerate(pieces):

        @pl.when(jnp.logical_and(i >= cuts[n], i < cuts[n + 1]))
        def _():
            piece[...] = total


def within(first, last):
    return lambda i, *_: (jnp.clip(i, first, last - 1) - first, 0)


def cut_specs(sizes, rows, width):
    cuts = [int(n) // rows for n in np.cumsum((0,) + tuple(sizes))]
    return cuts, [
        pl.BlockSpec((rows, width), within(cuts[k], cuts[k + 1])) for k in range(len(sizes))
    ]


def forward_part(part, after, ho, mw, a, sizes, rows=128):
    half, local = ho.shape
    width = mw.shape[1]
    steps = half // rows
    cuts, specs = cut_specs(sizes, rows, width)
    there = pl.BlockSpec((rows, width), lambda i: (part * steps + i, 0))
    return launch(
        functools.partial(forward_kernel, cuts=cuts),
        "forward",
        (steps,),
        (),
        after,
        [
            (ho, pl.BlockSpec((rows, local), lambda i: (i, 0))),
            (mw, once(local, width)),
            (a, there),
        ],
        [((n, width), F32, spec) for n, spec in zip(sizes, specs)],
        flops=2 * half * width * local,
    )


def backward_kernel(dq0, dq1, dk, dv, w, a, tok, *rest, cuts):
    pieces, sums = rest[:-1], rest[-1]
    i = pl.program_id(0)

    def one(dq):
        total = nt(dq[...], w[0]) + nt(dk[...], w[1]) + nt(dv[...], w[2]) + a[...]
        for n, piece in enumerate(pieces):

            @pl.when(jnp.logical_and(i >= cuts[n], i < cuts[n + 1]))
            def _():
                piece[...] = total

        unit, _ = norm_rows(tok[...].astype(F32))
        both = jnp.concatenate(
            [jnp.sum(total * unit, axis=0, keepdims=True), jnp.sum(total, axis=0, keepdims=True)],
            axis=0,
        )

        @pl.when(i == 0)
        def _():
            sums[...] = both

        @pl.when(i > 0)
        def _():
            sums[...] += both

    half = pl.num_programs(0) // 2

    @pl.when(i < half)
    def _():
        one(dq0)

    @pl.when(i >= half)
    def _():
        one(dq1)


def backward_pass(after, dq0, dq1, dk, dv, w3, a, tok, sizes, rows=256):
    length, local = dk.shape
    width = w3.shape[1]
    steps = length // rows
    cuts, specs = cut_specs(sizes, rows, width)
    here = pl.BlockSpec((rows, width), lambda i: (i, 0))
    narrow = pl.BlockSpec((rows, local), lambda i: (i, 0))
    return launch(
        functools.partial(backward_kernel, cuts=cuts),
        "backward",
        (steps,),
        (),
        after,
        [
            (dq0, pl.BlockSpec((rows, local), within(0, steps // 2))),
            (dq1, pl.BlockSpec((rows, local), within(steps // 2, steps))),
            (dk, narrow),
            (dv, narrow),
            (w3, once(3, width, local)),
            (a, here),
            (tok, here),
        ],
        [((n, width), F32, spec) for n, spec in zip(sizes, specs)]
        + [((2, width), F32, whole(2, width))],
        vmem=60,
        flops=6 * length * width * local,
    )


def gate_kernel(*refs):
    pass


def gate(after, *arrays):
    anywhere = pl.BlockSpec(memory_space=pltpu.HBM)
    n = len(after)
    return pl.pallas_call(
        gate_kernel,
        in_specs=[anywhere] * (n + len(arrays)),
        out_specs=[anywhere] * len(arrays),
        out_shape=[jax.ShapeDtypeStruct(x.shape, x.dtype) for x in arrays],
        input_output_aliases={n + i: i for i in range(len(arrays))},
        name="gate",
    )(*after, *arrays)


def tail_kernel(place, normed_t, ho0, ho1, cot, dq0, dq1, dk, dv, own0, own1, other0, other1):
    n = normed_t[...]
    half = dq0.shape[0]
    first = place[0] == 0

    def put(mine, x, own, other):
        @pl.when(mine)
        def _():
            own[...] = x

        @pl.when(jnp.logical_not(mine))
        def _():
            other[...] = x

    put(first, nn(n[:, :half], dq0[...]) + nn(n[:, half:], dq1[...]), own0, other0)
    put(first, nn(n, dk[...]), own1, other1)
    put(jnp.logical_not(first), nn(n, dv[...]), own0, other0)
    g = tn(ho0[...], cot[:half, :]) + tn(ho1[...], cot[half:, :])
    columns = g.shape[1] // 2
    g = jnp.concatenate([g[:, :columns], g[:, columns:]], axis=0)
    put(jnp.logical_not(first), g, own1, other1)


def tail(place, after, normed_t, ho0, ho1, cot, dq0, dq1, dk, dv):
    width, length = normed_t.shape
    local = dk.shape[1]
    half = length // 2
    assert 2 * local == width
    return launch(
        tail_kernel,
        "tail",
        (1,),
        (place,),
        after,
        [(normed_t, once(width, length))]
        + [(x, once(half, local)) for x in (ho0, ho1)]
        + [(cot, once(length, width))]
        + [(x, once(half, local)) for x in (dq0, dq1)]
        + [(x, once(length, local)) for x in (dk, dv)],
        [((width, local), F32, once(width, local))] * 4,
        vmem=36,
        flops=8 * length * width * local,
    )


def finish_kernel(*refs, cuts, last):
    refs, token = refs[:-1], refs[-1]
    token[...] = jnp.zeros_like(token)
    n = len(cuts) - 1
    wide, (mine, got), (row, out) = refs[: -2 * n - 2], (refs[-2 * n - 2 : -n - 2], refs[-n - 2 : -2]), refs[-2:]
    i = pl.program_id(0)
    x = wide[0][...].astype(F32)

    def one(total):
        if not last:
            out[...] = (x + total + row[...]).astype(BF16)
            return
        unit, inverse = norm_rows(x)
        d_unit = total * row[...]
        centre = jnp.mean(d_unit, axis=1, keepdims=True)
        slope = jnp.mean(d_unit * unit, axis=1, keepdims=True)
        out[...] = (
            wide[1][...].astype(F32) + inverse * (d_unit - centre - unit * slope)
        ).astype(BF16)

    for k in range(n):

        @pl.when(jnp.logical_and(i >= cuts[k], i < cuts[k + 1]))
        def _():
            one(mine[k][...] + got[k][...])


def finish(name, after, wide, mine, got, row, start=0, into=None, rows=128, vmem=16):
    length, width = wide[0].shape
    cuts, pieces = cut_specs([x.shape[0] for x in mine], rows, width)
    first = start // rows
    here = pl.BlockSpec((rows, width), lambda i: (first + i, 0))
    return launch(
        functools.partial(finish_kernel, cuts=cuts, last=len(wide) > 1),
        name,
        (cuts[-1],),
        (),
        after,
        [(x, here) for x in wide]
        + list(zip(mine, pieces))
        + list(zip(got, pieces))
        + [(row, whole(1, width))],
        [((length, width), BF16, here), TOKEN],
        vmem=vmem,
        into=into,
    )


def halve_kernel(place, a, b, c, d, keep, send):
    keep[...] = a[...] + b[...]
    send[...] = c[...] + d[...]


def halve(place, slot, after, mine, got):
    n, width = mine.shape
    h = n // 2
    rows = h // 2 if h * width > (256 << 10) else h
    steps = h // rows

    def bit(place):
        return 0 if slot is None else place[slot]

    keep = pl.BlockSpec((rows, width), lambda i, place: (bit(place) * steps + i, 0))
    send = pl.BlockSpec((rows, width), lambda i, place: ((1 - bit(place)) * steps + i, 0))
    here = pl.BlockSpec((rows, width), lambda i, _: (i, 0))
    return launch(
        halve_kernel,
        "halve",
        (steps,),
        (place,),
        after,
        [(mine, keep), (got, keep), (mine, send), (got, send)],
        [((h, width), F32, here)] * 2,
    )


def pack_kernel(a, b, c, d, *rest):
    small, out = rest[:-1], rest[-1]
    n, width = a.shape
    top = SMALL if small else 0
    out[top : top + n, :] = a[...] + b[...]
    out[top + n :, :] = c[...] + d[...]
    if small:
        rows = [
            x[i : i + 1, j : j + width]
            for x in small
            for i in range(x.shape[0])
            for j in range(0, x.shape[1], width)
        ]
        rows.append(jnp.zeros((SMALL - len(rows), width), F32))
        out[:top, :] = jnp.concatenate(rows, axis=0)


def pack(after, a, b, c, d, small=()):
    shape = (a.shape[0] + c.shape[0] + (SMALL if small else 0), a.shape[1])
    return launch(
        pack_kernel,
        "pack",
        (1,),
        (),
        after,
        [(x, whole(*x.shape)) for x in (a, b, c, d, *small)],
        [(shape, F32, whole(*shape))],
    )[0]


def plus_kernel(a, b, out):
    out[...] = a[...] + b[...]


def plus(after, a, b):
    return launch(
        plus_kernel,
        "plus",
        (1,),
        (),
        after,
        [(x, whole(*x.shape)) for x in (a, b)],
        [(a.shape, F32, whole(*a.shape))],
    )[0]


def part_kernel(a, b, first, second):
    n = first.shape[0]
    first[...] = a[:n, :] + b[:n, :]
    second[...] = a[n:, :] + b[n:, :]


def part(after, n, a, b):
    shapes = [(n, a.shape[1]), (a.shape[0] - n, a.shape[1])]
    return launch(
        part_kernel,
        "part",
        (1,),
        (),
        after,
        [(x, whole(*x.shape)) for x in (a, b)],
        [(shape, F32, whole(*shape)) for shape in shapes],
    )


def join_kernel(place, mine, got, out, *scratch, slot, top):
    sems = scratch[-1]
    h = mine.shape[0] - top
    bit = place[slot]
    copies = [
        pltpu.make_async_copy(
            mine.at[pl.ds(top, h)], out.at[pl.ds(pl.multiple_of(top + bit * h, 8), h)], sems.at[0]
        ),
        pltpu.make_async_copy(
            got.at[pl.ds(top, h)],
            out.at[pl.ds(pl.multiple_of(top + (1 - bit) * h, 8), h)],
            sems.at[1],
        ),
    ]
    if top:
        small = scratch[0]
        copies += [
            pltpu.make_async_copy(x.at[pl.ds(0, top)], small.at[i], sems.at[2 + i])
            for i, x in enumerate((mine, got))
        ]
    for copy in copies:
        copy.start()
    for copy in copies:
        copy.wait()
    if top:
        out[:top, :] = small[0] + small[1]


def join(place, slot, after, mine, got, top=0):
    n, width = mine.shape
    anywhere = pl.BlockSpec(memory_space=pltpu.HBM)
    rows = 2 * n - top
    return launch(
        functools.partial(join_kernel, slot=slot, top=top),
        "join",
        (1,),
        (place,),
        after,
        [(mine, anywhere), (got, anywhere)],
        [((rows, width), F32, once(rows, width))],
        ([pltpu.VMEM((2, top, width), F32)] if top else []) + [pltpu.SemaphoreType.DMA((4,))],
    )[0]


def place_kernel(place, *refs, pieces, rows):
    srcs, (qkv, merge, token, buf, in_sems, out_sems) = refs[: len(pieces)], refs[len(pieces) :]
    token[...] = jnp.zeros_like(token)
    arriving = [
        pltpu.make_async_copy(src.at[pl.ds(src.shape[0] - rows, rows)], buf.at[i], in_sems.at[i])
        for i, src in enumerate(srcs)
    ]
    for copy in arriving:
        copy.start()
    for i, (near, part, mine) in enumerate(pieces):
        j = 2 * (1 - place[0] if near else place[0]) + part
        bit = place[NEAR + part] if near else place[bit_slot(part, 0)]
        start = pl.multiple_of((bit if mine else 1 - bit) * rows, rows)
        arriving[i].wait()

        @pl.when(j < 3)
        def _():
            pltpu.make_async_copy(
                buf.at[i], qkv.at[jnp.minimum(j, 2), pl.ds(start, rows)], out_sems.at[i]
            ).start()

        @pl.when(j == 3)
        def _():
            pltpu.make_async_copy(
                buf.at[i], merge.at[:, pl.ds(start, rows)], out_sems.at[i]
            ).start()

    for i in range(len(pieces)):
        pltpu.make_async_copy(buf.at[i], qkv.at[0, pl.ds(0, rows)], out_sems.at[i]).wait()


def place_pieces(place, after, arrays, pieces, width, into=None):
    local = arrays[0].shape[1]
    rows = width // 2
    anywhere = pl.BlockSpec(memory_space=pltpu.HBM)
    return launch(
        functools.partial(place_kernel, pieces=pieces, rows=rows),
        "place",
        (1,),
        (place,),
        after,
        [(x, anywhere) for x in arrays],
        [((3, width, local), F32, anywhere), ((local, width), F32, anywhere), TOKEN],
        [
            pltpu.VMEM((len(arrays), rows, local), F32),
            pltpu.SemaphoreType.DMA((len(arrays),)),
            pltpu.SemaphoreType.DMA((len(arrays),)),
        ],
        into=into,
    )


def small_kernel(own0, own1, near0, near1, out):
    out[...] = (own0[...] + own1[...]) + (near0[...] + near1[...])


def small_sums(after, arrays):
    width = arrays[0].shape[1]
    top = pl.BlockSpec((SMALL, width), lambda i: (0, 0))
    return launch(
        small_kernel,
        "small_sums",
        (1,),
        (),
        after,
        [(x, top) for x in arrays],
        [((SMALL, width), F32, whole(SMALL, width))],
    )[0]


def spread_kernel(gathered, up, down, token, buf, in_sems, out_sems):
    token[...] = jnp.zeros_like(token)
    count, rows, width = gathered.shape
    piece = rows // 2
    half = count // 2
    slots = buf.shape[0]

    def outs(n):
        slot = n % slots
        return (
            pltpu.make_async_copy(
                buf.at[slot, pl.ds(0, piece)],
                down.at[n // half, pl.ds((n % half) * piece, piece)],
                out_sems.at[2 * slot],
            ),
            pltpu.make_async_copy(
                buf.at[slot, pl.ds(piece, piece)],
                up.at[pl.ds((n % half) * piece, piece), pl.ds((n // half) * width, width)],
                out_sems.at[2 * slot + 1],
            ),
        )

    def arrive(n):
        slot = n % slots
        return pltpu.make_async_copy(gathered.at[n], buf.at[slot], in_sems.at[slot])

    ahead = slots // 2
    for n in range(count + ahead):
        if n < count:
            if n >= slots:
                for copy in outs(n - slots):
                    copy.wait()
            arrive(n).start()
        if n >= ahead:
            arrive(n - ahead).wait()
            for copy in outs(n - ahead):
                copy.start()
    for n in range(count - slots, count):
        for copy in outs(n):
            copy.wait()


def spread(after, gathered, slots=16):
    count, rows, width = gathered.shape
    piece = rows // 2
    half = count // 2
    anywhere = pl.BlockSpec(memory_space=pltpu.HBM)
    return launch(
        spread_kernel,
        "spread",
        (1,),
        (),
        after,
        [(gathered, anywhere)],
        [
            ((half * piece, 2 * width), F32, anywhere),
            ((2, half * piece, width), F32, anywhere),
            TOKEN,
        ],
        [
            pltpu.VMEM((slots, rows, width), F32),
            pltpu.SemaphoreType.DMA((slots,)),
            pltpu.SemaphoreType.DMA((2 * slots,)),
        ],
        vmem=60,
    )


AXES = ("xlo", "z", "y", "core", "tensor")
RINGS = ("z", "y", "core")
DIRECTIONS = (("y", 0), ("z", 0), ("y", 1), ("z", 1))
SWAP = ((0, 1), (1, 0))


def partner(place, bit):
    return place ^ 1 if bit == 0 else 3 - place


def bit_at(place, bit):
    return int(place in (1, 2)) if bit == 0 else int(place >= 2)


def order_of(core, part):
    return [(core + 2 * part + step) % 4 for step in range(4)]


def spot_of(z, y, core, part):
    spot = 0
    for direction in order_of(core, part):
        axis, bit = DIRECTIONS[direction]
        spot = 2 * spot + bit_at(y if axis == "y" else z, bit)
    return spot


def step_pairs(part, step):
    pairs = []
    for z in range(4):
        for y in range(4):
            for core in range(2):
                axis, bit = DIRECTIONS[order_of(core, part)[step]]
                z2, y2 = (z, partner(y, bit)) if axis == "y" else (partner(z, bit), y)
                pairs.append(((z * 4 + y) * 2 + core, (z2 * 4 + y2) * 2 + core))
    return pairs


def place_table():
    rows = []
    for z in range(4):
        for y in range(4):
            for core in range(2):
                row = [core]
                for part in range(2):
                    for direction in order_of(core, part):
                        axis, bit = DIRECTIONS[direction]
                        row.append(bit_at(y if axis == "y" else z, bit))
                for half in (core, 1 - core):
                    row.append(half)
                    for part in range(2):
                        here = spot_of(z, y, half, part)
                        row += [
                            here ^ spot_of(z2, y2, half, part) for z2 in range(4) for y2 in range(4)
                        ]
                for part in range(2):
                    axis, bit = DIRECTIONS[order_of(1 - core, part)[0]]
                    row.append(bit_at(y if axis == "y" else z, bit))
                rows.append(row)
    return np.array(rows, np.int32)


OWN = 9
OTHER = OWN + 33
NEAR = OTHER + 33


def bit_slot(part, step):
    return 1 + 4 * part + step


def send_step(x, part, step):
    return lax.ppermute(x, RINGS, step_pairs(part, step))


def exchange(x, axis):
    return lax.ppermute(x, axis, SWAP)


def body(
    tokens,
    norm_gain,
    norm_shift,
    qkv_weight,
    merge_weight,
    up_weight,
    inner_shift,
    down_weight,
    outer_shift,
    cotangent,
):
    length, width = tokens.shape
    local = merge_weight.shape[0]
    hidden = up_weight.shape[1]
    place = lax.dynamic_index_in_dim(
        jnp.asarray(place_table()), lax.axis_index(RINGS), 0, keepdims=False
    )
    cos, sin = rotary_tables(length)
    w3 = qkv_weight.transpose(1, 0, 2)
    gain, shift, inner_row = norm_gain[None], norm_shift[None], inner_shift[None]

    normed, normed_t, q, k, v, dh, outer_g = project(
        tokens, gain, shift, w3, merge_weight, cotangent, cos, sin
    )
    out_f, dn_f, active, d_pre, inner_g = hidden_pass(
        (outer_g,), normed, cotangent, up_weight, inner_row, down_weight
    )

    (down_s,) = down_grad(place, OTHER, (inner_g,), active, cotangent)
    down_got = exchange(down_s, "core")
    (up_s,) = up_grad(place, OTHER, (down_s,), normed_t, d_pre)
    up_got = exchange(up_s, "core")

    ho0, dq0, dk_part, dv_part = attend(0, (up_s,), q, k, v, dh, cos, sin)
    mine = list(forward_part(0, (dq0,), ho0, merge_weight, out_f, (512,)))
    theirs = [exchange(mine[0], "tensor")]

    def flat(x):
        return x.reshape(-1, x.shape[-1])

    down_k, down_s = map(flat, down_grad(place, OWN, (mine[0],), active, cotangent, down_got))
    down_got = send_step(down_s, 0, 0)
    up_k, up_s = map(flat, up_grad(place, OWN, (down_s,), normed_t, d_pre, up_got))
    up_got = send_step(up_s, 1, 0)

    ho1, dq1, dk, dv = attend(1, (up_s,), q, k, v, dh, cos, sin, (dk_part, dv_part))
    mine += forward_part(1, (dq1,), ho1, merge_weight, out_f, (512,))
    theirs += [exchange(x, "tensor") for x in mine[1:]]

    own0, own1, tail_s0, tail_s1 = tail(
        place, (mine[1],), normed_t, ho0, ho1, cotangent, dq0, dq1, dk, dv
    )
    tail_got0 = exchange(tail_s0, "core")
    tail_got1 = exchange(tail_s1, "core")
    down_k, down_s = halve(place, None, (tail_s0, theirs[0]), down_k, down_got)
    down_got = send_step(down_s, 0, 1)
    up_k, up_s = halve(place, None, (down_s,), up_k, up_got)
    up_got = send_step(up_s, 1, 1)

    tail_k0, tail_s0 = halve(place, bit_slot(0, 0), (up_s,), own0, tail_got0)
    tail_got0 = send_step(tail_s0, 0, 0)
    tail_k1, tail_s1 = halve(place, bit_slot(1, 0), (tail_s0,), own1, tail_got1)
    tail_got1 = send_step(tail_s1, 1, 0)

    *back, sums = backward_pass(
        (tail_s1,), dq0, dq1, dk, dv, w3, dn_f, tokens, (512, 512)
    )

    down_k, down_s = halve(place, None, (sums,), down_k, down_got)
    down_got = send_step(down_s, 0, 2)
    up_k, up_s = halve(place, None, (down_s,), up_k, up_got)
    up_got = send_step(up_s, 1, 2)

    tail_k0, tail_s0 = halve(place, bit_slot(0, 1), (up_s,), tail_k0, tail_got0)
    tail_got0 = send_step(tail_s0, 0, 1)
    tail_k1, tail_s1 = halve(place, bit_slot(1, 1), (tail_s0,), tail_k1, tail_got1)
    tail_got1 = send_step(tail_s1, 1, 1)

    down_k, down_s = halve(place, None, (tail_s1,), down_k, down_got)
    down_got = send_step(down_s, 0, 3)
    up_k, up_s = halve(place, None, (down_s,), up_k, up_got)
    up_got = send_step(up_s, 1, 3)

    tail_k0, tail_s0 = halve(place, bit_slot(0, 2), (up_s, theirs[1]), tail_k0, tail_got0)
    tail_got0 = send_step(tail_s0, 0, 2)
    tail_k1, tail_s1 = halve(place, bit_slot(1, 2), (tail_s0,), tail_k1, tail_got1)
    tail_got1 = send_step(tail_s1, 1, 2)

    feed_x = pack((tail_s1,), down_k, down_got, up_k, up_got)
    feed_got = exchange(feed_x, "xlo")

    tail_k0, tail_s0 = halve(place, bit_slot(0, 3), (feed_x,), tail_k0, tail_got0)
    tail_got0 = send_step(tail_s0, 0, 3)
    tail_k1, tail_s1 = halve(place, bit_slot(1, 3), (tail_s0,), tail_k1, tail_got1)
    tail_got1 = send_step(tail_s1, 1, 3)

    feed_x = plus((tail_s1,), feed_x, feed_got)
    gathered = lax.all_gather(feed_x, ("core", "z", "y"))

    tail_x = pack(
        (feed_x,), tail_k0, tail_got0, tail_k1, tail_got1, (sums, outer_g, inner_g)
    )
    tail_got = exchange(tail_x, "xlo")

    tail0, tail1 = part((tail_x,), SMALL + tail_k0.shape[0], tail_x, tail_got)
    tail_got0 = send_step(tail0, 0, 3)
    tail_got1 = send_step(tail1, 1, 3)

    back = gate((tail1,), *back)
    back_got = [exchange(x, "tensor") for x in back]

    turn = back[0]
    for step in (3, 2, 1):
        tail0 = join(
            place, bit_slot(0, step), (turn, tail1), tail0, tail_got0, top=SMALL
        )
        tail_got0 = send_step(tail0, 0, step - 1)
        sink = (back_got[0],) if step == 1 else ()
        tail1 = join(place, bit_slot(1, step), (tail0, *sink), tail1, tail_got1)
        tail_got1 = send_step(tail1, 1, step - 1)
        turn = tail1
        if step == 2:
            block_out, turn = finish(
                "finish_out", (tail1,), (tokens,), mine, theirs, outer_shift[None]
            )

    token_grad, turn = finish(
        "finish_grad", (tail1,), (tokens, cotangent), back[:1], back_got[:1], gain, vmem=60
    )
    near0, near1 = exchange(tail0, "core"), exchange(tail1, "core")
    up_out, down_out, turn = spread((turn, near0, near1), gathered)
    down_out = down_out.reshape(hidden, width)
    tail_got0, tail_got1 = gate((turn,), tail_got0, tail_got1)
    near_got0, near_got1 = exchange(tail_got0, "core"), exchange(tail_got1, "core")
    kinds = [(near, part) for near in (False, True) for part in range(2)]
    qkv_out, merge_out, turn = place_pieces(
        place,
        (tail_got0,),
        (tail0, tail1, near0, near1),
        [(*kind, True) for kind in kinds],
        width,
    )
    small = small_sums((turn,), (tail0, tail_got0, near0, near_got0))
    small_got = exchange(small, "tensor")
    qkv_out, merge_out, turn = place_pieces(
        place,
        (small,),
        (tail_got0, tail_got1, near_got0, near_got1),
        [(*kind, False) for kind in kinds],
        width,
        into={0: qkv_out, 1: merge_out},
    )
    token_grad, _ = finish(
        "finish_grad", (turn,), (tokens, cotangent), back[1:], back_got[1:], gain,
        start=length // 2, into={0: token_grad}, vmem=60,
    )
    pair = (small[:4] + small_got[:4]).reshape(2, width)
    return (
        block_out,
        token_grad,
        pair[0],
        pair[1],
        qkv_out.transpose(1, 0, 2),
        merge_out,
        up_out,
        small[6 : 6 + hidden // local].reshape(hidden),
        down_out,
        small[4:6].reshape(width),
    )


def solution(mesh):
    dp = AXES[:4]
    finer = Mesh(mesh.devices.reshape(2, 4, 4, 2, 2), AXES)
    return jax.shard_map(
        body,
        mesh=finer,
        in_specs=(
            P(dp, None),
            P(),
            P(),
            P(None, None, "tensor"),
            P("tensor", None),
            P(None, "tensor"),
            P("tensor"),
            P("tensor", None),
            P(),
            P(dp, None),
        ),
        out_specs=(
            P(dp, None),
            P(dp, None),
            P(),
            P(),
            P(None, None, "tensor"),
            P("tensor", None),
            P(None, "tensor"),
            P("tensor"),
            P("tensor", None),
            P(),
        ),
        check_vma=False,
    )
```

```python
import functools

import jax
import jax.numpy as jnp
import numpy as np
from jax import lax
from jax.experimental import pallas as pl
from jax.experimental.pallas import tpu as pltpu
from jax.sharding import Mesh
from jax.sharding import PartitionSpec as P

F32 = jnp.float32
BF16 = jnp.bfloat16
HEAD = 64
ROT = 32
PAIR = 2 * HEAD
epsilon = 1e-05


def nn(a, b):
    return jnp.dot(a, b, preferred_element_type=F32)


def nt(a, b):
    return lax.dot_general(a, b, (((1,), (1,)), ((), ())), preferred_element_type=F32)


def tn(a, b):
    return lax.dot_general(a, b, (((0,), (0,)), ((), ())), preferred_element_type=F32)


def rotary_tables(length):
    half = ROT // 2
    rates = np.float32(10000.0) ** (-np.arange(half, dtype=np.float32) / np.float32(half))
    angles = np.arange(length, dtype=np.float32)[:, None] * rates[None, :].astype(np.float32)
    angles = np.repeat(angles, 2, axis=1)
    sign = np.where(np.arange(ROT) % 2 == 0, -1.0, 1.0)
    rest = np.ones((length, HEAD - ROT))
    cosine = np.concatenate([np.cos(angles), rest], axis=1)
    sine = np.concatenate([np.sin(angles) * sign, 0 * rest], axis=1)
    return tuple(jnp.asarray(np.tile(x, (1, 2)).astype(np.float32)) for x in (cosine, sine))


def swap_pairs(x):
    lane = lax.broadcasted_iota(jnp.int32, x.shape, 1)
    return jnp.where(lane % 2 == 0, pltpu.roll(x, PAIR - 1, 1), pltpu.roll(x, 1, 1))


def launch(kernel, name, grid, scalars, after, ins, outs, scratch=(), vmem=16, flops=0, into=None):
    into = into or {}
    after = (*after, *into.values())
    first, skipped = len(scalars), len(after)

    def without(*refs):
        kernel(*refs[:first], *refs[first + skipped :])

    got = pl.pallas_call(
        without,
        grid_spec=pltpu.PrefetchScalarGridSpec(
            num_scalar_prefetch=first,
            grid=grid,
            in_specs=[pl.BlockSpec(memory_space=pltpu.HBM)] * skipped + [spec for _, spec in ins],
            out_specs=[spec for _, _, spec in outs],
            scratch_shapes=list(scratch),
        ),
        out_shape=[jax.ShapeDtypeStruct(shape, dtype) for shape, dtype, _ in outs],
        compiler_params=pltpu.CompilerParams(vmem_limit_bytes=vmem << 20),
        input_output_aliases={
            first + skipped - len(into) + i: out for i, out in enumerate(into)
        },
        cost_estimate=pl.CostEstimate(
            flops=flops,
            bytes_accessed=sum(x.size * x.dtype.itemsize for x, _ in ins)
            + sum(int(np.prod(shape)) * jnp.dtype(dtype).itemsize for shape, dtype, _ in outs),
            transcendentals=0,
        ),
        name=name,
    )(*scalars, *after, *[array for array, _ in ins])
    return got


TOKEN = ((8, 128), F32, pl.BlockSpec((8, 128), lambda *_: (0, 0)))


def whole(*shape):
    return pl.BlockSpec(shape, lambda *_: (0,) * len(shape))


def once(*shape):
    return pl.BlockSpec(shape, lambda *_: (0,) * len(shape), pipeline_mode=pl.Buffered(1))


gelu_rate = float(np.sqrt(2 / np.pi))
SMALL = 16


def norm_rows(x):
    centred = x - jnp.mean(x, axis=1, keepdims=True)
    inverse = lax.rsqrt(jnp.mean(centred * centred, axis=1, keepdims=True) + epsilon)
    return centred * inverse, inverse


def project_kernel(
    tok, gain, shift, w_in, mw_in, cot, cos, sin, normed, normed_t, q, k, v, dh, outer, w, mw, sems
):
    first = pl.program_id(0) == 0
    copies = [pltpu.make_async_copy(mw_in, mw, sems.at[0])] + [
        pltpu.make_async_copy(w_in.at[which], w.at[which], sems.at[1 + which]) for which in range(3)
    ]

    @pl.when(first)
    def _():
        for copy in copies:
            copy.start()

    def body(arriving):
        unit, _ = norm_rows(tok[...].astype(F32))
        n = (unit * gain[...] + shift[...]).astype(BF16)
        normed[...] = n
        normed_t[...] = n.T
        total = jnp.sum(cot[...].astype(F32), axis=0, keepdims=True)
        outer[...] = total if arriving else outer[...] + total
        if arriving:
            copies[0].wait()
        dh[...] = nt(cot[...], mw[...]).astype(BF16)
        c = cos[...]
        s = sin[...]
        for which, ref in enumerate((q, k, v)):
            if arriving:
                copies[1 + which].wait()
            joined = nn(n, w[which])
            if which == 2:
                ref[...] = joined.astype(BF16)
                continue
            for p in range(joined.shape[1] // PAIR):
                block = joined[:, p * PAIR : (p + 1) * PAIR]
                turned = (block * c + swap_pairs(block) * s).astype(BF16)
                if which == 0:
                    turned = turned * jnp.asarray(HEAD**-0.5, BF16)
                ref[:, p * PAIR : (p + 1) * PAIR] = turned

    @pl.when(first)
    def _():
        body(True)

    @pl.when(jnp.logical_not(first))
    def _():
        body(False)


def project(tok, gain, shift, w3, mw, cot, cos, sin, rows=256):
    length, width = tok.shape
    local = mw.shape[0]

    def row_block(n):
        return pl.BlockSpec((rows, n), lambda i: (i, 0))

    def out(n):
        return ((length, n), BF16, row_block(n))

    return launch(
        project_kernel,
        "project",
        (length // rows,),
        (),
        (),
        [
            (tok, row_block(width)),
            (gain, whole(1, width)),
            (shift, whole(1, width)),
            (w3, pl.BlockSpec(memory_space=pltpu.HBM)),
            (mw, pl.BlockSpec(memory_space=pltpu.HBM)),
            (cot, row_block(width)),
            (cos, row_block(PAIR)),
            (sin, row_block(PAIR)),
        ],
        [out(width), ((width, length), BF16, pl.BlockSpec((width, rows), lambda i: (0, i)))]
        + [out(local)] * 4
        + [((1, width), F32, whole(1, width))],
        [
            pltpu.VMEM((3, width, local), BF16),
            pltpu.VMEM((local, width), BF16),
            pltpu.SemaphoreType.DMA((4,)),
        ],
        vmem=60,
        flops=8 * length * width * local,
    )


def hidden_kernel(normed, cot, up_in, shift, down_in, out, dn, act, dpre, ig, up, down, sems, *, cols):
    first = pl.program_id(0) == 0
    cuts = [slice(j, j + cols) for j in range(0, up.shape[1], cols)]
    copies = []
    for j, s in enumerate(cuts):
        copies.append(
            (
                pltpu.make_async_copy(up_in.at[:, s], up.at[:, s], sems.at[2 * j]),
                pltpu.make_async_copy(down_in.at[s, :], down.at[s, :], sems.at[2 * j + 1]),
            )
        )

    @pl.when(first)
    def _():
        for pair in copies:
            for copy in pair:
                copy.start()

    def body(arriving):
        n = normed[...]
        c = cot[...]
        sums = []
        for j, s in enumerate(cuts):
            if arriving:
                for copy in copies[j]:
                    copy.wait()
            v = nn(n, up[:, s]) + shift[:, s]
            da = nt(c, down[s, :])
            square = v * v
            t = jnp.tanh(gelu_rate * v * (1.0 + 0.044715 * square))
            h = 0.5 * (1.0 + t)
            act[:, s] = (v * h).astype(BF16)
            slope = h + (0.5 * gelu_rate) * v * (1.0 - t * t) * (1.0 + (3 * 0.044715) * square)
            d_pre = (da * slope).astype(BF16)
            dpre[:, s] = d_pre
            sums.append(jnp.sum(d_pre.astype(F32), axis=0, keepdims=True))
        sums = jnp.concatenate(sums, axis=1)
        ig[...] = sums if arriving else ig[...] + sums
        out[...] = nn(act[...], down[...])
        dn[...] = nt(dpre[...], up[...])

    @pl.when(first)
    def _():
        body(True)

    @pl.when(jnp.logical_not(first))
    def _():
        body(False)


def hidden_pass(after, normed, cot, up, shift, down, rows=256, cols=512):
    length, width = normed.shape
    hidden = up.shape[1]

    def here(n):
        return pl.BlockSpec((rows, n), lambda i: (i, 0))

    return launch(
        functools.partial(hidden_kernel, cols=cols),
        "hidden",
        (length // rows,),
        (),
        after,
        [
            (normed, here(width)),
            (cot, here(width)),
            (up, pl.BlockSpec(memory_space=pltpu.HBM)),
            (shift, whole(1, hidden)),
            (down, pl.BlockSpec(memory_space=pltpu.HBM)),
        ],
        [((length, width), F32, here(width))] * 2
        + [((length, hidden), BF16, here(hidden))] * 2
        + [((1, hidden), F32, whole(1, hidden))],
        [
            pltpu.VMEM((width, hidden), BF16),
            pltpu.VMEM((hidden, width), BF16),
            pltpu.SemaphoreType.DMA((2 * hidden // cols,)),
        ],
        vmem=60,
        flops=9 * length * width * hidden,
    )


def grad_kernel(place, lhs, rhs, *rest, base, product, own):
    if own:
        got, keep, send, buf, sems, land, land_sems = rest
    else:
        out, buf, sems = rest
    j = pl.program_id(0)
    size = buf.shape[1] // 8

    def arriving(n):
        return pltpu.make_async_copy(
            got.at[place[base + n]], land.at[pl.ds(n * size, size)], land_sems.at[n]
        )

    if own:

        @pl.when(j == 0)
        def _():
            for n in range(16):
                arriving(n).start()

    buf[j] = product(lhs[...], rhs[...])
    if own:

        @pl.when(j == 0)
        def _():
            for n in range(8):
                arriving(n).wait()

        @pl.when(j == 1)
        def _():
            for n in range(8, 16):
                arriving(n).wait()

        buf[j] += land[pl.ds(pl.multiple_of(j * 8 * size, size), 8 * size), :]

    for i in range(8):
        spot = place[base + j * 8 + i]
        block = buf.at[j, pl.ds(i * size, size)]
        sem = sems.at[j * 8 + i]
        if own:

            @pl.when(spot < 8)
            def _():
                pltpu.make_async_copy(block, keep.at[spot], sem).start()

            @pl.when(spot >= 8)
            def _():
                pltpu.make_async_copy(block, send.at[spot - 8], sem).start()

        else:
            pltpu.make_async_copy(block, out.at[spot], sem).start()

    @pl.when(j == 1)
    def _():
        for n in range(16):
            block = buf.at[n // 8, pl.ds((n % 8) * size, size)]
            pltpu.make_async_copy(block, (keep if own else out).at[0], sems.at[n]).wait()


def grad(place, base, spots, after, lhs, rhs, specs, product, got=None):
    width = 1024
    rows = 1024
    own = got is not None
    piece = rows // 16
    anywhere = pl.BlockSpec(memory_space=pltpu.HBM)
    scratch = [pltpu.VMEM((2, rows // 2, width), F32), pltpu.SemaphoreType.DMA((16,))]
    if own:
        scratch += [pltpu.VMEM((rows, width), F32), pltpu.SemaphoreType.DMA((16,))]
    outs = [((8 if own else 16, piece, width), F32, anywhere)] * (2 if own else 1)
    return launch(
        functools.partial(grad_kernel, base=spots, product=product, own=own),
        "grad",
        (2,),
        (place,),
        after,
        [(lhs, specs[0]), (rhs, specs[1])] + ([(got, anywhere)] if own else []),
        outs,
        scratch,
        vmem=24,
        flops=2 * rows * width * lhs.shape[0],
    )


def down_grad(place, base, after, active, cot, got=None):
    length, width = cot.shape
    block = pl.BlockSpec((length, 512), lambda j, place: (0, place[base] * 2 + j))
    return grad(
        place, base, base + 1, after, active, cot, (block, once(length, width)), tn, got
    )


def up_grad(place, base, after, normed_t, d_pre, got=None):
    width, length = normed_t.shape
    rows = pl.BlockSpec((512, length), lambda j, _: (j, 0))
    half = pl.BlockSpec(
        (length, 1024), lambda j, place: (0, place[base]), pipeline_mode=pl.Buffered(1)
    )
    return grad(place, base, base + 17, after, normed_t, d_pre, (rows, half), nn, got)


def attend_kernel(*refs, last, sub):
    if last:
        q, do, k, v, dk_in, dv_in, cos, sin, ho, dq, dk, dv, dk_sum, dv_sum = refs
    else:
        q, do, k, v, cos, sin, ho, dq, dk_sum, dv_sum = refs
    block = q.shape[0]
    seen = k.shape[0]
    low = lax.broadcasted_iota(jnp.int32, (sub, PAIR), 1) < HEAD
    zero = jnp.zeros((sub, PAIR), BF16)
    causal = lax.broadcasted_iota(jnp.int32, (sub, sub), 1) <= lax.broadcasted_iota(
        jnp.int32, (sub, sub), 0
    )
    for i in range(block // sub):
        before = seen - block + i * sub
        upto = before + sub
        rows = slice(i * sub, (i + 1) * sub)
        keys = k[0:upto, :]
        values = v[0:upto, :]
        heads = [
            [jnp.where(low, x[rows, :], zero), jnp.where(low, zero, x[rows, :])] for x in (q, do)
        ]
        scores = [nt(x, keys) for x in heads[0]]
        d_probs = [nt(x, values) for x in heads[1]]
        probs_low, d_scores = [], []
        for h in range(2):
            edge = jnp.where(causal, scores[h][:, before:], -1e30)
            if before:
                edge = jnp.concatenate([scores[h][:, :before], edge], axis=1)
            expo = jnp.exp(edge - jnp.max(edge, axis=1, keepdims=True))
            probs = expo * (1.0 / jnp.sum(expo, axis=1, keepdims=True))
            inner = jnp.sum(probs * d_probs[h], axis=1, keepdims=True)
            probs_low.append(probs.astype(BF16))
            d_scores.append((probs * (d_probs[h] - inner)).astype(BF16))
        mixed = [nn(x, values) for x in probs_low]
        ho[rows, :] = jnp.where(low, mixed[0], mixed[1]).astype(BF16)
        d_query = [nn(x, keys) for x in d_scores]
        d_query = jnp.where(low, d_query[0], d_query[1]) * HEAD**-0.5
        turn = slice(before, upto)
        dq[rows, :] = (
            d_query * cos[turn, :] - swap_pairs(d_query) * sin[turn, :]
        ).astype(BF16)
        for left, right, total in ((probs_low, heads[1], dv_sum), (d_scores, heads[0], dk_sum)):
            add = tn(left[0], right[0]) + tn(left[1], right[1])
            if i == 0:
                total[0:upto, :] = add
            else:
                total[0:before, :] += add[:before]
                total[before:upto, :] = add[before:]
    if last:
        before = seen - block
        dk_sum[0:before, :] += dk_in[...]
        dv_sum[0:before, :] += dv_in[...]
        for i in range(seen // block):
            rows = slice(i * block, (i + 1) * block)
            d_keys = dk_sum[rows, :]
            dk[rows, :] = (d_keys * cos[rows, :] - swap_pairs(d_keys) * sin[rows, :]).astype(BF16)
            dv[rows, :] = dv_sum[rows, :].astype(BF16)


def attend(part, after, q, k, v, do, cos, sin, carried=(), sub=256):
    length, local = q.shape
    half = length // 2
    seen = half * (part + 1)
    rows = pl.BlockSpec((half, PAIR), lambda p: (part, p))
    keys = pl.BlockSpec((seen, PAIR), lambda p: (0, p))
    table = pl.BlockSpec((seen, PAIR), lambda p: (0, 0))
    here = pl.BlockSpec((half, PAIR), lambda p: (0, p))
    outs = [((half, local), BF16, here)] * 2
    scratch = ()
    if part == 0:
        outs += [((half, local), F32, here)] * 2
    else:
        outs += [((length, local), BF16, keys)] * 2
        scratch = [pltpu.VMEM((length, PAIR), F32)] * 2
    return launch(
        functools.partial(attend_kernel, last=part == 1, sub=sub),
        "attend",
        (local // PAIR,),
        (),
        after,
        [(q, rows), (do, rows), (k, keys), (v, keys)]
        + [(x, here) for x in carried]
        + [(cos, table), (sin, table)],
        outs,
        scratch,
        flops=30 * half * seen * PAIR * local // PAIR,
    )


def forward_kernel(ho, mw, a, *pieces, cuts):
    i = pl.program_id(0)
    total = nn(ho[...], mw[...]) + a[...]
    for n, piece in enumerate(pieces):

        @pl.when(jnp.logical_and(i >= cuts[n], i < cuts[n + 1]))
        def _():
            piece[...] = total


def within(first, last):
    return lambda i, *_: (jnp.clip(i, first, last - 1) - first, 0)


def cut_specs(sizes, rows, width):
    cuts = [int(n) // rows for n in np.cumsum((0,) + tuple(sizes))]
    return cuts, [
        pl.BlockSpec((rows, width), within(cuts[k], cuts[k + 1])) for k in range(len(sizes))
    ]


def forward_part(part, after, ho, mw, a, sizes, rows=128):
    half, local = ho.shape
    width = mw.shape[1]
    steps = half // rows
    cuts, specs = cut_specs(sizes, rows, width)
    there = pl.BlockSpec((rows, width), lambda i: (part * steps + i, 0))
    return launch(
        functools.partial(forward_kernel, cuts=cuts),
        "forward",
        (steps,),
        (),
        after,
        [
            (ho, pl.BlockSpec((rows, local), lambda i: (i, 0))),
            (mw, once(local, width)),
            (a, there),
        ],
        [((n, width), F32, spec) for n, spec in zip(sizes, specs)],
        flops=2 * half * width * local,
    )


def backward_kernel(dq0, dq1, dk, dv, w, a, tok, *rest, spots):
    pieces, (sums, buf, sems) = rest[:-3], rest[-3:]
    i = pl.program_id(0)
    steps = len(spots)
    rows = buf.shape[1]
    slot = i % 2

    def leaving(step):
        return [
            pltpu.make_async_copy(
                buf.at[step % 2, pl.ds(half * rows // 2, rows // 2)],
                pieces[k].at[pl.ds(start, rows // 2)],
                sems.at[step % 2, half],
            )
            for half, (k, start) in enumerate(spots[step])
        ]

    for step in range(2, steps):

        @pl.when(i == step)
        def _():
            for copy in leaving(step - 2):
                copy.wait()

    def one(dq):
        total = nt(dq[...], w[0]) + nt(dk[...], w[1]) + nt(dv[...], w[2]) + a[...]
        buf[slot] = total
        unit, _ = norm_rows(tok[...].astype(F32))
        both = jnp.concatenate(
            [jnp.sum(total * unit, axis=0, keepdims=True), jnp.sum(total, axis=0, keepdims=True)],
            axis=0,
        )

        @pl.when(i == 0)
        def _():
            sums[...] = both

        @pl.when(i > 0)
        def _():
            sums[...] += both

    @pl.when(i < steps // 2)
    def _():
        one(dq0)

    @pl.when(i >= steps // 2)
    def _():
        one(dq1)

    for step in range(steps):

        @pl.when(i == step)
        def _():
            for copy in leaving(step):
                copy.start()

    @pl.when(i == steps - 1)
    def _():
        for step in (steps - 2, steps - 1):
            for copy in leaving(step):
                copy.wait()


def backward_pass(after, dq0, dq1, dk, dv, w3, a, tok, sizes, rows=256):
    length, local = dk.shape
    width = w3.shape[1]
    steps = length // rows
    spots = [(k, start) for k, n in enumerate(sizes) for start in range(0, n, rows // 2)]
    spots = [spots[2 * i : 2 * i + 2] for i in range(steps)]
    here = pl.BlockSpec((rows, width), lambda i: (i, 0))
    narrow = pl.BlockSpec((rows, local), lambda i: (i, 0))
    anywhere = pl.BlockSpec(memory_space=pltpu.HBM)
    return launch(
        functools.partial(backward_kernel, spots=spots),
        "backward",
        (steps,),
        (),
        after,
        [
            (dq0, pl.BlockSpec((rows, local), within(0, steps // 2))),
            (dq1, pl.BlockSpec((rows, local), within(steps // 2, steps))),
            (dk, narrow),
            (dv, narrow),
            (w3, once(3, width, local)),
            (a, here),
            (tok, here),
        ],
        [((n, width), F32, anywhere) for n in sizes] + [((2, width), F32, whole(2, width))],
        [pltpu.VMEM((2, rows, width), F32), pltpu.SemaphoreType.DMA((2, 2))],
        vmem=60,
        flops=6 * length * width * local,
    )


def gate_kernel(*refs):
    pass


def gate(after, *arrays):
    anywhere = pl.BlockSpec(memory_space=pltpu.HBM)
    n = len(after)
    return pl.pallas_call(
        gate_kernel,
        in_specs=[anywhere] * (n + len(arrays)),
        out_specs=[anywhere] * len(arrays),
        out_shape=[jax.ShapeDtypeStruct(x.shape, x.dtype) for x in arrays],
        input_output_aliases={n + i: i for i in range(len(arrays))},
        name="gate",
    )(*after, *arrays)


def tail_kernel(place, normed_t, ho0, ho1, cot, dq0, dq1, dk, dv, own0, own1, other0, other1):
    n = normed_t[...]
    half = dq0.shape[0]
    first = place[0] == 0

    def put(mine, x, own, other):
        @pl.when(mine)
        def _():
            own[...] = x

        @pl.when(jnp.logical_not(mine))
        def _():
            other[...] = x

    put(first, nn(n[:, :half], dq0[...]) + nn(n[:, half:], dq1[...]), own0, other0)
    put(first, nn(n, dk[...]), own1, other1)
    put(jnp.logical_not(first), nn(n, dv[...]), own0, other0)
    g = tn(ho0[...], cot[:half, :]) + tn(ho1[...], cot[half:, :])
    columns = g.shape[1] // 2
    g = jnp.concatenate([g[:, :columns], g[:, columns:]], axis=0)
    put(jnp.logical_not(first), g, own1, other1)


def tail(place, after, normed_t, ho0, ho1, cot, dq0, dq1, dk, dv):
    width, length = normed_t.shape
    local = dk.shape[1]
    half = length // 2
    assert 2 * local == width
    return launch(
        tail_kernel,
        "tail",
        (1,),
        (place,),
        after,
        [(normed_t, once(width, length))]
        + [(x, once(half, local)) for x in (ho0, ho1)]
        + [(cot, once(length, width))]
        + [(x, once(half, local)) for x in (dq0, dq1)]
        + [(x, once(length, local)) for x in (dk, dv)],
        [((width, local), F32, once(width, local))] * 4,
        vmem=36,
        flops=8 * length * width * local,
    )


def finish_kernel(*refs, cuts, last):
    refs, token = refs[:-1], refs[-1]
    token[...] = jnp.zeros_like(token)
    n = len(cuts) - 1
    wide, (mine, got), (row, out) = refs[: -2 * n - 2], (refs[-2 * n - 2 : -n - 2], refs[-n - 2 : -2]), refs[-2:]
    i = pl.program_id(0)
    x = wide[0][...].astype(F32)

    def one(total):
        if not last:
            out[...] = (x + total + row[...]).astype(BF16)
            return
        unit, inverse = norm_rows(x)
        d_unit = total * row[...]
        centre = jnp.mean(d_unit, axis=1, keepdims=True)
        slope = jnp.mean(d_unit * unit, axis=1, keepdims=True)
        out[...] = (
            wide[1][...].astype(F32) + inverse * (d_unit - centre - unit * slope)
        ).astype(BF16)

    for k in range(n):

        @pl.when(jnp.logical_and(i >= cuts[k], i < cuts[k + 1]))
        def _():
            one(mine[k][...] + got[k][...])


def finish(name, after, wide, mine, got, row, start=0, into=None, rows=128, vmem=16):
    length, width = wide[0].shape
    cuts, pieces = cut_specs([x.shape[0] for x in mine], rows, width)
    first = start // rows
    here = pl.BlockSpec((rows, width), lambda i: (first + i, 0))
    return launch(
        functools.partial(finish_kernel, cuts=cuts, last=len(wide) > 1),
        name,
        (cuts[-1],),
        (),
        after,
        [(x, here) for x in wide]
        + list(zip(mine, pieces))
        + list(zip(got, pieces))
        + [(row, whole(1, width))],
        [((length, width), BF16, here), TOKEN],
        vmem=vmem,
        into=into,
    )


def halve_kernel(place, a, b, c, d, keep, send):
    keep[...] = a[...] + b[...]
    send[...] = c[...] + d[...]


def halve(place, slot, after, mine, got):
    n, width = mine.shape
    h = n // 2
    rows = h // 2 if h * width > (256 << 10) else h
    steps = h // rows

    def bit(place):
        return 0 if slot is None else place[slot]

    keep = pl.BlockSpec((rows, width), lambda i, place: (bit(place) * steps + i, 0))
    send = pl.BlockSpec((rows, width), lambda i, place: ((1 - bit(place)) * steps + i, 0))
    here = pl.BlockSpec((rows, width), lambda i, _: (i, 0))
    return launch(
        halve_kernel,
        "halve",
        (steps,),
        (place,),
        after,
        [(mine, keep), (got, keep), (mine, send), (got, send)],
        [((h, width), F32, here)] * 2,
    )


def pack_kernel(a, b, c, d, *rest):
    small, out = rest[:-1], rest[-1]
    n, width = a.shape
    top = SMALL if small else 0
    out[top : top + n, :] = a[...] + b[...]
    out[top + n :, :] = c[...] + d[...]
    if small:
        rows = [
            x[i : i + 1, j : j + width]
            for x in small
            for i in range(x.shape[0])
            for j in range(0, x.shape[1], width)
        ]
        rows.append(jnp.zeros((SMALL - len(rows), width), F32))
        out[:top, :] = jnp.concatenate(rows, axis=0)


def pack(after, a, b, c, d, small=()):
    shape = (a.shape[0] + c.shape[0] + (SMALL if small else 0), a.shape[1])
    return launch(
        pack_kernel,
        "pack",
        (1,),
        (),
        after,
        [(x, whole(*x.shape)) for x in (a, b, c, d, *small)],
        [(shape, F32, whole(*shape))],
    )[0]


def plus_kernel(a, b, out):
    out[...] = a[...] + b[...]


def plus(after, a, b):
    return launch(
        plus_kernel,
        "plus",
        (1,),
        (),
        after,
        [(x, whole(*x.shape)) for x in (a, b)],
        [(a.shape, F32, whole(*a.shape))],
    )[0]


def part_kernel(a, b, first, second):
    n = first.shape[0]
    first[...] = a[:n, :] + b[:n, :]
    second[...] = a[n:, :] + b[n:, :]


def part(after, n, a, b):
    shapes = [(n, a.shape[1]), (a.shape[0] - n, a.shape[1])]
    return launch(
        part_kernel,
        "part",
        (1,),
        (),
        after,
        [(x, whole(*x.shape)) for x in (a, b)],
        [(shape, F32, whole(*shape)) for shape in shapes],
    )


def join_kernel(place, mine, got, out, *scratch, slot, top):
    sems = scratch[-1]
    h = mine.shape[0] - top
    bit = place[slot]
    copies = [
        pltpu.make_async_copy(
            mine.at[pl.ds(top, h)], out.at[pl.ds(pl.multiple_of(top + bit * h, 8), h)], sems.at[0]
        ),
        pltpu.make_async_copy(
            got.at[pl.ds(top, h)],
            out.at[pl.ds(pl.multiple_of(top + (1 - bit) * h, 8), h)],
            sems.at[1],
        ),
    ]
    if top:
        small = scratch[0]
        copies += [
            pltpu.make_async_copy(x.at[pl.ds(0, top)], small.at[i], sems.at[2 + i])
            for i, x in enumerate((mine, got))
        ]
    for copy in copies:
        copy.start()
    for copy in copies:
        copy.wait()
    if top:
        out[:top, :] = small[0] + small[1]


def join(place, slot, after, mine, got, top=0):
    n, width = mine.shape
    anywhere = pl.BlockSpec(memory_space=pltpu.HBM)
    rows = 2 * n - top
    return launch(
        functools.partial(join_kernel, slot=slot, top=top),
        "join",
        (1,),
        (place,),
        after,
        [(mine, anywhere), (got, anywhere)],
        [((rows, width), F32, once(rows, width))],
        ([pltpu.VMEM((2, top, width), F32)] if top else []) + [pltpu.SemaphoreType.DMA((4,))],
    )[0]


def place_kernel(place, *refs, pieces, rows):
    srcs, (qkv, merge, token, buf, in_sems, out_sems) = refs[: len(pieces)], refs[len(pieces) :]
    token[...] = jnp.zeros_like(token)
    arriving = [
        pltpu.make_async_copy(src.at[pl.ds(src.shape[0] - rows, rows)], buf.at[i], in_sems.at[i])
        for i, src in enumerate(srcs)
    ]
    for copy in arriving:
        copy.start()
    for i, (near, part, mine) in enumerate(pieces):
        j = 2 * (1 - place[0] if near else place[0]) + part
        bit = place[NEAR + part] if near else place[bit_slot(part, 0)]
        start = pl.multiple_of((bit if mine else 1 - bit) * rows, rows)
        arriving[i].wait()

        @pl.when(j < 3)
        def _():
            pltpu.make_async_copy(
                buf.at[i], qkv.at[jnp.minimum(j, 2), pl.ds(start, rows)], out_sems.at[i]
            ).start()

        @pl.when(j == 3)
        def _():
            pltpu.make_async_copy(
                buf.at[i], merge.at[:, pl.ds(start, rows)], out_sems.at[i]
            ).start()

    for i in range(len(pieces)):
        pltpu.make_async_copy(buf.at[i], qkv.at[0, pl.ds(0, rows)], out_sems.at[i]).wait()


def place_pieces(place, after, arrays, pieces, width, into=None):
    local = arrays[0].shape[1]
    rows = width // 2
    anywhere = pl.BlockSpec(memory_space=pltpu.HBM)
    return launch(
        functools.partial(place_kernel, pieces=pieces, rows=rows),
        "place",
        (1,),
        (place,),
        after,
        [(x, anywhere) for x in arrays],
        [((3, width, local), F32, anywhere), ((local, width), F32, anywhere), TOKEN],
        [
            pltpu.VMEM((len(arrays), rows, local), F32),
            pltpu.SemaphoreType.DMA((len(arrays),)),
            pltpu.SemaphoreType.DMA((len(arrays),)),
        ],
        into=into,
    )


def small_kernel(own0, own1, near0, near1, out):
    out[...] = (own0[...] + own1[...]) + (near0[...] + near1[...])


def small_sums(after, arrays):
    width = arrays[0].shape[1]
    top = pl.BlockSpec((SMALL, width), lambda i: (0, 0))
    return launch(
        small_kernel,
        "small_sums",
        (1,),
        (),
        after,
        [(x, top) for x in arrays],
        [((SMALL, width), F32, whole(SMALL, width))],
    )[0]


def spread_kernel(gathered, up, down, token, buf, in_sems, out_sems):
    token[...] = jnp.zeros_like(token)
    count, rows, width = gathered.shape
    piece = rows // 2
    half = count // 2
    slots = buf.shape[0]

    def outs(n):
        slot = n % slots
        return (
            pltpu.make_async_copy(
                buf.at[slot, pl.ds(0, piece)],
                down.at[n // half, pl.ds((n % half) * piece, piece)],
                out_sems.at[2 * slot],
            ),
            pltpu.make_async_copy(
                buf.at[slot, pl.ds(piece, piece)],
                up.at[pl.ds((n % half) * piece, piece), pl.ds((n // half) * width, width)],
                out_sems.at[2 * slot + 1],
            ),
        )

    def arrive(n):
        slot = n % slots
        return pltpu.make_async_copy(gathered.at[n], buf.at[slot], in_sems.at[slot])

    ahead = slots // 2
    for n in range(count + ahead):
        if n < count:
            if n >= slots:
                for copy in outs(n - slots):
                    copy.wait()
            arrive(n).start()
        if n >= ahead:
            arrive(n - ahead).wait()
            for copy in outs(n - ahead):
                copy.start()
    for n in range(count - slots, count):
        for copy in outs(n):
            copy.wait()


def spread(after, gathered, slots=16):
    count, rows, width = gathered.shape
    piece = rows // 2
    half = count // 2
    anywhere = pl.BlockSpec(memory_space=pltpu.HBM)
    return launch(
        spread_kernel,
        "spread",
        (1,),
        (),
        after,
        [(gathered, anywhere)],
        [
            ((half * piece, 2 * width), F32, anywhere),
            ((2, half * piece, width), F32, anywhere),
            TOKEN,
        ],
        [
            pltpu.VMEM((slots, rows, width), F32),
            pltpu.SemaphoreType.DMA((slots,)),
            pltpu.SemaphoreType.DMA((2 * slots,)),
        ],
        vmem=60,
    )


AXES = ("xlo", "z", "y", "core", "tensor")
RINGS = ("z", "y", "core")
DIRECTIONS = (("y", 0), ("z", 0), ("y", 1), ("z", 1))
SWAP = ((0, 1), (1, 0))


def partner(place, bit):
    return place ^ 1 if bit == 0 else 3 - place


def bit_at(place, bit):
    return int(place in (1, 2)) if bit == 0 else int(place >= 2)


def order_of(core, part):
    return [(core + 2 * part + step) % 4 for step in range(4)]


def spot_of(z, y, core, part):
    spot = 0
    for direction in order_of(core, part):
        axis, bit = DIRECTIONS[direction]
        spot = 2 * spot + bit_at(y if axis == "y" else z, bit)
    return spot


def step_pairs(part, step):
    pairs = []
    for z in range(4):
        for y in range(4):
            for core in range(2):
                axis, bit = DIRECTIONS[order_of(core, part)[step]]
                z2, y2 = (z, partner(y, bit)) if axis == "y" else (partner(z, bit), y)
                pairs.append(((z * 4 + y) * 2 + core, (z2 * 4 + y2) * 2 + core))
    return pairs


def place_table():
    rows = []
    for z in range(4):
        for y in range(4):
            for core in range(2):
                row = [core]
                for part in range(2):
                    for direction in order_of(core, part):
                        axis, bit = DIRECTIONS[direction]
                        row.append(bit_at(y if axis == "y" else z, bit))
                for half in (core, 1 - core):
                    row.append(half)
                    for part in range(2):
                        here = spot_of(z, y, half, part)
                        row += [
                            here ^ spot_of(z2, y2, half, part) for z2 in range(4) for y2 in range(4)
                        ]
                for part in range(2):
                    axis, bit = DIRECTIONS[order_of(1 - core, part)[0]]
                    row.append(bit_at(y if axis == "y" else z, bit))
                rows.append(row)
    return np.array(rows, np.int32)


OWN = 9
OTHER = OWN + 33
NEAR = OTHER + 33


def bit_slot(part, step):
    return 1 + 4 * part + step


def send_step(x, part, step):
    return lax.ppermute(x, RINGS, step_pairs(part, step))


def exchange(x, axis):
    return lax.ppermute(x, axis, SWAP)


def body(
    tokens,
    norm_gain,
    norm_shift,
    qkv_weight,
    merge_weight,
    up_weight,
    inner_shift,
    down_weight,
    outer_shift,
    cotangent,
):
    length, width = tokens.shape
    local = merge_weight.shape[0]
    hidden = up_weight.shape[1]
    place = lax.dynamic_index_in_dim(
        jnp.asarray(place_table()), lax.axis_index(RINGS), 0, keepdims=False
    )
    cos, sin = rotary_tables(length)
    w3 = qkv_weight.transpose(1, 0, 2)
    gain, shift, inner_row = norm_gain[None], norm_shift[None], inner_shift[None]

    normed, normed_t, q, k, v, dh, outer_g = project(
        tokens, gain, shift, w3, merge_weight, cotangent, cos, sin
    )
    out_f, dn_f, active, d_pre, inner_g = hidden_pass(
        (outer_g,), normed, cotangent, up_weight, inner_row, down_weight
    )

    (down_s,) = down_grad(place, OTHER, (inner_g,), active, cotangent)
    down_got = exchange(down_s, "core")
    (up_s,) = up_grad(place, OTHER, (down_s,), normed_t, d_pre)
    up_got = exchange(up_s, "core")

    ho0, dq0, dk_part, dv_part = attend(0, (up_s,), q, k, v, dh, cos, sin)
    mine = list(forward_part(0, (dq0,), ho0, merge_weight, out_f, (512,)))
    theirs = [exchange(mine[0], "tensor")]

    def flat(x):
        return x.reshape(-1, x.shape[-1])

    down_k, down_s = map(flat, down_grad(place, OWN, (mine[0],), active, cotangent, down_got))
    down_got = send_step(down_s, 0, 0)
    up_k, up_s = map(flat, up_grad(place, OWN, (down_s,), normed_t, d_pre, up_got))
    up_got = send_step(up_s, 1, 0)

    ho1, dq1, dk, dv = attend(1, (up_s,), q, k, v, dh, cos, sin, (dk_part, dv_part))
    mine += forward_part(1, (dq1,), ho1, merge_weight, out_f, (512,))
    theirs += [exchange(x, "tensor") for x in mine[1:]]

    own0, own1, tail_s0, tail_s1 = tail(
        place, (mine[1],), normed_t, ho0, ho1, cotangent, dq0, dq1, dk, dv
    )
    tail_got0 = exchange(tail_s0, "core")
    tail_got1 = exchange(tail_s1, "core")
    down_k, down_s = halve(place, None, (tail_s0, theirs[0]), down_k, down_got)
    down_got = send_step(down_s, 0, 1)
    up_k, up_s = halve(place, None, (down_s,), up_k, up_got)
    up_got = send_step(up_s, 1, 1)

    tail_k0, tail_s0 = halve(place, bit_slot(0, 0), (up_s,), own0, tail_got0)
    tail_got0 = send_step(tail_s0, 0, 0)
    tail_k1, tail_s1 = halve(place, bit_slot(1, 0), (tail_s0,), own1, tail_got1)
    tail_got1 = send_step(tail_s1, 1, 0)

    *back, sums = backward_pass(
        (tail_s1,), dq0, dq1, dk, dv, w3, dn_f, tokens, (128, 256, 512, 128)
    )

    down_k, down_s = halve(place, None, (sums,), down_k, down_got)
    down_got = send_step(down_s, 0, 2)
    up_k, up_s = halve(place, None, (down_s,), up_k, up_got)
    up_got = send_step(up_s, 1, 2)

    tail_k0, tail_s0 = halve(place, bit_slot(0, 1), (up_s,), tail_k0, tail_got0)
    tail_got0 = send_step(tail_s0, 0, 1)
    tail_k1, tail_s1 = halve(place, bit_slot(1, 1), (tail_s0,), tail_k1, tail_got1)
    tail_got1 = send_step(tail_s1, 1, 1)

    down_k, down_s = halve(place, None, (tail_s1,), down_k, down_got)
    down_got = send_step(down_s, 0, 3)
    up_k, up_s = halve(place, None, (down_s,), up_k, up_got)
    up_got = send_step(up_s, 1, 3)

    tail_k0, tail_s0 = halve(place, bit_slot(0, 2), (up_s, theirs[1]), tail_k0, tail_got0)
    tail_got0 = send_step(tail_s0, 0, 2)
    tail_k1, tail_s1 = halve(place, bit_slot(1, 2), (tail_s0,), tail_k1, tail_got1)
    tail_got1 = send_step(tail_s1, 1, 2)

    feed_x = pack((tail_s1,), down_k, down_got, up_k, up_got)
    feed_got = exchange(feed_x, "xlo")
    back[0] = gate((feed_x,), back[0])[0]
    back_got = [exchange(back[0], "tensor")]

    tail_k0, tail_s0 = halve(place, bit_slot(0, 3), (feed_x,), tail_k0, tail_got0)
    tail_got0 = send_step(tail_s0, 0, 3)
    tail_k1, tail_s1 = halve(place, bit_slot(1, 3), (tail_s0,), tail_k1, tail_got1)
    tail_got1 = send_step(tail_s1, 1, 3)

    feed_x = plus((tail_s1,), feed_x, feed_got)
    gathered = lax.all_gather(feed_x, ("core", "z", "y"))

    tail_x = pack(
        (feed_x,), tail_k0, tail_got0, tail_k1, tail_got1, (sums, outer_g, inner_g)
    )
    tail_got = exchange(tail_x, "xlo")

    tail0, tail1 = part((tail_x, back_got[0]), SMALL + tail_k0.shape[0], tail_x, tail_got)
    tail_got0 = send_step(tail0, 0, 3)
    tail_got1 = send_step(tail1, 1, 3)

    back[1:] = gate((tail1,), *back[1:])
    back_got += [exchange(x, "tensor") for x in back[1:]]

    turn = back[1]
    for step in (3, 2, 1):
        tail0 = join(
            place, bit_slot(0, step), (turn, tail1), tail0, tail_got0, top=SMALL
        )
        tail_got0 = send_step(tail0, 0, step - 1)
        sink = (back_got[1],) if step == 2 else ()
        tail1 = join(place, bit_slot(1, step), (tail0, *sink), tail1, tail_got1)
        tail_got1 = send_step(tail1, 1, step - 1)
        turn = tail1
        if step == 2:
            block_out, turn = finish(
                "finish_out", (tail1,), (tokens,), mine, theirs, outer_shift[None]
            )

    token_grad, turn = finish(
        "finish_grad", (tail1,), (tokens, cotangent), back[:2], back_got[:2], gain, vmem=60
    )
    near0, near1 = exchange(tail0, "core"), exchange(tail1, "core")
    up_out, down_out, turn = spread((turn, near0, near1), gathered)
    down_out = down_out.reshape(hidden, width)
    tail_got0, tail_got1 = gate((turn, back_got[2]), tail_got0, tail_got1)
    near_got0, near_got1 = exchange(tail_got0, "core"), exchange(tail_got1, "core")
    kinds = [(near, part) for near in (False, True) for part in range(2)]
    qkv_out, merge_out, turn = place_pieces(
        place,
        (tail_got0,),
        (tail0, tail1, near0, near1),
        [(*kind, True) for kind in kinds],
        width,
    )
    small = small_sums((turn,), (tail0, tail_got0, near0, near_got0))
    small_got = exchange(small, "tensor")
    qkv_out, merge_out, turn = place_pieces(
        place,
        (small,),
        (tail_got0, tail_got1, near_got0, near_got1),
        [(*kind, False) for kind in kinds],
        width,
        into={0: qkv_out, 1: merge_out},
    )
    for k, start in ((2, 384), (3, 896)):
        token_grad, turn = finish(
            "finish_grad", (turn,), (tokens, cotangent), back[k : k + 1], back_got[k : k + 1],
            gain, start=start, into={0: token_grad}, vmem=60,
        )
    pair = (small[:4] + small_got[:4]).reshape(2, width)
    return (
        block_out,
        token_grad,
        pair[0],
        pair[1],
        qkv_out.transpose(1, 0, 2),
        merge_out,
        up_out,
        small[6 : 6 + hidden // local].reshape(hidden),
        down_out,
        small[4:6].reshape(width),
    )


def solution(mesh):
    dp = AXES[:4]
    finer = Mesh(mesh.devices.reshape(2, 4, 4, 2, 2), AXES)
    return jax.shard_map(
        body,
        mesh=finer,
        in_specs=(
            P(dp, None),
            P(),
            P(),
            P(None, None, "tensor"),
            P("tensor", None),
            P(None, "tensor"),
            P("tensor"),
            P("tensor", None),
            P(),
            P(dp, None),
        ),
        out_specs=(
            P(dp, None),
            P(dp, None),
            P(),
            P(),
            P(None, None, "tensor"),
            P("tensor", None),
            P(None, "tensor"),
            P("tensor"),
            P("tensor", None),
            P(),
        ),
        check_vma=False,
    )
```

```python
import functools

import jax
import jax.numpy as jnp
import numpy as np
from jax import lax
from jax.experimental import pallas as pl
from jax.experimental.pallas import tpu as pltpu
from jax.sharding import Mesh
from jax.sharding import PartitionSpec as P

F32 = jnp.float32
BF16 = jnp.bfloat16
HEAD = 64
ROT = 32
PAIR = 2 * HEAD
epsilon = 1e-05


def nn(a, b):
    return jnp.dot(a, b, preferred_element_type=F32)


def nt(a, b):
    return lax.dot_general(a, b, (((1,), (1,)), ((), ())), preferred_element_type=F32)


def tn(a, b):
    return lax.dot_general(a, b, (((0,), (0,)), ((), ())), preferred_element_type=F32)


def rotary_tables(length):
    half = ROT // 2
    rates = np.float32(10000.0) ** (-np.arange(half, dtype=np.float32) / np.float32(half))
    angles = np.arange(length, dtype=np.float32)[:, None] * rates[None, :].astype(np.float32)
    angles = np.repeat(angles, 2, axis=1)
    sign = np.where(np.arange(ROT) % 2 == 0, -1.0, 1.0)
    rest = np.ones((length, HEAD - ROT))
    cosine = np.concatenate([np.cos(angles), rest], axis=1)
    sine = np.concatenate([np.sin(angles) * sign, 0 * rest], axis=1)
    return tuple(jnp.asarray(np.tile(x, (1, 2)).astype(np.float32)) for x in (cosine, sine))


def swap_pairs(x):
    lane = lax.broadcasted_iota(jnp.int32, x.shape, 1)
    return jnp.where(lane % 2 == 0, pltpu.roll(x, PAIR - 1, 1), pltpu.roll(x, 1, 1))


def launch(kernel, name, grid, scalars, after, ins, outs, scratch=(), vmem=16, flops=0, into=None):
    into = into or {}
    after = (*after, *into.values())
    first, skipped = len(scalars), len(after)

    def without(*refs):
        kernel(*refs[:first], *refs[first + skipped :])

    got = pl.pallas_call(
        without,
        grid_spec=pltpu.PrefetchScalarGridSpec(
            num_scalar_prefetch=first,
            grid=grid,
            in_specs=[pl.BlockSpec(memory_space=pltpu.HBM)] * skipped + [spec for _, spec in ins],
            out_specs=[spec for _, _, spec in outs],
            scratch_shapes=list(scratch),
        ),
        out_shape=[jax.ShapeDtypeStruct(shape, dtype) for shape, dtype, _ in outs],
        compiler_params=pltpu.CompilerParams(vmem_limit_bytes=vmem << 20),
        input_output_aliases={
            first + skipped - len(into) + i: out for i, out in enumerate(into)
        },
        cost_estimate=pl.CostEstimate(
            flops=flops,
            bytes_accessed=sum(x.size * x.dtype.itemsize for x, _ in ins)
            + sum(int(np.prod(shape)) * jnp.dtype(dtype).itemsize for shape, dtype, _ in outs),
            transcendentals=0,
        ),
        name=name,
    )(*scalars, *after, *[array for array, _ in ins])
    return got


TOKEN = ((8, 128), F32, pl.BlockSpec((8, 128), lambda *_: (0, 0)))


def whole(*shape):
    return pl.BlockSpec(shape, lambda *_: (0,) * len(shape))


def once(*shape):
    return pl.BlockSpec(shape, lambda *_: (0,) * len(shape), pipeline_mode=pl.Buffered(1))


gelu_rate = float(np.sqrt(2 / np.pi))
SMALL = 16


def norm_rows(x):
    centred = x - jnp.mean(x, axis=1, keepdims=True)
    inverse = lax.rsqrt(jnp.mean(centred * centred, axis=1, keepdims=True) + epsilon)
    return centred * inverse, inverse


def project_kernel(
    tok, gain, shift, w_in, mw_in, cot, cos, sin, normed, normed_t, q, k, v, dh, outer, w, mw, sems
):
    first = pl.program_id(0) == 0
    copies = [pltpu.make_async_copy(mw_in, mw, sems.at[0])] + [
        pltpu.make_async_copy(w_in.at[which], w.at[which], sems.at[1 + which]) for which in range(3)
    ]

    @pl.when(first)
    def _():
        for copy in copies:
            copy.start()

    def body(arriving):
        unit, _ = norm_rows(tok[...].astype(F32))
        n = (unit * gain[...] + shift[...]).astype(BF16)
        normed[...] = n
        normed_t[...] = n.T
        total = jnp.sum(cot[...].astype(F32), axis=0, keepdims=True)
        outer[...] = total if arriving else outer[...] + total
        if arriving:
            copies[0].wait()
        dh[...] = nt(cot[...], mw[...]).astype(BF16)
        c = cos[...]
        s = sin[...]
        for which, ref in enumerate((q, k, v)):
            if arriving:
                copies[1 + which].wait()
            joined = nn(n, w[which])
            if which == 2:
                ref[...] = joined.astype(BF16)
                continue
            for p in range(joined.shape[1] // PAIR):
                block = joined[:, p * PAIR : (p + 1) * PAIR]
                turned = (block * c + swap_pairs(block) * s).astype(BF16)
                if which == 0:
                    turned = turned * jnp.asarray(HEAD**-0.5, BF16)
                ref[:, p * PAIR : (p + 1) * PAIR] = turned

    @pl.when(first)
    def _():
        body(True)

    @pl.when(jnp.logical_not(first))
    def _():
        body(False)


def project(tok, gain, shift, w3, mw, cot, cos, sin, rows=256):
    length, width = tok.shape
    local = mw.shape[0]

    def row_block(n):
        return pl.BlockSpec((rows, n), lambda i: (i, 0))

    def out(n):
        return ((length, n), BF16, row_block(n))

    return launch(
        project_kernel,
        "project",
        (length // rows,),
        (),
        (),
        [
            (tok, row_block(width)),
            (gain, whole(1, width)),
            (shift, whole(1, width)),
            (w3, pl.BlockSpec(memory_space=pltpu.HBM)),
            (mw, pl.BlockSpec(memory_space=pltpu.HBM)),
            (cot, row_block(width)),
            (cos, row_block(PAIR)),
            (sin, row_block(PAIR)),
        ],
        [out(width), ((width, length), BF16, pl.BlockSpec((width, rows), lambda i: (0, i)))]
        + [out(local)] * 4
        + [((1, width), F32, whole(1, width))],
        [
            pltpu.VMEM((3, width, local), BF16),
            pltpu.VMEM((local, width), BF16),
            pltpu.SemaphoreType.DMA((4,)),
        ],
        vmem=60,
        flops=8 * length * width * local,
    )


def hidden_kernel(normed, cot, up_in, shift, down_in, out, dn, act, dpre, ig, up, down, sems, *, cols):
    first = pl.program_id(0) == 0
    cuts = [slice(j, j + cols) for j in range(0, up.shape[1], cols)]
    copies = []
    for j, s in enumerate(cuts):
        copies.append(
            (
                pltpu.make_async_copy(up_in.at[:, s], up.at[:, s], sems.at[2 * j]),
                pltpu.make_async_copy(down_in.at[s, :], down.at[s, :], sems.at[2 * j + 1]),
            )
        )

    @pl.when(first)
    def _():
        for pair in copies:
            for copy in pair:
                copy.start()

    def body(arriving):
        n = normed[...]
        c = cot[...]
        sums = []
        for j, s in enumerate(cuts):
            if arriving:
                for copy in copies[j]:
                    copy.wait()
            v = nn(n, up[:, s]) + shift[:, s]
            da = nt(c, down[s, :])
            square = v * v
            t = jnp.tanh(gelu_rate * v * (1.0 + 0.044715 * square))
            h = 0.5 * (1.0 + t)
            act[:, s] = (v * h).astype(BF16)
            slope = h + (0.5 * gelu_rate) * v * (1.0 - t * t) * (1.0 + (3 * 0.044715) * square)
            d_pre = (da * slope).astype(BF16)
            dpre[:, s] = d_pre
            sums.append(jnp.sum(d_pre.astype(F32), axis=0, keepdims=True))
        sums = jnp.concatenate(sums, axis=1)
        ig[...] = sums if arriving else ig[...] + sums
        out[...] = nn(act[...], down[...])
        dn[...] = nt(dpre[...], up[...])

    @pl.when(first)
    def _():
        body(True)

    @pl.when(jnp.logical_not(first))
    def _():
        body(False)


def hidden_pass(after, normed, cot, up, shift, down, rows=256, cols=512):
    length, width = normed.shape
    hidden = up.shape[1]

    def here(n):
        return pl.BlockSpec((rows, n), lambda i: (i, 0))

    return launch(
        functools.partial(hidden_kernel, cols=cols),
        "hidden",
        (length // rows,),
        (),
        after,
        [
            (normed, here(width)),
            (cot, here(width)),
            (up, pl.BlockSpec(memory_space=pltpu.HBM)),
            (shift, whole(1, hidden)),
            (down, pl.BlockSpec(memory_space=pltpu.HBM)),
        ],
        [((length, width), F32, here(width))] * 2
        + [((length, hidden), BF16, here(hidden))] * 2
        + [((1, hidden), F32, whole(1, hidden))],
        [
            pltpu.VMEM((width, hidden), BF16),
            pltpu.VMEM((hidden, width), BF16),
            pltpu.SemaphoreType.DMA((2 * hidden // cols,)),
        ],
        vmem=52,
        flops=9 * length * width * hidden,
    )


def grad_kernel(place, lhs, rhs, *rest, base, product, own):
    if own:
        got, keep, send, buf, sems, land, land_sems = rest
    else:
        out, buf, sems = rest
    j = pl.program_id(0)
    size = buf.shape[1] // 8

    def arriving(n):
        return pltpu.make_async_copy(
            got.at[place[base + n]], land.at[pl.ds(n * size, size)], land_sems.at[n]
        )

    if own:

        @pl.when(j == 0)
        def _():
            for n in range(16):
                arriving(n).start()

    buf[j] = product(lhs[...], rhs[...])
    if own:

        @pl.when(j == 0)
        def _():
            for n in range(8):
                arriving(n).wait()

        @pl.when(j == 1)
        def _():
            for n in range(8, 16):
                arriving(n).wait()

        buf[j] += land[pl.ds(pl.multiple_of(j * 8 * size, size), 8 * size), :]

    for i in range(8):
        spot = place[base + j * 8 + i]
        block = buf.at[j, pl.ds(i * size, size)]
        sem = sems.at[j * 8 + i]
        if own:

            @pl.when(spot < 8)
            def _():
                pltpu.make_async_copy(block, keep.at[spot], sem).start()

            @pl.when(spot >= 8)
            def _():
                pltpu.make_async_copy(block, send.at[spot - 8], sem).start()

        else:
            pltpu.make_async_copy(block, out.at[spot], sem).start()

    @pl.when(j == 1)
    def _():
        for n in range(16):
            block = buf.at[n // 8, pl.ds((n % 8) * size, size)]
            pltpu.make_async_copy(block, (keep if own else out).at[0], sems.at[n]).wait()


def grad(place, base, spots, after, lhs, rhs, specs, product, got=None):
    width = 1024
    rows = 1024
    own = got is not None
    piece = rows // 16
    anywhere = pl.BlockSpec(memory_space=pltpu.HBM)
    scratch = [pltpu.VMEM((2, rows // 2, width), F32), pltpu.SemaphoreType.DMA((16,))]
    if own:
        scratch += [pltpu.VMEM((rows, width), F32), pltpu.SemaphoreType.DMA((16,))]
    outs = [((8 if own else 16, piece, width), F32, anywhere)] * (2 if own else 1)
    return launch(
        functools.partial(grad_kernel, base=spots, product=product, own=own),
        "grad",
        (2,),
        (place,),
        after,
        [(lhs, specs[0]), (rhs, specs[1])] + ([(got, anywhere)] if own else []),
        outs,
        scratch,
        vmem=28,
        flops=2 * rows * width * lhs.shape[0],
    )


def down_grad(place, base, after, active, cot, got=None):
    length, width = cot.shape
    block = pl.BlockSpec((length, 512), lambda j, place: (0, place[base] * 2 + j))
    return grad(
        place, base, base + 1, after, active, cot, (block, once(length, width)), tn, got
    )


def up_grad(place, base, after, normed_t, d_pre, got=None):
    width, length = normed_t.shape
    rows = pl.BlockSpec((512, length), lambda j, _: (j, 0))
    half = pl.BlockSpec(
        (length, 1024), lambda j, place: (0, place[base]), pipeline_mode=pl.Buffered(1)
    )
    return grad(place, base, base + 17, after, normed_t, d_pre, (rows, half), nn, got)


def attend_kernel(*refs, last, sub):
    if last:
        q, do, k, v, dk_in, dv_in, cos, sin, ho, dq, dk, dv, dk_sum, dv_sum = refs
    else:
        q, do, k, v, cos, sin, ho, dq, dk_sum, dv_sum = refs
    block = q.shape[0]
    seen = k.shape[0]
    low = lax.broadcasted_iota(jnp.int32, (sub, PAIR), 1) < HEAD
    zero = jnp.zeros((sub, PAIR), BF16)
    causal = lax.broadcasted_iota(jnp.int32, (sub, sub), 1) <= lax.broadcasted_iota(
        jnp.int32, (sub, sub), 0
    )
    for i in range(block // sub):
        before = seen - block + i * sub
        upto = before + sub
        rows = slice(i * sub, (i + 1) * sub)
        keys = k[0:upto, :]
        values = v[0:upto, :]
        heads = [
            [jnp.where(low, x[rows, :], zero), jnp.where(low, zero, x[rows, :])] for x in (q, do)
        ]
        scores = [nt(x, keys) for x in heads[0]]
        d_probs = [nt(x, values) for x in heads[1]]
        probs_low, d_scores = [], []
        for h in range(2):
            edge = jnp.where(causal, scores[h][:, before:], -1e30)
            if before:
                edge = jnp.concatenate([scores[h][:, :before], edge], axis=1)
            expo = jnp.exp(edge - jnp.max(edge, axis=1, keepdims=True))
            probs = expo * (1.0 / jnp.sum(expo, axis=1, keepdims=True))
            inner = jnp.sum(probs * d_probs[h], axis=1, keepdims=True)
            probs_low.append(probs.astype(BF16))
            d_scores.append((probs * (d_probs[h] - inner)).astype(BF16))
        mixed = [nn(x, values) for x in probs_low]
        ho[rows, :] = jnp.where(low, mixed[0], mixed[1]).astype(BF16)
        d_query = [nn(x, keys) for x in d_scores]
        d_query = jnp.where(low, d_query[0], d_query[1]) * HEAD**-0.5
        turn = slice(before, upto)
        dq[rows, :] = (
            d_query * cos[turn, :] - swap_pairs(d_query) * sin[turn, :]
        ).astype(BF16)
        for left, right, total in ((probs_low, heads[1], dv_sum), (d_scores, heads[0], dk_sum)):
            add = tn(left[0], right[0]) + tn(left[1], right[1])
            if i == 0:
                total[0:upto, :] = add
            else:
                total[0:before, :] += add[:before]
                total[before:upto, :] = add[before:]
    if last:
        before = seen - block
        dk_sum[0:before, :] += dk_in[...]
        dv_sum[0:before, :] += dv_in[...]
        for i in range(seen // block):
            rows = slice(i * block, (i + 1) * block)
            d_keys = dk_sum[rows, :]
            dk[rows, :] = (d_keys * cos[rows, :] - swap_pairs(d_keys) * sin[rows, :]).astype(BF16)
            dv[rows, :] = dv_sum[rows, :].astype(BF16)


def attend(part, after, q, k, v, do, cos, sin, carried=(), sub=256):
    length, local = q.shape
    half = length // 2
    seen = half * (part + 1)
    rows = pl.BlockSpec((half, PAIR), lambda p: (part, p))
    keys = pl.BlockSpec((seen, PAIR), lambda p: (0, p))
    table = pl.BlockSpec((seen, PAIR), lambda p: (0, 0))
    here = pl.BlockSpec((half, PAIR), lambda p: (0, p))
    outs = [((half, local), BF16, here)] * 2
    scratch = ()
    if part == 0:
        outs += [((half, local), F32, here)] * 2
    else:
        outs += [((length, local), BF16, keys)] * 2
        scratch = [pltpu.VMEM((length, PAIR), F32)] * 2
    return launch(
        functools.partial(attend_kernel, last=part == 1, sub=sub),
        "attend",
        (local // PAIR,),
        (),
        after,
        [(q, rows), (do, rows), (k, keys), (v, keys)]
        + [(x, here) for x in carried]
        + [(cos, table), (sin, table)],
        outs,
        scratch,
        flops=30 * half * seen * PAIR * local // PAIR,
    )


def forward_kernel(ho, mw, a, *pieces, cuts):
    i = pl.program_id(0)
    total = nn(ho[...], mw[...]) + a[...]
    for n, piece in enumerate(pieces):

        @pl.when(jnp.logical_and(i >= cuts[n], i < cuts[n + 1]))
        def _():
            piece[...] = total


def within(first, last):
    return lambda i, *_: (jnp.clip(i, first, last - 1) - first, 0)


def cut_specs(sizes, rows, width):
    cuts = [int(n) // rows for n in np.cumsum((0,) + tuple(sizes))]
    return cuts, [
        pl.BlockSpec((rows, width), within(cuts[k], cuts[k + 1])) for k in range(len(sizes))
    ]


def forward_part(part, after, ho, mw, a, sizes, rows=128):
    half, local = ho.shape
    width = mw.shape[1]
    steps = half // rows
    cuts, specs = cut_specs(sizes, rows, width)
    there = pl.BlockSpec((rows, width), lambda i: (part * steps + i, 0))
    return launch(
        functools.partial(forward_kernel, cuts=cuts),
        "forward",
        (steps,),
        (),
        after,
        [
            (ho, pl.BlockSpec((rows, local), lambda i: (i, 0))),
            (mw, once(local, width)),
            (a, there),
        ],
        [((n, width), F32, spec) for n, spec in zip(sizes, specs)],
        flops=2 * half * width * local,
    )


def backward_kernel(dq0, dq1, dk, dv, w, a, tok, *rest, spots):
    pieces, (sums, buf, sems) = rest[:-3], rest[-3:]
    i = pl.program_id(0)
    steps = len(spots)
    rows = buf.shape[1]
    slot = i % 2

    def leaving(step):
        return [
            pltpu.make_async_copy(
                buf.at[step % 2, pl.ds(half * rows // 2, rows // 2)],
                pieces[k].at[pl.ds(start, rows // 2)],
                sems.at[step % 2, half],
            )
            for half, (k, start) in enumerate(spots[step])
        ]

    for step in range(2, steps):

        @pl.when(i == step)
        def _():
            for copy in leaving(step - 2):
                copy.wait()

    def one(dq):
        total = nt(dq[...], w[0]) + nt(dk[...], w[1]) + nt(dv[...], w[2]) + a[...]
        buf[slot] = total
        unit, _ = norm_rows(tok[...].astype(F32))
        both = jnp.concatenate(
            [jnp.sum(total * unit, axis=0, keepdims=True), jnp.sum(total, axis=0, keepdims=True)],
            axis=0,
        )

        @pl.when(i == 0)
        def _():
            sums[...] = both

        @pl.when(i > 0)
        def _():
            sums[...] += both

    @pl.when(i < steps // 2)
    def _():
        one(dq0)

    @pl.when(i >= steps // 2)
    def _():
        one(dq1)

    for step in range(steps):

        @pl.when(i == step)
        def _():
            for copy in leaving(step):
                copy.start()

    @pl.when(i == steps - 1)
    def _():
        for step in (steps - 2, steps - 1):
            for copy in leaving(step):
                copy.wait()


def backward_pass(after, dq0, dq1, dk, dv, w3, a, tok, sizes, rows=256):
    length, local = dk.shape
    width = w3.shape[1]
    steps = length // rows
    spots = [(k, start) for k, n in enumerate(sizes) for start in range(0, n, rows // 2)]
    spots = [spots[2 * i : 2 * i + 2] for i in range(steps)]
    here = pl.BlockSpec((rows, width), lambda i: (i, 0))
    narrow = pl.BlockSpec((rows, local), lambda i: (i, 0))
    anywhere = pl.BlockSpec(memory_space=pltpu.HBM)
    return launch(
        functools.partial(backward_kernel, spots=spots),
        "backward",
        (steps,),
        (),
        after,
        [
            (dq0, pl.BlockSpec((rows, local), within(0, steps // 2))),
            (dq1, pl.BlockSpec((rows, local), within(steps // 2, steps))),
            (dk, narrow),
            (dv, narrow),
            (w3, once(3, width, local)),
            (a, here),
            (tok, here),
        ],
        [((n, width), F32, anywhere) for n in sizes] + [((2, width), F32, whole(2, width))],
        [pltpu.VMEM((2, rows, width), F32), pltpu.SemaphoreType.DMA((2, 2))],
        vmem=44,
        flops=6 * length * width * local,
    )


def gate_kernel(*refs):
    pass


def gate(after, *arrays):
    anywhere = pl.BlockSpec(memory_space=pltpu.HBM)
    n = len(after)
    return pl.pallas_call(
        gate_kernel,
        in_specs=[anywhere] * (n + len(arrays)),
        out_specs=[anywhere] * len(arrays),
        out_shape=[jax.ShapeDtypeStruct(x.shape, x.dtype) for x in arrays],
        input_output_aliases={n + i: i for i in range(len(arrays))},
        name="gate",
    )(*after, *arrays)


def tail_kernel(place, normed_t, ho0, ho1, cot, dq0, dq1, dk, dv, own0, own1, other0, other1):
    n = normed_t[...]
    half = dq0.shape[0]
    first = place[0] == 0

    def put(mine, x, own, other):
        @pl.when(mine)
        def _():
            own[...] = x

        @pl.when(jnp.logical_not(mine))
        def _():
            other[...] = x

    put(first, nn(n[:, :half], dq0[...]) + nn(n[:, half:], dq1[...]), own0, other0)
    put(first, nn(n, dk[...]), own1, other1)
    put(jnp.logical_not(first), nn(n, dv[...]), own0, other0)
    g = tn(ho0[...], cot[:half, :]) + tn(ho1[...], cot[half:, :])
    columns = g.shape[1] // 2
    g = jnp.concatenate([g[:, :columns], g[:, columns:]], axis=0)
    put(jnp.logical_not(first), g, own1, other1)


def tail(place, after, normed_t, ho0, ho1, cot, dq0, dq1, dk, dv):
    width, length = normed_t.shape
    local = dk.shape[1]
    half = length // 2
    assert 2 * local == width
    return launch(
        tail_kernel,
        "tail",
        (1,),
        (place,),
        after,
        [(normed_t, once(width, length))]
        + [(x, once(half, local)) for x in (ho0, ho1)]
        + [(cot, once(length, width))]
        + [(x, once(half, local)) for x in (dq0, dq1)]
        + [(x, once(length, local)) for x in (dk, dv)],
        [((width, local), F32, once(width, local))] * 4,
        vmem=36,
        flops=8 * length * width * local,
    )


def finish_kernel(*refs, cuts, last):
    refs, token = refs[:-1], refs[-1]
    token[...] = jnp.zeros_like(token)
    n = len(cuts) - 1
    wide, (mine, got), (row, out) = refs[: -2 * n - 2], (refs[-2 * n - 2 : -n - 2], refs[-n - 2 : -2]), refs[-2:]
    i = pl.program_id(0)
    x = wide[0][...].astype(F32)

    def one(total):
        if not last:
            out[...] = (x + total + row[...]).astype(BF16)
            return
        unit, inverse = norm_rows(x)
        d_unit = total * row[...]
        centre = jnp.mean(d_unit, axis=1, keepdims=True)
        slope = jnp.mean(d_unit * unit, axis=1, keepdims=True)
        out[...] = (
            wide[1][...].astype(F32) + inverse * (d_unit - centre - unit * slope)
        ).astype(BF16)

    for k in range(n):

        @pl.when(jnp.logical_and(i >= cuts[k], i < cuts[k + 1]))
        def _():
            one(mine[k][...] + got[k][...])


def finish(name, after, wide, mine, got, row, start=0, into=None, rows=128, vmem=16):
    length, width = wide[0].shape
    cuts, pieces = cut_specs([x.shape[0] for x in mine], rows, width)
    first = start // rows
    here = pl.BlockSpec((rows, width), lambda i: (first + i, 0))
    return launch(
        functools.partial(finish_kernel, cuts=cuts, last=len(wide) > 1),
        name,
        (cuts[-1],),
        (),
        after,
        [(x, here) for x in wide]
        + list(zip(mine, pieces))
        + list(zip(got, pieces))
        + [(row, whole(1, width))],
        [((length, width), BF16, here), TOKEN],
        vmem=vmem,
        into=into,
    )


def halve_kernel(place, a, b, c, d, keep, send):
    keep[...] = a[...] + b[...]
    send[...] = c[...] + d[...]


def halve(place, slot, after, mine, got):
    n, width = mine.shape
    h = n // 2
    rows = h // 2 if h * width > (256 << 10) else h
    steps = h // rows

    def bit(place):
        return 0 if slot is None else place[slot]

    keep = pl.BlockSpec((rows, width), lambda i, place: (bit(place) * steps + i, 0))
    send = pl.BlockSpec((rows, width), lambda i, place: ((1 - bit(place)) * steps + i, 0))
    here = pl.BlockSpec((rows, width), lambda i, _: (i, 0))
    return launch(
        halve_kernel,
        "halve",
        (steps,),
        (place,),
        after,
        [(mine, keep), (got, keep), (mine, send), (got, send)],
        [((h, width), F32, here)] * 2,
    )


def pack_kernel(a, b, c, d, *rest):
    small, out = rest[:-1], rest[-1]
    n, width = a.shape
    top = SMALL if small else 0
    out[top : top + n, :] = a[...] + b[...]
    out[top + n :, :] = c[...] + d[...]
    if small:
        rows = [
            x[i : i + 1, j : j + width]
            for x in small
            for i in range(x.shape[0])
            for j in range(0, x.shape[1], width)
        ]
        rows.append(jnp.zeros((SMALL - len(rows), width), F32))
        out[:top, :] = jnp.concatenate(rows, axis=0)


def pack(after, a, b, c, d, small=()):
    shape = (a.shape[0] + c.shape[0] + (SMALL if small else 0), a.shape[1])
    return launch(
        pack_kernel,
        "pack",
        (1,),
        (),
        after,
        [(x, whole(*x.shape)) for x in (a, b, c, d, *small)],
        [(shape, F32, whole(*shape))],
    )[0]


def plus_kernel(a, b, out):
    out[...] = a[...] + b[...]


def plus(after, a, b):
    return launch(
        plus_kernel,
        "plus",
        (1,),
        (),
        after,
        [(x, whole(*x.shape)) for x in (a, b)],
        [(a.shape, F32, whole(*a.shape))],
    )[0]


def part_kernel(a, b, first, second):
    n = first.shape[0]
    first[...] = a[:n, :] + b[:n, :]
    second[...] = a[n:, :] + b[n:, :]


def part(after, n, a, b):
    shapes = [(n, a.shape[1]), (a.shape[0] - n, a.shape[1])]
    return launch(
        part_kernel,
        "part",
        (1,),
        (),
        after,
        [(x, whole(*x.shape)) for x in (a, b)],
        [(shape, F32, whole(*shape)) for shape in shapes],
    )


def join_kernel(place, mine, got, out, *scratch, slot, top):
    sems = scratch[-1]
    h = mine.shape[0] - top
    bit = place[slot]
    copies = [
        pltpu.make_async_copy(
            mine.at[pl.ds(top, h)], out.at[pl.ds(pl.multiple_of(top + bit * h, 8), h)], sems.at[0]
        ),
        pltpu.make_async_copy(
            got.at[pl.ds(top, h)],
            out.at[pl.ds(pl.multiple_of(top + (1 - bit) * h, 8), h)],
            sems.at[1],
        ),
    ]
    if top:
        small = scratch[0]
        copies += [
            pltpu.make_async_copy(x.at[pl.ds(0, top)], small.at[i], sems.at[2 + i])
            for i, x in enumerate((mine, got))
        ]
    for copy in copies:
        copy.start()
    for copy in copies:
        copy.wait()
    if top:
        out[:top, :] = small[0] + small[1]


def join(place, slot, after, mine, got, top=0):
    n, width = mine.shape
    anywhere = pl.BlockSpec(memory_space=pltpu.HBM)
    rows = 2 * n - top
    return launch(
        functools.partial(join_kernel, slot=slot, top=top),
        "join",
        (1,),
        (place,),
        after,
        [(mine, anywhere), (got, anywhere)],
        [((rows, width), F32, once(rows, width))],
        ([pltpu.VMEM((2, top, width), F32)] if top else []) + [pltpu.SemaphoreType.DMA((4,))],
    )[0]


def place_kernel(place, *refs, pieces, rows):
    srcs, (qkv, merge, token, buf, in_sems, out_sems) = refs[: len(pieces)], refs[len(pieces) :]
    token[...] = jnp.zeros_like(token)
    arriving = [
        pltpu.make_async_copy(src.at[pl.ds(src.shape[0] - rows, rows)], buf.at[i], in_sems.at[i])
        for i, src in enumerate(srcs)
    ]
    for copy in arriving:
        copy.start()
    for i, (near, part, mine) in enumerate(pieces):
        j = 2 * (1 - place[0] if near else place[0]) + part
        bit = place[NEAR + part] if near else place[bit_slot(part, 0)]
        start = pl.multiple_of((bit if mine else 1 - bit) * rows, rows)
        arriving[i].wait()

        @pl.when(j < 3)
        def _():
            pltpu.make_async_copy(
                buf.at[i], qkv.at[jnp.minimum(j, 2), pl.ds(start, rows)], out_sems.at[i]
            ).start()

        @pl.when(j == 3)
        def _():
            pltpu.make_async_copy(
                buf.at[i], merge.at[:, pl.ds(start, rows)], out_sems.at[i]
            ).start()

    for i in range(len(pieces)):
        pltpu.make_async_copy(buf.at[i], qkv.at[0, pl.ds(0, rows)], out_sems.at[i]).wait()


def place_pieces(place, after, arrays, pieces, width, into=None):
    local = arrays[0].shape[1]
    rows = width // 2
    anywhere = pl.BlockSpec(memory_space=pltpu.HBM)
    return launch(
        functools.partial(place_kernel, pieces=pieces, rows=rows),
        "place",
        (1,),
        (place,),
        after,
        [(x, anywhere) for x in arrays],
        [((3, width, local), F32, anywhere), ((local, width), F32, anywhere), TOKEN],
        [
            pltpu.VMEM((len(arrays), rows, local), F32),
            pltpu.SemaphoreType.DMA((len(arrays),)),
            pltpu.SemaphoreType.DMA((len(arrays),)),
        ],
        into=into,
    )


def small_kernel(own0, own1, near0, near1, out):
    out[...] = (own0[...] + own1[...]) + (near0[...] + near1[...])


def small_sums(after, arrays):
    width = arrays[0].shape[1]
    top = pl.BlockSpec((SMALL, width), lambda i: (0, 0))
    return launch(
        small_kernel,
        "small_sums",
        (1,),
        (),
        after,
        [(x, top) for x in arrays],
        [((SMALL, width), F32, whole(SMALL, width))],
    )[0]


def spread_kernel(gathered, up, down, token, buf, in_sems, out_sems):
    token[...] = jnp.zeros_like(token)
    count, rows, width = gathered.shape
    piece = rows // 2
    half = count // 2
    slots = buf.shape[0]

    def outs(n):
        slot = n % slots
        return (
            pltpu.make_async_copy(
                buf.at[slot, pl.ds(0, piece)],
                down.at[n // half, pl.ds((n % half) * piece, piece)],
                out_sems.at[2 * slot],
            ),
            pltpu.make_async_copy(
                buf.at[slot, pl.ds(piece, piece)],
                up.at[pl.ds((n % half) * piece, piece), pl.ds((n // half) * width, width)],
                out_sems.at[2 * slot + 1],
            ),
        )

    def arrive(n):
        slot = n % slots
        return pltpu.make_async_copy(gathered.at[n], buf.at[slot], in_sems.at[slot])

    ahead = slots // 2
    for n in range(count + ahead):
        if n < count:
            if n >= slots:
                for copy in outs(n - slots):
                    copy.wait()
            arrive(n).start()
        if n >= ahead:
            arrive(n - ahead).wait()
            for copy in outs(n - ahead):
                copy.start()
    for n in range(count - slots, count):
        for copy in outs(n):
            copy.wait()


def spread(after, gathered, slots=16):
    count, rows, width = gathered.shape
    piece = rows // 2
    half = count // 2
    anywhere = pl.BlockSpec(memory_space=pltpu.HBM)
    return launch(
        spread_kernel,
        "spread",
        (1,),
        (),
        after,
        [(gathered, anywhere)],
        [
            ((half * piece, 2 * width), F32, anywhere),
            ((2, half * piece, width), F32, anywhere),
            TOKEN,
        ],
        [
            pltpu.VMEM((slots, rows, width), F32),
            pltpu.SemaphoreType.DMA((slots,)),
            pltpu.SemaphoreType.DMA((2 * slots,)),
        ],
        vmem=60,
    )


AXES = ("xlo", "z", "y", "core", "tensor")
RINGS = ("z", "y", "core")
DIRECTIONS = (("y", 0), ("z", 0), ("y", 1), ("z", 1))
SWAP = ((0, 1), (1, 0))


def partner(place, bit):
    return place ^ 1 if bit == 0 else 3 - place


def bit_at(place, bit):
    return int(place in (1, 2)) if bit == 0 else int(place >= 2)


def order_of(core, part):
    return [(core + 2 * part + step) % 4 for step in range(4)]


def spot_of(z, y, core, part):
    spot = 0
    for direction in order_of(core, part):
        axis, bit = DIRECTIONS[direction]
        spot = 2 * spot + bit_at(y if axis == "y" else z, bit)
    return spot


def step_pairs(part, step):
    pairs = []
    for z in range(4):
        for y in range(4):
            for core in range(2):
                axis, bit = DIRECTIONS[order_of(core, part)[step]]
                z2, y2 = (z, partner(y, bit)) if axis == "y" else (partner(z, bit), y)
                pairs.append(((z * 4 + y) * 2 + core, (z2 * 4 + y2) * 2 + core))
    return pairs


def place_table():
    rows = []
    for z in range(4):
        for y in range(4):
            for core in range(2):
                row = [core]
                for part in range(2):
                    for direction in order_of(core, part):
                        axis, bit = DIRECTIONS[direction]
                        row.append(bit_at(y if axis == "y" else z, bit))
                for half in (core, 1 - core):
                    row.append(half)
                    for part in range(2):
                        here = spot_of(z, y, half, part)
                        row += [
                            here ^ spot_of(z2, y2, half, part) for z2 in range(4) for y2 in range(4)
                        ]
                for part in range(2):
                    axis, bit = DIRECTIONS[order_of(1 - core, part)[0]]
                    row.append(bit_at(y if axis == "y" else z, bit))
                rows.append(row)
    return np.array(rows, np.int32)


OWN = 9
OTHER = OWN + 33
NEAR = OTHER + 33


def bit_slot(part, step):
    return 1 + 4 * part + step


def send_step(x, part, step):
    return lax.ppermute(x, RINGS, step_pairs(part, step))


def exchange(x, axis):
    return lax.ppermute(x, axis, SWAP)


def body(
    tokens,
    norm_gain,
    norm_shift,
    qkv_weight,
    merge_weight,
    up_weight,
    inner_shift,
    down_weight,
    outer_shift,
    cotangent,
):
    length, width = tokens.shape
    local = merge_weight.shape[0]
    hidden = up_weight.shape[1]
    place = lax.dynamic_index_in_dim(
        jnp.asarray(place_table()), lax.axis_index(RINGS), 0, keepdims=False
    )
    cos, sin = rotary_tables(length)
    w3 = qkv_weight.transpose(1, 0, 2)
    gain, shift, inner_row = norm_gain[None], norm_shift[None], inner_shift[None]

    normed, normed_t, q, k, v, dh, outer_g = project(
        tokens, gain, shift, w3, merge_weight, cotangent, cos, sin
    )
    out_f, dn_f, active, d_pre, inner_g = hidden_pass(
        (), normed, cotangent, up_weight, inner_row, down_weight
    )

    (down_s,) = down_grad(place, OTHER, (), active, cotangent)
    down_got = exchange(down_s, "core")
    (up_s,) = up_grad(place, OTHER, (down_s,), normed_t, d_pre)
    up_got = exchange(up_s, "core")

    ho0, dq0, dk_part, dv_part = attend(0, (up_s,), q, k, v, dh, cos, sin)
    mine = list(forward_part(0, (dq0,), ho0, merge_weight, out_f, (512,)))
    theirs = [exchange(mine[0], "tensor")]

    def flat(x):
        return x.reshape(-1, x.shape[-1])

    down_k, down_s = map(flat, down_grad(place, OWN, (mine[0],), active, cotangent, down_got))
    down_got = send_step(down_s, 0, 0)
    up_k, up_s = map(flat, up_grad(place, OWN, (down_s,), normed_t, d_pre, up_got))
    up_got = send_step(up_s, 1, 0)

    ho1, dq1, dk, dv = attend(1, (up_s,), q, k, v, dh, cos, sin, (dk_part, dv_part))
    mine += forward_part(1, (dq1,), ho1, merge_weight, out_f, (512,))
    theirs += [exchange(x, "tensor") for x in mine[1:]]

    own0, own1, tail_s0, tail_s1 = tail(
        place, (mine[1],), normed_t, ho0, ho1, cotangent, dq0, dq1, dk, dv
    )
    tail_got0 = exchange(tail_s0, "core")
    tail_got1 = exchange(tail_s1, "core")
    down_k, down_s = halve(place, None, (tail_s0, theirs[0]), down_k, down_got)
    down_got = send_step(down_s, 0, 1)
    up_k, up_s = halve(place, None, (down_s,), up_k, up_got)
    up_got = send_step(up_s, 1, 1)

    tail_k0, tail_s0 = halve(place, bit_slot(0, 0), (up_s,), own0, tail_got0)
    tail_got0 = send_step(tail_s0, 0, 0)
    tail_k1, tail_s1 = halve(place, bit_slot(1, 0), (tail_s0,), own1, tail_got1)
    tail_got1 = send_step(tail_s1, 1, 0)

    *back, sums = backward_pass(
        (tail_s1,), dq0, dq1, dk, dv, w3, dn_f, tokens, (128, 256, 512, 128)
    )

    down_k, down_s = halve(place, None, (sums,), down_k, down_got)
    down_got = send_step(down_s, 0, 2)
    up_k, up_s = halve(place, None, (down_s,), up_k, up_got)
    up_got = send_step(up_s, 1, 2)

    tail_k0, tail_s0 = halve(place, bit_slot(0, 1), (up_s,), tail_k0, tail_got0)
    tail_got0 = send_step(tail_s0, 0, 1)
    tail_k1, tail_s1 = halve(place, bit_slot(1, 1), (tail_s0,), tail_k1, tail_got1)
    tail_got1 = send_step(tail_s1, 1, 1)

    down_k, down_s = halve(place, None, (tail_s1,), down_k, down_got)
    down_got = send_step(down_s, 0, 3)
    up_k, up_s = halve(place, None, (down_s,), up_k, up_got)
    up_got = send_step(up_s, 1, 3)

    tail_k0, tail_s0 = halve(place, bit_slot(0, 2), (up_s, theirs[1]), tail_k0, tail_got0)
    tail_got0 = send_step(tail_s0, 0, 2)
    tail_k1, tail_s1 = halve(place, bit_slot(1, 2), (tail_s0,), tail_k1, tail_got1)
    tail_got1 = send_step(tail_s1, 1, 2)

    feed_x = pack((tail_s1,), down_k, down_got, up_k, up_got)
    feed_got = exchange(feed_x, "xlo")
    back[0] = gate((feed_x,), back[0])[0]
    back_got = [exchange(back[0], "tensor")]

    tail_k0, tail_s0 = halve(place, bit_slot(0, 3), (feed_x,), tail_k0, tail_got0)
    tail_got0 = send_step(tail_s0, 0, 3)
    tail_k1, tail_s1 = halve(place, bit_slot(1, 3), (tail_s0,), tail_k1, tail_got1)
    tail_got1 = send_step(tail_s1, 1, 3)

    feed_x = plus((tail_s1,), feed_x, feed_got)
    gathered = lax.all_gather(feed_x, ("core", "z", "y"))

    tail_x = pack(
        (feed_x,), tail_k0, tail_got0, tail_k1, tail_got1, (sums, outer_g, inner_g)
    )
    tail_got = exchange(tail_x, "xlo")

    tail0, tail1 = part((tail_x, back_got[0]), SMALL + tail_k0.shape[0], tail_x, tail_got)
    tail_got0 = send_step(tail0, 0, 3)
    tail_got1 = send_step(tail1, 1, 3)

    back[1:] = gate((tail1,), *back[1:])
    back_got += [exchange(x, "tensor") for x in back[1:]]

    turn = back[1]
    for step in (3, 2, 1):
        tail0 = join(
            place, bit_slot(0, step), (turn, tail1), tail0, tail_got0, top=SMALL
        )
        tail_got0 = send_step(tail0, 0, step - 1)
        sink = (back_got[1],) if step == 1 else ()
        tail1 = join(place, bit_slot(1, step), (tail0, *sink), tail1, tail_got1)
        tail_got1 = send_step(tail1, 1, step - 1)
        turn = tail1
        if step == 2:
            block_out, turn = finish(
                "finish_out", (tail1,), (tokens,), mine, theirs, outer_shift[None]
            )

    token_grad, turn = finish(
        "finish_grad", (tail1,), (tokens, cotangent), back[:2], back_got[:2], gain, vmem=60
    )
    near0, near1 = exchange(tail0, "core"), exchange(tail1, "core")
    up_out, down_out, turn = spread((turn, near0, near1), gathered)
    down_out = down_out.reshape(hidden, width)
    tail_got0, tail_got1 = gate((turn, back_got[2]), tail_got0, tail_got1)
    near_got0, near_got1 = exchange(tail_got0, "core"), exchange(tail_got1, "core")
    kinds = [(near, part) for near in (False, True) for part in range(2)]
    qkv_out, merge_out, turn = place_pieces(
        place,
        (tail_got0,),
        (tail0, tail1, near0, near1),
        [(*kind, True) for kind in kinds],
        width,
    )
    small = small_sums((turn,), (tail0, tail_got0, near0, near_got0))
    small_got = exchange(small, "tensor")
    qkv_out, merge_out, turn = place_pieces(
        place,
        (small,),
        (tail_got0, tail_got1, near_got0, near_got1),
        [(*kind, False) for kind in kinds],
        width,
        into={0: qkv_out, 1: merge_out},
    )
    for k, start in ((2, 384), (3, 896)):
        token_grad, turn = finish(
            "finish_grad", (turn,), (tokens, cotangent), back[k : k + 1], back_got[k : k + 1],
            gain, start=start, into={0: token_grad}, vmem=60,
        )
    pair = (small[:4] + small_got[:4]).reshape(2, width)
    return (
        block_out,
        token_grad,
        pair[0],
        pair[1],
        qkv_out.transpose(1, 0, 2),
        merge_out,
        up_out,
        small[6 : 6 + hidden // local].reshape(hidden),
        down_out,
        small[4:6].reshape(width),
    )


def solution(mesh):
    dp = AXES[:4]
    finer = Mesh(mesh.devices.reshape(2, 4, 4, 2, 2), AXES)
    return jax.shard_map(
        body,
        mesh=finer,
        in_specs=(
            P(dp, None),
            P(),
            P(),
            P(None, None, "tensor"),
            P("tensor", None),
            P(None, "tensor"),
            P("tensor"),
            P("tensor", None),
            P(),
            P(dp, None),
        ),
        out_specs=(
            P(dp, None),
            P(dp, None),
            P(),
            P(),
            P(None, None, "tensor"),
            P("tensor", None),
            P(None, "tensor"),
            P("tensor"),
            P("tensor", None),
            P(),
        ),
        check_vma=False,
    )
```
